256 devices in a mesh: row: 16 (over z, core), col: 16 (over y, x).
Axes of the slice: x: 4, y: 4, z: 8, core: 2. Of those that a mesh axis runs over, the one named last changes fastest.
Arguments:
- hamiltonian: float32 [8, 16, 128, 8, 16, 128], P(None, 'row', None, None, 'col'), may hold values from -4 to 4, as said below
Outputs:
- band_form: float32 [8, 16, 128, 8, 16, 128], P(None, 'row', None, None, 'col')
The draws below stay inside these ranges and needn't reach their ends.
Inputs may be any that keep to these rules, and one draw needn't show every extreme that they name: The matrix laid out by hamiltonian is symmetric.
All inputs are finite; a program needn't handle non-finite values.
Results may differ from the reference program's by a relative error of at most 0.0001.
Values sent between devices are 32-bit elements; how exact they have to be, the bound alone decides.
A program may use at most 64 MiB of HBM per device.

```python
import jax
import jax.numpy as jnp
from jax import lax

N = 16384
NB = 128
PANELS = 2
TR = 8
TC = 8
N_ROW = 16
N_COL = 16


def locality(matrix):
    places = jnp.arange(N)
    distance = jnp.abs(places[:, None] - places[None, :])
    return jnp.where(distance >= 256, 0.2, 1.0) * matrix


def draw_hamiltonian(key, part):
    key = jax.random.fold_in(key, 11)
    base_key = jax.random.fold_in(key, 0)
    base = jnp.clip(jax.random.normal(base_key, (N, N), jnp.float32), -4.0, 4.0)
    symmetric = locality((base + base.T) * 0.5)
    return symmetric.reshape(TR, N_ROW, NB, TC, N_COL, NB)


def setup_inputs(seed: int = 0) -> dict:
    keys = jax.random.split(jax.random.key(seed), 2)
    return {
        "hamiltonian": draw_hamiltonian(jax.random.fold_in(keys[1], 71), 0),
    }


def product(first, second):
    return jnp.dot(first, second, precision=lax.Precision.HIGHEST)

def decompose(square):
    count = square.shape[0]
    positions = jnp.arange(count)

    def sweep(column_index, work):
        pivot_row = work[column_index]
        column = work[:, column_index] / pivot_row[column_index]
        below = jnp.where(positions > column_index, column, 0.0)
        after = jnp.where(positions > column_index, pivot_row, 0.0)
        work = work - below[:, None] * after[None, :]
        return work.at[:, column_index].set(jnp.where(positions > column_index, below, work[:, column_index]))
    work = lax.fori_loop(0, count, sweep, square)
    unit_lower = jnp.tril(work, -1) + jnp.eye(count, dtype=work.dtype)
    return (unit_lower, jnp.triu(work))

def factor_panel(gram_sum, top_block):
    lower_factor = jnp.linalg.cholesky(gram_sum)
    top_q = jax.scipy.linalg.solve_triangular(lower_factor, top_block.T, lower=True).T
    unit_lower, upper_part = decompose(top_q + jnp.eye(top_q.shape[0], dtype=top_q.dtype))
    coupling = jax.scipy.linalg.solve_triangular(unit_lower, upper_part.T, lower=True, unit_diagonal=True).T
    return (lower_factor, unit_lower, upper_part, coupling)

def reference(hamiltonian):
    tile_width = hamiltonian.shape[2]
    order = hamiltonian.shape[0] * hamiltonian.shape[1] * tile_width
    matrix = hamiltonian.reshape(order, order)
    positions = jnp.arange(order)
    for number in range(PANELS):
        first_row = (number + 1) * tile_width
        left_col = number * tile_width
        panel_rows = matrix[first_row:, left_col:first_row]
        gram_sum = product(panel_rows.T, panel_rows)
        lower_factor, unit_lower, upper_part, coupling = factor_panel(gram_sum, panel_rows[:tile_width])
        lower_q = jax.scipy.linalg.solve_triangular(lower_factor, panel_rows[tile_width:].T, lower=True)
        lower_y = jax.scipy.linalg.solve_triangular(upper_part.T, lower_q, lower=True).T
        vectors = jnp.concatenate([jnp.zeros((first_row, tile_width), jnp.float32), unit_lower, lower_y], 0)
        products = product(matrix, vectors)
        products = jnp.where((positions >= first_row)[:, None], products, 0.0)
        applied = product(products, coupling)
        inner_sums = product(vectors.T, applied)
        correction = applied - 0.5 * product(vectors, product(coupling.T, inner_sums))
        left_side = jnp.concatenate([correction, vectors], 1)
        right_side = jnp.concatenate([vectors, correction], 1)
        matrix = matrix - product(left_side, right_side.T)
        band_block = -lower_factor.T
        matrix = matrix.at[first_row:first_row + tile_width, left_col:first_row].set(band_block)
        matrix = matrix.at[first_row + tile_width:, left_col:first_row].set(0.0)
        matrix = matrix.at[left_col:first_row, first_row:first_row + tile_width].set(band_block.T)
        matrix = matrix.at[left_col:first_row, first_row + tile_width:].set(0.0)
    return matrix.reshape(hamiltonian.shape)
```

```python
import functools

import jax
import jax.numpy as jnp
from jax import lax
from jax.experimental import pallas as pl
from jax.experimental.pallas import tpu as pltpu
from jax.sharding import PartitionSpec as P

MESH = pl.DeviceIdType.MESH
NB = 128
NN = (((1,), (0,)), ((), ()))
NT = (((1,), (1,)), ((), ()))
TN = (((0,), (0,)), ((), ()))
VMEM_LIMIT = 56 << 20


def split(value):
    high = value.astype(jnp.bfloat16)
    low = (value - high.astype(jnp.float32)).astype(jnp.bfloat16)
    return high, low


def mxu(first, second, dims):
    return lax.dot_general(first, second, dims, preferred_element_type=jnp.float32)


def dot3(first, second, dims):
    fh, fl = split(first)
    sh, sl = split(second)
    return mxu(fh, sh, dims) + (mxu(fh, sl, dims) + mxu(fl, sh, dims))


def exact(first, second, dims=NN):
    return lax.dot_general(
        first, second, dims, precision=lax.Precision.HIGHEST, preferred_element_type=jnp.float32
    )


def iota(axis, shape):
    return lax.broadcasted_iota(jnp.int32, shape, axis)


def cholesky_blocks(g_ref, r_ref, first, last):
    sub = iota(0, (8, NB))
    lane = iota(1, (8, NB))

    def block(k, carry):
        base = pl.multiple_of(k * 8, 8)
        x = g_ref[pl.ds(base, 8), :]
        rolled = pltpu.roll(x, lax.rem(NB - base, NB), 1)
        cols = [jnp.broadcast_to(rolled[:, i : i + 1], (8, NB)) for i in range(8)]
        for i in range(8):
            scale = lax.rsqrt(cols[i][i : i + 1, :])
            column = cols[i] * scale
            below = jnp.where(sub > i, column, 0.0)
            row = x[i : i + 1, :] * scale
            x = jnp.where(sub == i, row, x - below * row)
            for m in range(i + 1, 8):
                cols[m] = cols[m] - below * column[m : m + 1, :]
        x = jnp.where(lane >= base + sub, x, 0.0)
        r_ref[pl.ds(base, 8), :] = x
        g_ref[...] -= exact(x, x, TN)
        return carry

    lax.fori_loop(first, last, block, 0)


def inverse_blocks(y_ref, t_ref, first, last):
    sub = iota(0, (8, NB))
    lane = iota(1, (8, NB))
    wide = iota(1, (NB, NB))

    def block(k, carry):
        base = pl.multiple_of(k * 8, 8)
        x = y_ref[pl.ds(base, 8), :]
        rolled = pltpu.roll(x, lax.rem(NB - base, NB), 1)
        cols = [jnp.broadcast_to(rolled[:, i : i + 1], (8, NB)) for i in range(8)]
        inside = (lane >= base) & (lane < base + 8)
        x = jnp.where(inside, jnp.where(lane - base == sub, 1.0, 0.0), x)
        for i in range(8):
            scale = 1.0 / cols[i][i : i + 1, :]
            factor = jnp.where(sub == i, 0.0, cols[i])
            row = x[i : i + 1, :] * scale
            x = jnp.where(sub == i, row, x - factor * row)
            for m in range(i + 1, 8):
                entry = cols[m][i : i + 1, :] * scale
                cols[m] = jnp.where(sub == i, entry, cols[m] - factor * entry)
        t_ref[pl.ds(base, 8), :] = x
        y = y_ref[...]
        chosen = (wide >= base) & (wide < base + 8)
        y_ref[...] = jnp.where(chosen, 0.0, y) - exact(jnp.where(chosen, y, 0.0), t_ref[...])
        y_ref[pl.ds(base, 8), :] = x
        t_ref[pl.ds(base, 8), :] = jnp.zeros((8, NB), jnp.float32)
        return carry

    lax.fori_loop(first, last, block, 0)


def reduce_kernel(n, tiles, *refs):
    rows = tiles * NB
    ch = rows // n
    pc = NB // n
    half = n // 2
    (
        a_hbm,
        c0r, f0r, c1r, f1r, c0c, f0c, c1c, f1c, r0_ref, r1_ref,
        abuf, ahi, alo, stg_r, stg_c, xr, xc, wpart, wrs, wch, wr, wc,
        ar_src, ar_slot, ar_res, h_src, h_slot, h_piece, h_ex, h_res,
        g_ref, y_ref, t_ref, asem, ss, rs,
    ) = refs
    r = lax.axis_index("row")
    c = lax.axis_index("col")
    parity = lax.rem(r, 2)
    level = r // 2

    load = pltpu.make_async_copy(a_hbm, abuf, asem)
    load.start()
    barrier = pltpu.get_barrier_semaphore()

    def greet(k, carry):
        pl.semaphore_signal(barrier, inc=1, device_id=(lax.rem(r + k, n), c), device_id_type=MESH)
        pl.semaphore_signal(barrier, inc=1, device_id=(r, lax.rem(c + k, n)), device_id_type=MESH)
        return carry

    lax.fori_loop(1, n, greet, 0)

    @pl.when(r != c)
    def _():
        pl.semaphore_signal(barrier, inc=1, device_id=(c, r), device_id_type=MESH)

    pl.semaphore_wait(barrier, 2 * (n - 1) + jnp.where(r != c, 1, 0))

    def send(src, dst, sem, device):
        pltpu.make_async_remote_copy(
            src, dst, ss.at[sem], rs.at[sem], device_id=device, device_id_type=MESH
        ).start()

    def over_cols(sem, src_of, dst_of):
        def one(k, carry):
            j = lax.rem(c + k, n)
            send(src_of(j), dst_of(j), sem, (r, j))
            return carry

        lax.fori_loop(1, n, one, 0)

    def over_rows(sem, src_of, dst_of):
        def one(k, carry):
            j = lax.rem(r + k, n)
            send(src_of(j), dst_of(j), sem, (j, c))
            return carry

        lax.fori_loop(1, n, one, 0)

    def wait(sem, sent, received):
        pltpu.make_async_copy(received, received, rs.at[sem]).wait()
        pltpu.make_async_copy(sent, sent, ss.at[sem]).wait()

    def scatter(t):
        @pl.when(c == t)
        def _():
            over_cols(
                t,
                lambda j: stg_r.at[pl.ds(j * ch, ch)],
                lambda j: xr.at[t, pl.ds(j * ch, ch)],
            )
            xr[t, pl.ds(t * ch, ch), :] = stg_r[pl.ds(t * ch, ch), :]

        @pl.when(r == t)
        def _():
            over_rows(
                3 + t,
                lambda j: stg_c.at[pl.ds(j * ch, ch)],
                lambda j: xc.at[t, j // 2, lax.rem(j, 2)],
            )
            xc[t, t // 2, t % 2] = stg_c[pl.ds(t * ch, ch), :]

    def scatter_wait(t):
        @pl.when(c == t)
        def _():
            sent = stg_r.at[pl.ds(0, (n - 1) * ch)]
            pltpu.make_async_copy(sent, sent, ss.at[t]).wait()

        @pl.when(c != t)
        def _():
            got = xr.at[t, pl.ds(c * ch, ch)]
            pltpu.make_async_copy(got, got, rs.at[t]).wait()

        @pl.when(r == t)
        def _():
            sent = stg_c.at[pl.ds(0, (n - 1) * ch)]
            pltpu.make_async_copy(sent, sent, ss.at[3 + t]).wait()

        @pl.when(r != t)
        def _():
            got = xc.at[t, level, parity]
            pltpu.make_async_copy(got, got, rs.at[3 + t]).wait()

    def gather_cols_start(buf, sem):
        mine = buf.at[pl.ds(c * ch, ch)]
        over_cols(sem, lambda j: mine, lambda j: mine)

    def gather_cols_wait(buf, sem):
        part = buf.at[pl.ds(0, (n - 1) * ch)]
        wait(sem, part, part)

    def gather_rows_start(buf, sem):
        mine = buf.at[level, parity]

        def one(k, carry):
            send(mine, mine, sem, (lax.rem(level + k, half) * 2 + parity, c))
            return carry

        lax.fori_loop(1, half, one, 0)

    def gather_rows_mid(buf, sem):
        part = buf.at[pl.ds(0, half - 1), 0]
        wait(sem, part, part)
        mine = buf.at[:, parity]
        send(mine, mine, sem + 1, (r + 1 - 2 * parity, c))

    def gather_rows_wait(buf, sem):
        part = buf.at[:, 0]
        wait(sem + 1, part, part)

    def sum_start(q, parts, sem):
        count = len(parts)
        for i, part in enumerate(parts):
            ar_src[q, i] = part
        over_cols(
            sem,
            lambda j: ar_src.at[q, pl.ds(0, count), pl.ds(j * pc, pc)],
            lambda j: ar_slot.at[q, c, pl.ds(0, count)],
        )
        ar_slot[q, c, 0:count] = ar_src[q, 0:count, pl.ds(c * pc, pc), :]

    def sum_mid(q, count, sem):
        got = ar_slot.at[q, pl.ds(0, n - 1), pl.ds(0, count)]
        wait(sem, got, got)
        total = ar_slot[q, 0, 0:count]
        for j in range(1, n):
            total = total + ar_slot[q, j, 0:count]
        mine = (q, pl.ds(0, count), pl.ds(c * pc, pc))
        ar_res[q, 0:count, pl.ds(c * pc, pc), :] = total
        over_cols(sem + 1, lambda j: ar_res.at[mine], lambda j: ar_res.at[mine])

    def sum_wait(q, count, sem):
        got = ar_res.at[q, pl.ds(0, count), pl.ds(0, (n - 1) * pc)]
        wait(sem + 1, got, got)

    def product_start(p, panel_c, panel_r, sem):
        ph, plo = split(panel_c)
        both = jnp.concatenate([ph, plo], axis=1)

        def one(a, carry):
            at = pl.multiple_of(a * NB, NB)
            high = ahi[pl.ds(at, NB), :]
            low = alo[pl.ds(at, NB), :]
            wide = mxu(high, both, NN)
            wpart[p, pl.ds(at, NB), :] = wide[:, :NB] + (wide[:, NB:] + mxu(low, ph, NN))
            return carry

        lax.fori_loop(0, tiles, one, 0)
        over_cols(
            sem,
            lambda j: wpart.at[p, pl.ds(j * ch, ch)],
            lambda j: wrs.at[p, c],
        )
        wrs[p, c] = wpart[p, pl.ds(c * ch, ch), :]
        h_src[p] = dot3(panel_r(), wpart[p], TN)
        over_cols(
            sem + 1,
            lambda j: h_src.at[p, pl.ds(j * pc, pc)],
            lambda j: h_slot.at[p, c],
        )
        h_slot[p, c] = h_src[p, pl.ds(c * pc, pc), :]

    def product_mid(p, sem):
        got = wrs.at[p, pl.ds(0, n - 1)]
        wait(sem, got, got)
        total = wrs[p, 0]
        for j in range(1, n):
            total = total + wrs[p, j]
        wch[p] = total

        @pl.when(r != c)
        def _():
            send(wch.at[p], wc.at[p, c // 2, lax.rem(c, 2)], sem + 2, (c, r))

        @pl.when(r == c)
        def _():
            wc[p, level, parity] = total

        wr[p, pl.ds(c * ch, ch), :] = total
        gather_cols_start(wr.at[p], sem + 3)
        got = h_slot.at[p, pl.ds(0, n - 1)]
        wait(sem + 1, got, got)
        total = h_slot[p, 0]
        for j in range(1, n):
            total = total + h_slot[p, j]
        h_piece[p] = total
        over_rows(sem + 6, lambda j: h_piece.at[p], lambda j: h_ex.at[p, r])
        h_ex[p, r] = total

    def product_late(p, sem):
        @pl.when(r != c)
        def _():
            wait(sem + 2, wch.at[p], wc.at[p, level, parity])

        gather_rows_start(wc.at[p], sem + 4)
        got = h_ex.at[p, pl.ds(0, n - 1)]
        wait(sem + 6, got, got)
        total = h_ex[p, 0]
        for j in range(1, n):
            total = total + h_ex[p, j]
        h_res[p, pl.ds(c * pc, pc), :] = total
        mine = h_res.at[p, pl.ds(c * pc, pc)]
        over_cols(sem + 7, lambda j: mine, lambda j: mine)

    def product_wait(p, sem):
        gather_rows_mid(wc.at[p], sem + 4)
        gather_cols_wait(wr.at[p], sem + 3)
        got = h_res.at[p, pl.ds(0, (n - 1) * pc)]
        wait(sem + 7, got, got)
        gather_rows_wait(wc.at[p], sem + 4)

    def flat(ref):
        return ref[...].reshape(rows, NB)

    def core(r_mat, z, h, k, corner):
        kr = exact(k, r_mat)
        s = h + kr + kr.T + exact(exact(r_mat, corner, TN), r_mat)
        return 0.5 * exact(exact(z, s, TN), z), exact(r_mat, z)

    zero_tile = jnp.zeros((NB, NB), jnp.float32)

    load.wait()
    for t in range(3):

        @pl.when(c == t)
        def _():
            for a in range(tiles):
                stg_r[a * NB : (a + 1) * NB, :] = abuf[pl.ds(a * NB * tiles, NB, stride=tiles), :]

            @pl.when(r == 0)
            def _():
                stg_r[0:NB, :] = zero_tile

        @pl.when(r == t)
        def _():
            for b in range(tiles):
                stg_c[b * NB : (b + 1) * NB, :] = abuf[pl.ds(b, NB, stride=tiles), :].T

            @pl.when(c == 0)
            def _():
                stg_c[0:NB, :] = zero_tile

        scatter(t)
    t_ref[...] = zero_tile
    scatter_wait(0)
    gather_rows_start(xc.at[0], 6)
    gather_cols_start(xr.at[0], 8)

    def to_parts(a, carry):
        for b in range(tiles):
            high, low = split(abuf[pl.ds(a * NB * tiles + b, NB, stride=tiles), :])
            at = pl.multiple_of(a * NB, NB)
            ahi[pl.ds(at, NB), b * NB : (b + 1) * NB] = high
            alo[pl.ds(at, NB), b * NB : (b + 1) * NB] = low
        return carry

    lax.fori_loop(0, tiles, to_parts, 0)
    scatter_wait(1)
    scatter_wait(2)
    gather_rows_mid(xc.at[0], 6)
    gather_rows_wait(xc.at[0], 6)
    x0c = flat(xc.at[0])
    first = jnp.where(c == 1, x0c[0:NB], 0.0)
    second = jnp.where(c == 2, x0c[0:NB], 0.0)
    sum_start(0, [dot3(x0c, x0c, TN), first, second], 9)

    def x0r():
        gather_cols_wait(xr.at[0], 8)
        return xr[0]

    product_start(0, x0c, x0r, 20)
    gather_rows_start(xc.at[1], 11)
    gather_cols_start(xr.at[1], 13)
    sum_mid(0, 3, 9)
    sum_wait(0, 3, 9)
    g_ref[...] = ar_res[0, 0]
    cholesky_blocks(g_ref, r0_ref, 0, NB // 8)
    product_mid(0, 20)
    gather_rows_mid(xc.at[1], 11)
    gather_rows_wait(xc.at[1], 11)
    x1c = flat(xc.at[1])
    first = jnp.where(c == 1, x1c[0:NB], 0.0)
    second = jnp.where(c == 2, x1c[0:NB], 0.0)
    sum_start(1, [dot3(flat(xc.at[0]), x1c, TN), first, second], 14)
    y_ref[...] = ar_res[0, 0] + exact(ar_res[0, 1], r0_ref[...], TN)
    product_late(0, 20)
    inverse_blocks(y_ref, t_ref, 0, NB // 16)
    sum_mid(1, 3, 14)
    inverse_blocks(y_ref, t_ref, NB // 16, NB // 8)
    product_wait(0, 20)
    gather_cols_wait(xr.at[1], 13)
    sum_wait(1, 3, 14)
    gather_rows_start(xc.at[2], 16)
    gather_cols_start(xr.at[2], 18)

    r0 = r0_ref[...]
    z0 = y_ref[...]
    k0 = ar_res[1, 0]
    b0, rz0 = core(r0, z0, h_res[0], k0, ar_res[1, 1])
    f01 = ar_res[0, 1] + r0
    f02 = ar_res[0, 2]
    c01 = exact(k0, z0, TN) + exact(ar_res[1, 1], rz0) - exact(f01, b0)
    coef = jnp.concatenate([z0, rz0, -b0], axis=0)
    back = jnp.concatenate([f01, c01], axis=1)

    def first_panel(f_ref, c_ref, p_ref, x0, x1, w, index):
        f_ref[...] = x0

        @pl.when(index == 1)
        def _():
            f_ref[0:NB, :] = f_ref[0:NB, :] + r0

        c_ref[...] = dot3(jnp.concatenate([w, x1, f_ref[...]], axis=1), coef, NN)

        @pl.when(index == 0)
        def _():
            c_ref[0:NB, :] = zero_tile

        left = jnp.concatenate([c_ref[...], f_ref[...]], axis=1)
        p_ref[...] = x1 - dot3(left, back, NT)

        @pl.when(index <= 1)
        def _():
            p_ref[0:NB, :] = zero_tile

    first_panel(f0c, c0c, f1c, flat(xc.at[0]), flat(xc.at[1]), flat(wc.at[0]), c)
    p1c = f1c[...]
    first = jnp.where(c == 2, p1c[0:NB], 0.0)
    left = jnp.concatenate([p1c, f0c[...], c0c[...]], axis=1)
    inner = dot3(left, p1c, TN)
    sum_start(2, [inner[0:NB], inner[NB : 2 * NB], inner[2 * NB :], first], 30)

    def p1r():
        first_panel(f0r, c0r, f1r, xr[0], xr[1], wr[0], r)
        return f1r[...]

    product_start(1, p1c, p1r, 34)
    sum_mid(2, 4, 30)
    sum_wait(2, 4, 30)
    g_ref[...] = ar_res[2, 0]
    cholesky_blocks(g_ref, r1_ref, 0, NB // 8)
    product_mid(1, 34)
    gather_rows_mid(xc.at[2], 16)
    gather_rows_wait(xc.at[2], 16)
    x2c = flat(xc.at[2])
    first = jnp.where(c == 2, x2c[0:NB], 0.0)
    left = jnp.concatenate([flat(xc.at[0]), f1c[...]], axis=1)
    inner = dot3(left, x2c, TN)
    sum_start(3, [inner[0:NB], inner[NB:], first], 32)
    y_ref[...] = ar_res[2, 0] + exact(ar_res[2, 3], r1_ref[...], TN)
    product_late(1, 34)
    inverse_blocks(y_ref, t_ref, 0, NB // 16)
    sum_mid(3, 3, 32)
    inverse_blocks(y_ref, t_ref, NB // 16, NB // 8)
    product_wait(1, 34)
    gather_cols_wait(xr.at[2], 18)
    sum_wait(3, 3, 32)

    r1 = r1_ref[...]
    z1 = y_ref[...]
    j1 = ar_res[2, 1]
    j2 = ar_res[2, 2]
    c02 = exact(ar_res[3, 0], z0, TN) + exact(ar_res[1, 2], rz0) - exact(f02, b0)
    cross = exact(j2, j1, TN)
    cf = exact(c02, f02, NT)
    k1 = ar_res[3, 1] - exact(j2, f02, (((0,), (1,)), ((), ()))) - exact(j1, c02, (((0,), (1,)), ((), ())))
    b1, rz1 = core(r1, z1, h_res[1] - cross - cross.T, k1, ar_res[3, 2] - cf - cf.T)
    coef = jnp.concatenate(
        [
            z1,
            rz1,
            -exact(j1, z1) - exact(f02, rz1, TN),
            -exact(j2, z1) - exact(c02, rz1, TN),
            -b1,
        ],
        axis=0,
    )

    def second_panel(f_ref, c_ref, c0, f0, x2, w, index):
        @pl.when(index == 2)
        def _():
            f_ref[0:NB, :] = f_ref[0:NB, :] + r1

        c_ref[...] = dot3(jnp.concatenate([w, x2, c0, f0, f_ref[...]], axis=1), coef, NN)

        @pl.when(index <= 1)
        def _():
            c_ref[0:NB, :] = zero_tile

    second_panel(f1c, c1c, c0c[...], f0c[...], flat(xc.at[2]), flat(wc.at[1]), c)
    second_panel(f1r, c1r, c0r[...], f0r[...], xr[2], wr[1], r)


def update_kernel(n, tiles, where_ref, a_ref, l0, l1, l2, l3, q0, q1, q2, q3, r0_ref, r1_ref, o_ref, hi, lo):
    a = pl.program_id(0)
    r = where_ref[0]
    c = where_ref[1]

    @pl.when(a == 0)
    def _():
        for i, q in enumerate((q0, q1, q2, q3)):
            high, low = split(q[...])
            hi[:, i * NB : (i + 1) * NB] = high
            lo[:, i * NB : (i + 1) * NB] = low

    lh, ll = split(jnp.concatenate([l0[...], l1[...], l2[...], l3[...]], axis=1))
    change = mxu(lh, hi[...], NT) + (mxu(lh, lo[...], NT) + mxu(ll, hi[...], NT))
    for b in range(tiles):
        at = pl.ds(b, NB, stride=tiles)
        o_ref[at, :] = a_ref[at, :] - change[:, b * NB : (b + 1) * NB]
    row_tile = a * n + r
    zero = jnp.zeros((NB, NB), jnp.float32)
    for p, r_ref in enumerate((r0_ref, r1_ref)):

        @pl.when((c == p) & (row_tile == p + 1))
        def _():
            o_ref[pl.ds(0, NB, stride=tiles), :] = -r_ref[...]

        @pl.when((c == p) & (row_tile > p + 1))
        def _():
            o_ref[pl.ds(0, NB, stride=tiles), :] = zero

        @pl.when(row_tile == p)
        def _():
            for b in range(tiles):
                at = pl.ds(b, NB, stride=tiles)

                @pl.when(b * n + c == p + 1)
                def _():
                    o_ref[at, :] = -r_ref[...].T

                @pl.when(b * n + c > p + 1)
                def _():
                    o_ref[at, :] = zero


def local(hamiltonian):
    tiles = hamiltonian.shape[0]
    n = lax.axis_size("row")
    rows = tiles * NB
    ch = rows // n
    pc = NB // n
    half = n // 2
    f32 = jnp.float32
    block = hamiltonian.reshape(rows * tiles, NB)
    side = jax.ShapeDtypeStruct((rows, NB), f32)
    square = jax.ShapeDtypeStruct((NB, NB), f32)
    vmem = pl.BlockSpec(memory_space=pltpu.VMEM)
    outs = pl.pallas_call(
        functools.partial(reduce_kernel, n, tiles),
        out_shape=[side] * 8 + [square] * 2,
        in_specs=[pl.BlockSpec(memory_space=pl.ANY)],
        out_specs=[vmem] * 10,
        scratch_shapes=[
            pltpu.VMEM((rows * tiles, NB), f32),
            pltpu.VMEM((rows, rows), jnp.bfloat16),
            pltpu.VMEM((rows, rows), jnp.bfloat16),
            pltpu.VMEM((rows, NB), f32),
            pltpu.VMEM((rows, NB), f32),
            pltpu.VMEM((3, rows, NB), f32),
            pltpu.VMEM((3, half, 2, ch, NB), f32),
            pltpu.VMEM((2, rows, NB), f32),
            pltpu.VMEM((2, n, ch, NB), f32),
            pltpu.VMEM((2, ch, NB), f32),
            pltpu.VMEM((2, rows, NB), f32),
            pltpu.VMEM((2, half, 2, ch, NB), f32),
            pltpu.VMEM((4, 4, NB, NB), f32),
            pltpu.VMEM((4, n, 4, pc, NB), f32),
            pltpu.VMEM((4, 4, NB, NB), f32),
            pltpu.VMEM((2, NB, NB), f32),
            pltpu.VMEM((2, n, pc, NB), f32),
            pltpu.VMEM((2, pc, NB), f32),
            pltpu.VMEM((2, n, pc, NB), f32),
            pltpu.VMEM((2, NB, NB), f32),
            pltpu.VMEM((NB, NB), f32),
            pltpu.VMEM((NB, NB), f32),
            pltpu.VMEM((NB, NB), f32),
            pltpu.SemaphoreType.DMA,
            pltpu.SemaphoreType.DMA((42,)),
            pltpu.SemaphoreType.DMA((42,)),
        ],
        compiler_params=pltpu.CompilerParams(
            collective_id=0, has_side_effects=True, vmem_limit_bytes=VMEM_LIMIT
        ),
        name="reduce_panels",
    )(block)
    c0r, f0r, c1r, f1r, c0c, f0c, c1c, f1c, r0, r1 = outs
    where = jnp.stack([lax.axis_index("row"), lax.axis_index("col")]).astype(jnp.int32)
    tile_spec = pl.BlockSpec((NB, NB), lambda a, *_: (a, 0))
    full_spec = pl.BlockSpec((rows, NB), lambda a, *_: (0, 0))
    square_spec = pl.BlockSpec((NB, NB), lambda a, *_: (0, 0))
    block_spec = pl.BlockSpec((NB * tiles, NB), lambda a, *_: (a, 0))
    result = pl.pallas_call(
        functools.partial(update_kernel, n, tiles),
        out_shape=jax.ShapeDtypeStruct((rows * tiles, NB), f32),
        grid_spec=pltpu.PrefetchScalarGridSpec(
            num_scalar_prefetch=1,
            grid=(tiles,),
            in_specs=[block_spec] + [tile_spec] * 4 + [full_spec] * 4 + [square_spec] * 2,
            out_specs=block_spec,
            scratch_shapes=[
                pltpu.VMEM((rows, 4 * NB), jnp.bfloat16),
                pltpu.VMEM((rows, 4 * NB), jnp.bfloat16),
            ],
        ),
        compiler_params=pltpu.CompilerParams(vmem_limit_bytes=VMEM_LIMIT),
        name="update_matrix",
    )(where, block, c0r, f0r, c1r, f1r, f0c, c0c, f1c, c1c, r0, r1)
    return result.reshape(hamiltonian.shape)


def solution(mesh):
    spec = P(None, "row", None, None, "col", None)
    return jax.shard_map(local, mesh=mesh, in_specs=(spec,), out_specs=spec, check_vma=False)
```

```python
import functools

import jax
import jax.numpy as jnp
from jax import lax
from jax.experimental import pallas as pl
from jax.experimental.pallas import tpu as pltpu
from jax.sharding import PartitionSpec as P

MESH = pl.DeviceIdType.MESH
NB = 128
NN = (((1,), (0,)), ((), ()))
NT = (((1,), (1,)), ((), ()))
TN = (((0,), (0,)), ((), ()))
TT = (((0,), (1,)), ((), ()))
VMEM_LIMIT = 56 << 20


def split(value):
    high = value.astype(jnp.bfloat16)
    low = (value - high.astype(jnp.float32)).astype(jnp.bfloat16)
    return high, low


def mxu(first, second, dims):
    return lax.dot_general(first, second, dims, preferred_element_type=jnp.float32)


def dot3(first, second, dims):
    fh, fl = split(first)
    sh, sl = split(second)
    return mxu(fh, sh, dims) + (mxu(fh, sl, dims) + mxu(fl, sh, dims))


def exact(first, second, dims=NN):
    return lax.dot_general(
        first, second, dims, precision=lax.Precision.HIGHEST, preferred_element_type=jnp.float32
    )


def iota(axis, shape):
    return lax.broadcasted_iota(jnp.int32, shape, axis)


def cholesky_blocks(g_ref, r_ref, first, last):
    sub = iota(0, (8, NB))
    lane = iota(1, (8, NB))

    def block(k, carry):
        base = pl.multiple_of(k * 8, 8)
        x = g_ref[pl.ds(base, 8), :]
        rolled = pltpu.roll(x, lax.rem(NB - base, NB), 1)
        cols = [jnp.broadcast_to(rolled[:, i : i + 1], (8, NB)) for i in range(8)]
        for i in range(8):
            scale = lax.rsqrt(cols[i][i : i + 1, :])
            column = cols[i] * scale
            below = jnp.where(sub > i, column, 0.0)
            row = x[i : i + 1, :] * scale
            x = jnp.where(sub == i, row, x - below * row)
            for m in range(i + 1, 8):
                cols[m] = cols[m] - below * column[m : m + 1, :]
        x = jnp.where(lane >= base + sub, x, 0.0)
        r_ref[pl.ds(base, 8), :] = x
        g_ref[...] -= exact(x, x, TN)
        return carry

    lax.fori_loop(first, last, block, 0)


def inverse_blocks(y_ref, t_ref, first, last):
    sub = iota(0, (8, NB))
    lane = iota(1, (8, NB))
    wide = iota(1, (NB, NB))

    def block(k, carry):
        base = pl.multiple_of(k * 8, 8)
        x = y_ref[pl.ds(base, 8), :]
        rolled = pltpu.roll(x, lax.rem(NB - base, NB), 1)
        cols = [jnp.broadcast_to(rolled[:, i : i + 1], (8, NB)) for i in range(8)]
        inside = (lane >= base) & (lane < base + 8)
        x = jnp.where(inside, jnp.where(lane - base == sub, 1.0, 0.0), x)
        for i in range(8):
            scale = 1.0 / cols[i][i : i + 1, :]
            factor = jnp.where(sub == i, 0.0, cols[i])
            row = x[i : i + 1, :] * scale
            x = jnp.where(sub == i, row, x - factor * row)
            for m in range(i + 1, 8):
                entry = cols[m][i : i + 1, :] * scale
                cols[m] = jnp.where(sub == i, entry, cols[m] - factor * entry)
        t_ref[pl.ds(base, 8), :] = x
        y = y_ref[...]
        chosen = (wide >= base) & (wide < base + 8)
        y_ref[...] = jnp.where(chosen, 0.0, y) - exact(jnp.where(chosen, y, 0.0), t_ref[...])
        y_ref[pl.ds(base, 8), :] = x
        t_ref[pl.ds(base, 8), :] = jnp.zeros((8, NB), jnp.float32)
        return carry

    lax.fori_loop(first, last, block, 0)


def reduce_kernel(n, tiles, *refs):
    rows = tiles * NB
    ch = rows // n
    pc = NB // n
    half = n // 2
    per_tile = NB // ch
    (
        a_hbm, out_hbm,
        abuf, ahi, alo, thi, tlo, stg_r, stg_c, xr, xc,
        wpart_r, wslot_r, wpart_c, wsib, wsum, wslot_c, wch, wr, wc,
        panel_r, panel_c, cor_r, cor_c, lh, ll, qh, ql,
        ar_src, ar_slot, ar_res, h_src, h_slot, h_piece, h_ex, h_res,
        g_ref, y_ref, t_ref, r0_ref, r1_ref, asem, osem, ss, rs,
    ) = refs
    r = lax.axis_index("row")
    c = lax.axis_index("col")
    parity = lax.rem(r, 2)
    level = r // 2
    sibling = (r + 1 - 2 * parity, c)

    load = pltpu.make_async_copy(a_hbm, abuf, asem)
    load.start()
    barrier = pltpu.get_barrier_semaphore()

    def greet(k, carry):
        pl.semaphore_signal(barrier, inc=1, device_id=(lax.rem(r + k, n), c), device_id_type=MESH)
        pl.semaphore_signal(barrier, inc=1, device_id=(r, lax.rem(c + k, n)), device_id_type=MESH)
        return carry

    lax.fori_loop(1, n, greet, 0)

    @pl.when(r != c)
    def _():
        pl.semaphore_signal(barrier, inc=1, device_id=(c, r), device_id_type=MESH)

    def send(src, dst, sem, device):
        pltpu.make_async_remote_copy(
            src, dst, ss.at[sem], rs.at[sem], device_id=device, device_id_type=MESH
        ).start()

    def over_cols(sem, src_of, dst_of):
        def one(k, carry):
            j = lax.rem(c + k, n)
            send(src_of(j), dst_of(j), sem, (r, j))
            return carry

        lax.fori_loop(1, n, one, 0)

    def over_rows(sem, src_of, dst_of):
        def one(k, carry):
            j = lax.rem(r + k, n)
            send(src_of(j), dst_of(j), sem, (j, c))
            return carry

        lax.fori_loop(1, n, one, 0)

    def wait_sent(sem, sent):
        pltpu.make_async_copy(sent, sent, ss.at[sem]).wait()

    def wait_received(sem, received):
        pltpu.make_async_copy(received, received, rs.at[sem]).wait()

    def wait(sem, part):
        wait_received(sem, part)
        wait_sent(sem, part)

    def scatter(t):
        @pl.when(c == t)
        def _():
            over_cols(
                t,
                lambda j: stg_r.at[pl.ds(j * ch, ch)],
                lambda j: xr.at[t, pl.ds(j * ch, ch)],
            )
            xr[t, pl.ds(t * ch, ch), :] = stg_r[pl.ds(t * ch, ch), :]

        @pl.when(r == t)
        def _():
            over_rows(
                3 + t,
                lambda j: stg_c.at[pl.ds(j * ch, ch)],
                lambda j: xc.at[t, j // 2, lax.rem(j, 2)],
            )
            xc[t, t // 2, t % 2] = stg_c[pl.ds(t * ch, ch), :]

    def scatter_wait(t):
        @pl.when(c == t)
        def _():
            wait_sent(t, stg_r.at[pl.ds(0, (n - 1) * ch)])

        @pl.when(c != t)
        def _():
            wait_received(t, xr.at[t, pl.ds(c * ch, ch)])

        @pl.when(r == t)
        def _():
            wait_sent(3 + t, stg_c.at[pl.ds(0, (n - 1) * ch)])

        @pl.when(r != t)
        def _():
            wait_received(3 + t, xc.at[t, level, parity])

    def gather_cols_start(buf, sem):
        mine = buf.at[pl.ds(c * ch, ch)]
        over_cols(sem, lambda j: mine, lambda j: mine)

    def gather_cols_wait(buf, sem):
        wait(sem, buf.at[pl.ds(0, (n - 1) * ch)])

    def gather_rows_start(buf, sem):
        mine = buf.at[level, parity]

        def one(k, carry):
            send(mine, mine, sem, (lax.rem(level + k, half) * 2 + parity, c))
            return carry

        lax.fori_loop(1, half, one, 0)

    def gather_rows_mid(buf, sem):
        wait(sem, buf.at[pl.ds(0, half - 1), 0])
        mine = buf.at[:, parity]
        send(mine, mine, sem + 1, sibling)

    def gather_rows_wait(buf, sem):
        wait(sem + 1, buf.at[:, 0])

    def sum_start(q, parts, sem, over, me):
        count = len(parts)
        for i, part in enumerate(parts):
            ar_src[q, i] = part
        over(
            sem,
            lambda j: ar_src.at[q, pl.ds(0, count), pl.ds(j * pc, pc)],
            lambda j: ar_slot.at[q, me, pl.ds(0, count)],
        )
        ar_slot[q, me, 0:count] = ar_src[q, 0:count, pl.ds(me * pc, pc), :]

    def sum_slots(q, count, sem):
        wait(sem, ar_slot.at[q, pl.ds(0, n - 1), pl.ds(0, count)])
        total = ar_slot[q, 0, 0:count]
        for j in range(1, n):
            total = total + ar_slot[q, j, 0:count]
        return total

    def sum_spread(q, count, sem, over, me):
        mine = (q, pl.ds(0, count), pl.ds(me * pc, pc))
        over(sem + 1, lambda j: ar_res.at[mine], lambda j: ar_res.at[mine])

    def sum_mid(q, count, sem, over, me):
        ar_res[q, 0:count, pl.ds(me * pc, pc), :] = sum_slots(q, count, sem)
        sum_spread(q, count, sem, over, me)

    def sum_wait(q, count, sem):
        wait(sem + 1, ar_res.at[q, pl.ds(0, count), pl.ds(0, (n - 1) * pc)])

    def all_start(p, part, sem, over, me):
        h_src[p] = part
        over(sem, lambda j: h_src.at[p, pl.ds(j * pc, pc)], lambda j: h_slot.at[p, me])
        h_slot[p, me] = h_src[p, pl.ds(me * pc, pc), :]

    def all_mid(p, sem, over, me):
        wait(sem, h_slot.at[p, pl.ds(0, n - 1)])
        total = h_slot[p, 0]
        for j in range(1, n):
            total = total + h_slot[p, j]
        h_piece[p] = total
        over(sem + 1, lambda j: h_piece.at[p], lambda j: h_ex.at[p, me])
        h_ex[p, me] = total

    def all_late(p, sem, over, me):
        wait(sem + 1, h_ex.at[p, pl.ds(0, n - 1)])
        total = h_ex[p, 0]
        for j in range(1, n):
            total = total + h_ex[p, j]
        h_res[p, pl.ds(me * pc, pc), :] = total
        mine = h_res.at[p, pl.ds(me * pc, pc)]
        over(sem + 2, lambda j: mine, lambda j: mine)

    def all_wait(p, sem):
        wait(sem + 2, h_res.at[p, pl.ds(0, (n - 1) * pc)])

    def tile_product(high_ref, low_ref, at, both):
        wide = mxu(high_ref[pl.ds(at, NB), :], both, NN)
        return wide[:, :NB] + (wide[:, NB:] + mxu(low_ref[pl.ds(at, NB), :], both[:, :NB], NN))

    def halves(panel):
        return jnp.concatenate(split(panel), axis=1)

    def flat(ref):
        return ref[...].reshape(rows, NB)

    def flip(value):
        return jnp.concatenate(
            [value[i * NB : (i + 1) * NB].T for i in range(tiles)], axis=1
        )

    def core(r_mat, z, h, k, corner):
        kr = exact(k, r_mat)
        s = h + kr + kr.T + exact(exact(r_mat, corner, TN), r_mat)
        return 0.5 * exact(exact(z, s, TN), z)

    zero_tile = jnp.zeros((NB, NB), jnp.float32)
    block_rows = min(rows, 2 * NB)

    def keep_left(i, value):
        lh[:, i * NB : (i + 1) * NB], ll[:, i * NB : (i + 1) * NB] = split(value)

    def keep_right(i, value):
        qh[i * NB : (i + 1) * NB, :], ql[i * NB : (i + 1) * NB, :] = split(flip(value))

    def apply(p, finish):
        depth = slice(2 * p * NB, 2 * (p + 1) * NB)

        def one(i, carry):
            at = pl.multiple_of(i * block_rows, block_rows)
            high = lh[pl.ds(at, block_rows), depth]
            low = ll[pl.ds(at, block_rows), depth]
            for b in range(0, tiles, 2):
                cols = slice(b * NB, (b + 2) * NB)
                change = mxu(high, qh[depth, cols], NN) + (
                    mxu(high, ql[depth, cols], NN) + mxu(low, qh[depth, cols], NN)
                )
                for k in range(block_rows // NB):
                    for j in range(2):
                        spot = pl.ds((at + k * NB) * tiles + b + j, NB, stride=tiles)
                        part = change[k * NB : (k + 1) * NB, j * NB : (j + 1) * NB]
                        abuf[spot, :] = abuf[spot, :] - part
            if finish:
                area = pl.ds(pl.multiple_of(at * tiles, block_rows), block_rows * tiles)
                pltpu.make_async_copy(abuf.at[area], out_hbm.at[area], osem).start()
            return carry

        lax.fori_loop(0, rows // block_rows, one, 0)

    def write_band(p, r_ref):
        @pl.when(c == p)
        def _():
            for a in range(tiles):
                spot = pl.ds(a * NB * tiles, NB, stride=tiles)

                @pl.when(a * n + r == p + 1)
                def _():
                    abuf[spot, :] = -r_ref[...]

                @pl.when(a * n + r > p + 1)
                def _():
                    abuf[spot, :] = zero_tile

        @pl.when(r == p)
        def _():
            for b in range(tiles):
                spot = pl.ds(b, NB, stride=tiles)

                @pl.when(b * n + c == p + 1)
                def _():
                    abuf[spot, :] = -r_ref[...].T

                @pl.when(b * n + c > p + 1)
                def _():
                    abuf[spot, :] = zero_tile

    load.wait()
    for t in range(3):

        @pl.when(c == t)
        def _():
            for a in range(tiles):
                stg_r[a * NB : (a + 1) * NB, :] = abuf[pl.ds(a * NB * tiles, NB, stride=tiles), :]

            @pl.when(r == 0)
            def _():
                stg_r[0:NB, :] = zero_tile

        @pl.when(r == t)
        def _():
            for b in range(tiles):
                stg_c[b * NB : (b + 1) * NB, :] = abuf[pl.ds(b, NB, stride=tiles), :].T

            @pl.when(c == 0)
            def _():
                stg_c[0:NB, :] = zero_tile

    pl.semaphore_wait(barrier, 2 * (n - 1) + jnp.where(r != c, 1, 0))
    for t in range(3):
        scatter(t)

    @pl.when(r == 0)
    def _():
        mine = stg_c[...]
        first = jnp.where(c == 1, mine[0:NB], 0.0)
        second = jnp.where(c == 2, mine[0:NB], 0.0)
        sum_start(0, [dot3(mine, mine, TN), first, second], 9, over_cols, c)

    t_ref[...] = zero_tile
    scatter_wait(0)
    gather_rows_start(xc.at[0], 6)

    g_mine = (0, pl.ds(0, 3), pl.ds(c * pc, pc))

    @pl.when(r == 0)
    def _():
        ar_res[0, 0:3, pl.ds(c * pc, pc), :] = sum_slots(0, 3, 9)
        over_rows(19, lambda j: ar_res.at[g_mine], lambda j: ar_res.at[g_mine])

    gather_cols_start(xr.at[0], 8)

    def to_parts(a, carry):
        at = pl.multiple_of(a * NB, NB)
        for b in range(tiles):
            high, low = split(abuf[pl.ds(a * NB * tiles + b, NB, stride=tiles), :])
            ahi[pl.ds(at, NB), b * NB : (b + 1) * NB] = high
            alo[pl.ds(at, NB), b * NB : (b + 1) * NB] = low
        return carry

    lax.fori_loop(0, tiles, to_parts, 0)

    @pl.when(r == 0)
    def _():
        wait_sent(19, ar_res.at[0, pl.ds(0, 3), pl.ds(0, (n - 1) * pc)])

    @pl.when(r != 0)
    def _():
        wait_received(19, ar_res.at[g_mine])

    sum_spread(0, 3, 9, over_cols, c)
    scatter_wait(1)
    gather_cols_start(xr.at[1], 13)
    scatter_wait(2)

    def to_flipped(b, carry):
        at = pl.multiple_of(b * NB, NB)
        for a in range(tiles):
            high, low = split(abuf[pl.ds(a * NB * tiles + b, NB, stride=tiles), :].T)
            thi[pl.ds(at, NB), a * NB : (a + 1) * NB] = high
            tlo[pl.ds(at, NB), a * NB : (a + 1) * NB] = low
        return carry

    lax.fori_loop(0, tiles, to_flipped, 0)
    gather_rows_mid(xc.at[0], 6)
    gather_rows_wait(xc.at[0], 6)

    both = halves(flat(xc.at[0]))

    def first_product(a, carry):
        at = pl.multiple_of(a * NB, NB)
        wpart_r[pl.ds(at, NB), :] = tile_product(ahi, alo, at, both)
        for i in range(per_tile):
            j = a * per_tile + i
            mine = wpart_r.at[pl.ds(j * ch, ch)]

            @pl.when(j != c)
            def _():
                send(mine, wslot_r.at[c], 20, (r, j))

        return carry

    lax.fori_loop(0, tiles, first_product, 0)
    wslot_r[c] = wpart_r[pl.ds(c * ch, ch), :]
    gather_rows_start(xc.at[1], 11)
    gather_cols_wait(xr.at[0], 8)
    all_start(0, dot3(xr[0], wpart_r[...], TN), 26, over_rows, r)
    gather_cols_wait(xr.at[1], 13)
    first = jnp.where(r == 1, xr[1, 0:NB], 0.0)
    second = jnp.where(r == 2, xr[1, 0:NB], 0.0)
    sum_start(1, [dot3(xr[0], xr[1], TN), first, second], 14, over_rows, r)
    sum_wait(0, 3, 9)
    g_ref[...] = ar_res[0, 0]
    cholesky_blocks(g_ref, r0_ref, 0, NB // 16)
    all_mid(0, 26, over_cols, c)
    sum_mid(1, 3, 14, over_rows, r)
    gather_rows_mid(xc.at[1], 11)
    gather_rows_start(xc.at[2], 16)
    cholesky_blocks(g_ref, r0_ref, NB // 16, NB // 8)

    wait(20, wslot_r.at[pl.ds(0, n - 1)])
    total = wslot_r[0]
    for j in range(1, n):
        total = total + wslot_r[j]
    wr[0, pl.ds(c * ch, ch), :] = total
    gather_cols_start(wr.at[0], 23)
    wch[0] = total

    @pl.when(r != c)
    def _():
        send(wch.at[0], wc.at[0, c // 2, lax.rem(c, 2)], 22, (c, r))

    @pl.when(r == c)
    def _():
        wc[0, level, parity] = total

    all_late(0, 26, over_rows, r)
    y_ref[...] = ar_res[0, 0] + exact(ar_res[0, 1], r0_ref[...], TN)
    inverse_blocks(y_ref, t_ref, 0, 3 * NB // 32)
    sum_wait(1, 3, 14)
    gather_rows_mid(xc.at[2], 16)

    @pl.when(r != c)
    def _():
        wait_received(22, wc.at[0, level, parity])
        wait_sent(22, wch.at[0])

    gather_rows_start(wc.at[0], 24)
    inverse_blocks(y_ref, t_ref, 3 * NB // 32, NB // 8)
    r0 = r0_ref[...]
    z0 = y_ref[...]
    k0 = ar_res[1, 0]
    rz0 = exact(r0, z0)
    f01 = ar_res[0, 1] + r0
    f02 = ar_res[0, 2]
    all_wait(0, 26)
    b0 = core(r0, z0, h_res[0], k0, ar_res[1, 1])
    c01 = exact(k0, z0, TN) + exact(ar_res[1, 1], rz0) - exact(f01, b0)
    coef = jnp.concatenate([z0, rz0, -b0], axis=0)
    back = jnp.concatenate([f01, c01], axis=1)

    def first_panel(f_ref, c_ref, x0, x1, w, index):
        f_ref[0] = x0

        @pl.when(index == 1)
        def _():
            f_ref[0, 0:NB, :] = f_ref[0, 0:NB, :] + r0

        c_ref[0] = dot3(jnp.concatenate([w, x1, f_ref[0]], axis=1), coef, NN)

        @pl.when(index == 0)
        def _():
            c_ref[0, 0:NB, :] = zero_tile

        left = jnp.concatenate([c_ref[0], f_ref[0]], axis=1)
        f_ref[1] = x1 - dot3(left, back, NT)

        @pl.when(index <= 1)
        def _():
            f_ref[1, 0:NB, :] = zero_tile

    gather_cols_wait(wr.at[0], 23)
    gather_cols_start(xr.at[2], 18)
    first_panel(panel_r, cor_r, xr[0], xr[1], wr[0], r)

    p1r = panel_r[1]
    first = jnp.where(r == 2, p1r[0:NB], 0.0)
    inner = dot3(jnp.concatenate([p1r, panel_r[0], cor_r[0]], axis=1), p1r, TN)
    sum_start(2, [inner[0:NB], inner[NB : 2 * NB], inner[2 * NB :], first], 30, over_rows, r)
    both = halves(p1r)

    def second_product(b, carry):
        at = pl.multiple_of(b * NB, NB)
        value = tile_product(thi, tlo, at, both).reshape(per_tile, ch, NB)
        for i in range(per_tile):
            j = b * per_tile + i
            wpart_c[j // 2, lax.rem(j, 2)] = value[i]
        return carry

    lax.fori_loop(0, tiles, second_product, 0)
    send(wpart_c.at[:, 1 - parity], wsib, 34, sibling)
    gather_rows_mid(wc.at[0], 24)
    sum_mid(2, 4, 30, over_rows, r)
    wait(34, wsib)
    wsum[...] = wpart_c[:, parity] + wsib[...]

    def spread(k, carry):
        to = lax.rem(level + k, half)
        send(wsum.at[to], wslot_c.at[level], 35, (to * 2 + parity, c))
        return carry

    lax.fori_loop(1, half, spread, 0)
    wslot_c[level] = wsum[level]
    gather_rows_wait(xc.at[1], 11)
    gather_rows_wait(xc.at[2], 16)
    gather_rows_wait(wc.at[0], 24)
    first_panel(panel_c, cor_c, flat(xc.at[0]), flat(xc.at[1]), flat(wc.at[0]), c)
    p1c = panel_c[1]
    all_start(1, dot3(p1c, flat(wpart_c), TN), 36, over_cols, c)
    x2c = flat(xc.at[2])
    first = jnp.where(c == 2, x2c[0:NB], 0.0)
    inner = dot3(jnp.concatenate([flat(xc.at[0]), p1c], axis=1), x2c, TN)
    sum_start(3, [inner[0:NB], inner[NB:], first], 32, over_cols, c)
    keep_left(0, cor_r[0])
    keep_left(1, panel_r[0])
    keep_right(0, panel_c[0])
    keep_right(1, cor_c[0])
    sum_wait(2, 4, 30)
    g_ref[...] = ar_res[2, 0]
    cholesky_blocks(g_ref, r1_ref, 0, NB // 16)

    wait(35, wslot_c.at[pl.ds(0, half - 1)])
    total = wslot_c[0]
    for j in range(1, half):
        total = total + wslot_c[j]
    wc[1, level, parity] = total
    gather_rows_start(wc.at[1], 39)
    wch[1] = total

    @pl.when(r != c)
    def _():
        send(wch.at[1], wr.at[1, pl.ds(r * ch, ch)], 41, (c, r))

    @pl.when(r == c)
    def _():
        wr[1, pl.ds(c * ch, ch), :] = total

    all_mid(1, 36, over_rows, r)
    sum_mid(3, 3, 32, over_cols, c)
    cholesky_blocks(g_ref, r1_ref, NB // 16, NB // 8)
    all_late(1, 36, over_cols, c)
    y_ref[...] = ar_res[2, 0] + exact(ar_res[2, 3], r1_ref[...], TN)

    @pl.when(r != c)
    def _():
        wait_received(41, wr.at[1, pl.ds(c * ch, ch)])
        wait_sent(41, wch.at[1])

    gather_cols_start(wr.at[1], 42)
    inverse_blocks(y_ref, t_ref, 0, NB // 16)
    gather_rows_mid(wc.at[1], 39)
    inverse_blocks(y_ref, t_ref, NB // 16, NB // 8)
    apply(0, False)
    write_band(0, r0_ref)
    write_band(1, r1_ref)
    r1 = r1_ref[...]
    z1 = y_ref[...]
    j1 = ar_res[2, 1]
    j2 = ar_res[2, 2]
    rz1 = exact(r1, z1)
    sum_wait(3, 3, 32)
    c02 = exact(ar_res[3, 0], z0, TN) + exact(ar_res[1, 2], rz0) - exact(f02, b0)
    cross = exact(j2, j1, TN)
    cf = exact(c02, f02, NT)
    k1 = ar_res[3, 1] - exact(j2, f02, TT) - exact(j1, c02, TT)
    fold1 = -exact(j1, z1) - exact(f02, rz1, TN)
    fold2 = -exact(j2, z1) - exact(c02, rz1, TN)
    all_wait(1, 36)
    b1 = core(r1, z1, h_res[1] - cross - cross.T, k1, ar_res[3, 2] - cf - cf.T)
    coef = jnp.concatenate([z1, rz1, fold1, fold2, -b1], axis=0)

    def second_panel(f_ref, c_ref, x2, w, index):
        @pl.when(index == 2)
        def _():
            f_ref[1, 0:NB, :] = f_ref[1, 0:NB, :] + r1

        c_ref[1] = dot3(jnp.concatenate([w, x2, c_ref[0], f_ref[0], f_ref[1]], axis=1), coef, NN)

        @pl.when(index <= 1)
        def _():
            c_ref[1, 0:NB, :] = zero_tile

    gather_rows_wait(wc.at[1], 39)
    second_panel(panel_c, cor_c, flat(xc.at[2]), flat(wc.at[1]), c)
    keep_right(2, panel_c[1])
    keep_right(3, cor_c[1])
    gather_cols_wait(xr.at[2], 18)
    gather_cols_wait(wr.at[1], 42)
    second_panel(panel_r, cor_r, xr[2], wr[1], r)
    keep_left(2, cor_r[1])
    keep_left(3, panel_r[1])
    apply(1, True)
    pltpu.make_async_copy(abuf, out_hbm, osem).wait()


def local(hamiltonian):
    tiles = hamiltonian.shape[0]
    n = lax.axis_size("row")
    rows = tiles * NB
    ch = rows // n
    pc = NB // n
    half = n // 2
    f32 = jnp.float32
    bf16 = jnp.bfloat16
    block = hamiltonian.reshape(rows * tiles, NB)
    shapes = [
        ((rows * tiles, NB), f32),
        ((rows, rows), bf16),
        ((rows, rows), bf16),
        ((rows, rows), bf16),
        ((rows, rows), bf16),
        ((rows, NB), f32),
        ((rows, NB), f32),
        ((3, rows, NB), f32),
        ((3, half, 2, ch, NB), f32),
        ((rows, NB), f32),
        ((n, ch, NB), f32),
        ((half, 2, ch, NB), f32),
        ((half, ch, NB), f32),
        ((half, ch, NB), f32),
        ((half, ch, NB), f32),
        ((2, ch, NB), f32),
        ((2, rows, NB), f32),
        ((2, half, 2, ch, NB), f32),
        ((2, rows, NB), f32),
        ((2, rows, NB), f32),
        ((2, rows, NB), f32),
        ((2, rows, NB), f32),
        ((rows, 4 * NB), bf16),
        ((rows, 4 * NB), bf16),
        ((4 * NB, rows), bf16),
        ((4 * NB, rows), bf16),
        ((4, 4, NB, NB), f32),
        ((4, n, 4, pc, NB), f32),
        ((4, 4, NB, NB), f32),
        ((2, NB, NB), f32),
        ((2, n, pc, NB), f32),
        ((2, pc, NB), f32),
        ((2, n, pc, NB), f32),
        ((2, NB, NB), f32),
    ] + [((NB, NB), f32)] * 5
    result = pl.pallas_call(
        functools.partial(reduce_kernel, n, tiles),
        out_shape=jax.ShapeDtypeStruct((rows * tiles, NB), f32),
        in_specs=[pl.BlockSpec(memory_space=pl.ANY)],
        out_specs=pl.BlockSpec(memory_space=pl.ANY),
        scratch_shapes=[pltpu.VMEM(*shape) for shape in shapes]
        + [
            pltpu.SemaphoreType.DMA,
            pltpu.SemaphoreType.DMA,
            pltpu.SemaphoreType.DMA((43,)),
            pltpu.SemaphoreType.DMA((43,)),
        ],
        compiler_params=pltpu.CompilerParams(
            collective_id=0, has_side_effects=True, vmem_limit_bytes=VMEM_LIMIT
        ),
        name="reduce_panels",
    )(block)
    return result.reshape(hamiltonian.shape)


def solution(mesh):
    spec = P(None, "row", None, None, "col", None)
    return jax.shard_map(local, mesh=mesh, in_specs=(spec,), out_specs=spec, check_vma=False)
```

```python
import functools

import jax
import jax.numpy as jnp
from jax import lax
from jax.experimental import pallas as pl
from jax.experimental.pallas import tpu as pltpu
from jax.sharding import PartitionSpec as P

MESH = pl.DeviceIdType.MESH
NB = 128
NN = (((1,), (0,)), ((), ()))
NT = (((1,), (1,)), ((), ()))
TN = (((0,), (0,)), ((), ()))
TT = (((0,), (1,)), ((), ()))
VMEM_LIMIT = 56 << 20
CHOL_WIDTH = 32
INV_WIDTH = 16
CHOL_BLOCKS = NB // CHOL_WIDTH
INV_BLOCKS = NB // INV_WIDTH


def split(value):
    high = value.astype(jnp.bfloat16)
    low = (value - high.astype(jnp.float32)).astype(jnp.bfloat16)
    return high, low


def mxu(first, second, dims):
    return lax.dot_general(first, second, dims, preferred_element_type=jnp.float32)


def dot3(first, second, dims):
    fh, fl = split(first)
    sh, sl = split(second)
    return mxu(fh, sh, dims) + (mxu(fh, sl, dims) + mxu(fl, sh, dims))


def exact(first, second, dims=NN):
    return lax.dot_general(
        first, second, dims, precision=lax.Precision.HIGHEST, preferred_element_type=jnp.float32
    )


def iota(axis, shape):
    return lax.broadcasted_iota(jnp.int32, shape, axis)


def leading_columns(x, base, width):
    rolled = pltpu.roll(x, lax.rem(NB - base, NB), 1)
    return [jnp.broadcast_to(rolled[:, i : i + 1], (width, NB)) for i in range(width)]


def cholesky_blocks(g_ref, r_ref, first, last):
    width = CHOL_WIDTH
    sub = iota(0, (width, NB))
    lane = iota(1, (width, NB))

    def block(k, carry):
        base = pl.multiple_of(k * width, width)
        x = g_ref[pl.ds(base, width), :]
        cols = leading_columns(x, base, width)
        for i in range(width):
            scale = lax.rsqrt(cols[i][i : i + 1, :])
            column = cols[i] * scale
            below = jnp.where(sub > i, column, 0.0)
            row = x[i : i + 1, :] * scale
            x = jnp.where(sub == i, row, x - below * row)
            for m in range(i + 1, width):
                cols[m] = cols[m] - below * column[m : m + 1, :]
        x = jnp.where(lane >= base + sub, x, 0.0)
        r_ref[pl.ds(base, width), :] = x
        g_ref[...] -= exact(x, x, TN)
        return carry

    lax.fori_loop(first, last, block, 0)


def inverse_blocks(y_ref, t_ref, first, last):
    width = INV_WIDTH
    sub = iota(0, (width, NB))
    lane = iota(1, (width, NB))
    wide = iota(1, (NB, NB))

    def block(k, carry):
        base = pl.multiple_of(k * width, width)
        x = y_ref[pl.ds(base, width), :]
        cols = leading_columns(x, base, width)
        inside = (lane >= base) & (lane < base + width)
        x = jnp.where(inside, jnp.where(lane - base == sub, 1.0, 0.0), x)
        for i in range(width):
            scale = 1.0 / cols[i][i : i + 1, :]
            factor = jnp.where(sub == i, 0.0, cols[i])
            row = x[i : i + 1, :] * scale
            x = jnp.where(sub == i, row, x - factor * row)
            for m in range(i + 1, width):
                entry = cols[m][i : i + 1, :] * scale
                cols[m] = jnp.where(sub == i, entry, cols[m] - factor * entry)
        t_ref[pl.ds(base, width), :] = x
        y = y_ref[...]
        chosen = (wide >= base) & (wide < base + width)
        y_ref[...] = jnp.where(chosen, 0.0, y) - exact(jnp.where(chosen, y, 0.0), t_ref[...])
        y_ref[pl.ds(base, width), :] = x
        t_ref[pl.ds(base, width), :] = jnp.zeros((width, NB), jnp.float32)
        return carry

    lax.fori_loop(first, last, block, 0)


def reduce_kernel(n, tiles, *refs):
    rows = tiles * NB
    ch = rows // n
    pc = NB // n
    half = n // 2
    per_tile = NB // ch
    (
        a_hbm, a_out, lh_out, ll_out, qh_out, ql_out,
        abuf, ahi, alo, thi, tlo, stg_r, stg_c, xr, xc,
        wpart_r, wslot_r, wpart_c, wsib, wsum, wslot_c, wch, wr, wc,
        panel_r, panel_c, cor_r, cor_c, lh, ll, qh, ql,
        ar_src, ar_slot, ar_res, h_src, h_slot, h_piece, h_ex, h_res,
        g_ref, y_ref, t_ref, r0_ref, r1_ref, asem, osem, osem2, osem3, osem4, ss, rs,
    ) = refs
    r = lax.axis_index("row")
    c = lax.axis_index("col")
    parity = lax.rem(r, 2)
    level = r // 2
    sibling = (r + 1 - 2 * parity, c)

    load = pltpu.make_async_copy(a_hbm, abuf, asem)
    load.start()
    barrier = pltpu.get_barrier_semaphore()

    def greet(k, carry):
        pl.semaphore_signal(barrier, inc=1, device_id=(lax.rem(r + k, n), c), device_id_type=MESH)
        pl.semaphore_signal(barrier, inc=1, device_id=(r, lax.rem(c + k, n)), device_id_type=MESH)
        return carry

    lax.fori_loop(1, n, greet, 0)

    @pl.when(r != c)
    def _():
        pl.semaphore_signal(barrier, inc=1, device_id=(c, r), device_id_type=MESH)

    def send(src, dst, sem, device):
        pltpu.make_async_remote_copy(
            src, dst, ss.at[sem], rs.at[sem], device_id=device, device_id_type=MESH
        ).start()

    def over_cols(sem, src_of, dst_of):
        def one(k, carry):
            j = lax.rem(c + k, n)
            send(src_of(j), dst_of(j), sem, (r, j))
            return carry

        lax.fori_loop(1, n, one, 0)

    def over_rows(sem, src_of, dst_of):
        def one(k, carry):
            j = lax.rem(r + k, n)
            send(src_of(j), dst_of(j), sem, (j, c))
            return carry

        lax.fori_loop(1, n, one, 0)

    def wait_sent(sem, sent):
        pltpu.make_async_copy(sent, sent, ss.at[sem]).wait()

    def wait_received(sem, received):
        pltpu.make_async_copy(received, received, rs.at[sem]).wait()

    def wait(sem, part):
        wait_received(sem, part)
        wait_sent(sem, part)

    def scatter(t):
        @pl.when(c == t)
        def _():
            over_cols(
                t,
                lambda j: stg_r.at[pl.ds(j * ch, ch)],
                lambda j: xr.at[t, pl.ds(j * ch, ch)],
            )
            xr[t, pl.ds(t * ch, ch), :] = stg_r[pl.ds(t * ch, ch), :]

        @pl.when(r == t)
        def _():
            over_rows(
                3 + t,
                lambda j: stg_c.at[pl.ds(j * ch, ch)],
                lambda j: xc.at[t, j // 2, lax.rem(j, 2)],
            )
            xc[t, t // 2, t % 2] = stg_c[pl.ds(t * ch, ch), :]

    def scatter_wait(t):
        @pl.when(c == t)
        def _():
            wait_sent(t, stg_r.at[pl.ds(0, (n - 1) * ch)])

        @pl.when(c != t)
        def _():
            wait_received(t, xr.at[t, pl.ds(c * ch, ch)])

        @pl.when(r == t)
        def _():
            wait_sent(3 + t, stg_c.at[pl.ds(0, (n - 1) * ch)])

        @pl.when(r != t)
        def _():
            wait_received(3 + t, xc.at[t, level, parity])

    def gather_cols_start(buf, sem):
        mine = buf.at[pl.ds(c * ch, ch)]
        over_cols(sem, lambda j: mine, lambda j: mine)

    def gather_cols_wait(buf, sem):
        wait(sem, buf.at[pl.ds(0, (n - 1) * ch)])

    def gather_rows_start(buf, sem):
        mine = buf.at[level, parity]

        def one(k, carry):
            send(mine, mine, sem, (lax.rem(level + k, half) * 2 + parity, c))
            return carry

        lax.fori_loop(1, half, one, 0)

    def gather_rows_mid(buf, sem):
        wait(sem, buf.at[pl.ds(0, half - 1), 0])
        mine = buf.at[:, parity]
        send(mine, mine, sem + 1, sibling)

    def gather_rows_wait(buf, sem):
        wait(sem + 1, buf.at[:, 0])

    def sum_start(q, parts, sem, over, me):
        count = len(parts)
        for i, part in enumerate(parts):
            ar_src[q, i] = part
        over(
            sem,
            lambda j: ar_src.at[q, pl.ds(0, count), pl.ds(j * pc, pc)],
            lambda j: ar_slot.at[q, me, pl.ds(0, count)],
        )
        ar_slot[q, me, 0:count] = ar_src[q, 0:count, pl.ds(me * pc, pc), :]

    def sum_slots(q, count, sem):
        wait(sem, ar_slot.at[q, pl.ds(0, n - 1), pl.ds(0, count)])
        total = ar_slot[q, 0, 0:count]
        for j in range(1, n):
            total = total + ar_slot[q, j, 0:count]
        return total

    def sum_spread(q, count, sem, over, me):
        mine = (q, pl.ds(0, count), pl.ds(me * pc, pc))
        over(sem + 1, lambda j: ar_res.at[mine], lambda j: ar_res.at[mine])

    def sum_mid(q, count, sem, over, me):
        ar_res[q, 0:count, pl.ds(me * pc, pc), :] = sum_slots(q, count, sem)
        sum_spread(q, count, sem, over, me)

    def sum_wait(q, count, sem):
        wait(sem + 1, ar_res.at[q, pl.ds(0, count), pl.ds(0, (n - 1) * pc)])

    def all_start(p, part, sem, over, me):
        h_src[p] = part
        over(sem, lambda j: h_src.at[p, pl.ds(j * pc, pc)], lambda j: h_slot.at[p, me])
        h_slot[p, me] = h_src[p, pl.ds(me * pc, pc), :]

    def all_mid(p, sem, over, me):
        wait(sem, h_slot.at[p, pl.ds(0, n - 1)])
        total = h_slot[p, 0]
        for j in range(1, n):
            total = total + h_slot[p, j]
        h_piece[p] = total
        over(sem + 1, lambda j: h_piece.at[p], lambda j: h_ex.at[p, me])
        h_ex[p, me] = total

    def all_late(p, sem, over, me):
        wait(sem + 1, h_ex.at[p, pl.ds(0, n - 1)])
        total = h_ex[p, 0]
        for j in range(1, n):
            total = total + h_ex[p, j]
        h_res[p, pl.ds(me * pc, pc), :] = total
        mine = h_res.at[p, pl.ds(me * pc, pc)]
        over(sem + 2, lambda j: mine, lambda j: mine)

    def all_wait(p, sem):
        wait(sem + 2, h_res.at[p, pl.ds(0, (n - 1) * pc)])

    def tile_product(high_ref, low_ref, at, both):
        wide = mxu(high_ref[pl.ds(at, NB), :], both, NN)
        return wide[:, :NB] + (wide[:, NB:] + mxu(low_ref[pl.ds(at, NB), :], both[:, :NB], NN))

    def halves(panel):
        return jnp.concatenate(split(panel), axis=1)

    def flat(ref):
        return ref[...].reshape(rows, NB)

    def flip(value):
        return jnp.concatenate(
            [value[i * NB : (i + 1) * NB].T for i in range(tiles)], axis=1
        )

    def known_part(r_mat, k, corner):
        kr = exact(k, r_mat)
        return kr + kr.T + exact(exact(r_mat, corner, TN), r_mat)

    def core(z, inner_sum):
        return 0.5 * exact(exact(z, inner_sum, TN), z)

    zero_tile = jnp.zeros((NB, NB), jnp.float32)
    block_rows = min(rows, 2 * NB)

    def keep_left(p, first, second):
        for i, value in enumerate((first, second)):
            spot = slice(i * NB, (i + 1) * NB)
            lh[p, :, spot], ll[p, :, spot] = split(value)

    def keep_right(p, first, second):
        for i, value in enumerate((first, second)):
            spot = slice(i * NB, (i + 1) * NB)
            qh[p, spot, :], ql[p, spot, :] = split(flip(value))

    def apply_first():
        def one(i, carry):
            at = pl.multiple_of(i * block_rows, block_rows)
            high = lh[0, pl.ds(at, block_rows)]
            low = ll[0, pl.ds(at, block_rows)]
            for b in range(0, tiles, 2):
                cols = slice(b * NB, (b + 2) * NB)
                change = mxu(high, qh[0, :, cols], NN) + (
                    mxu(high, ql[0, :, cols], NN) + mxu(low, qh[0, :, cols], NN)
                )
                for k in range(block_rows // NB):
                    for j in range(2):
                        spot = pl.ds((at + k * NB) * tiles + b + j, NB, stride=tiles)
                        part = change[k * NB : (k + 1) * NB, j * NB : (j + 1) * NB]
                        abuf[spot, :] = abuf[spot, :] - part
            return carry

        lax.fori_loop(0, rows // block_rows, one, 0)

    def write_band(p, r_ref):
        @pl.when(c == p)
        def _():
            for a in range(tiles):
                spot = pl.ds(a * NB * tiles, NB, stride=tiles)

                @pl.when(a * n + r == p + 1)
                def _():
                    abuf[spot, :] = -r_ref[...]

                @pl.when(a * n + r > p + 1)
                def _():
                    abuf[spot, :] = zero_tile

        @pl.when(r == p)
        def _():
            for b in range(tiles):
                spot = pl.ds(b, NB, stride=tiles)

                @pl.when(b * n + c == p + 1)
                def _():
                    abuf[spot, :] = -r_ref[...].T

                @pl.when(b * n + c > p + 1)
                def _():
                    abuf[spot, :] = zero_tile

    load.wait()
    for t in range(3):

        @pl.when(c == t)
        def _():
            for a in range(tiles):
                stg_r[a * NB : (a + 1) * NB, :] = abuf[pl.ds(a * NB * tiles, NB, stride=tiles), :]

            @pl.when(r == 0)
            def _():
                stg_r[0:NB, :] = zero_tile

        @pl.when(r == t)
        def _():
            for b in range(tiles):
                stg_c[b * NB : (b + 1) * NB, :] = abuf[pl.ds(b, NB, stride=tiles), :].T

            @pl.when(c == 0)
            def _():
                stg_c[0:NB, :] = zero_tile

    pl.semaphore_wait(barrier, 2 * (n - 1) + jnp.where(r != c, 1, 0))
    for t in range(3):
        scatter(t)

    @pl.when(r == 0)
    def _():
        mine = stg_c[...]
        first = jnp.where(c == 1, mine[0:NB], 0.0)
        second = jnp.where(c == 2, mine[0:NB], 0.0)
        sum_start(0, [dot3(mine, mine, TN), first, second], 9, over_cols, c)

    t_ref[...] = zero_tile
    g_mine = (0, pl.ds(0, 3), pl.ds(c * pc, pc))

    @pl.when(r == 0)
    def _():
        ar_res[0, 0:3, pl.ds(c * pc, pc), :] = sum_slots(0, 3, 9)
        over_rows(19, lambda j: ar_res.at[g_mine], lambda j: ar_res.at[g_mine])

    scatter_wait(0)
    gather_rows_start(xc.at[0], 6)
    gather_cols_start(xr.at[0], 8)

    def to_parts(a, carry):
        at = pl.multiple_of(a * NB, NB)
        for b in range(tiles):
            high, low = split(abuf[pl.ds(a * NB * tiles + b, NB, stride=tiles), :])
            ahi[pl.ds(at, NB), b * NB : (b + 1) * NB] = high
            alo[pl.ds(at, NB), b * NB : (b + 1) * NB] = low
        return carry

    lax.fori_loop(0, tiles, to_parts, 0)

    def to_flipped(b, carry):
        at = pl.multiple_of(b * NB, NB)
        for a in range(tiles):
            high, low = split(abuf[pl.ds(a * NB * tiles + b, NB, stride=tiles), :].T)
            thi[pl.ds(at, NB), a * NB : (a + 1) * NB] = high
            tlo[pl.ds(at, NB), a * NB : (a + 1) * NB] = low
        return carry

    lax.fori_loop(0, tiles // 2, to_flipped, 0)

    @pl.when(r == 0)
    def _():
        wait_sent(19, ar_res.at[0, pl.ds(0, 3), pl.ds(0, (n - 1) * pc)])

    @pl.when(r != 0)
    def _():
        wait_received(19, ar_res.at[g_mine])

    sum_spread(0, 3, 9, over_cols, c)
    scatter_wait(1)
    scatter_wait(2)
    gather_rows_mid(xc.at[0], 6)
    gather_cols_start(xr.at[1], 13)
    gather_rows_wait(xc.at[0], 6)

    both = halves(flat(xc.at[0]))

    def first_product(a, carry):
        at = pl.multiple_of(a * NB, NB)
        wpart_r[pl.ds(at, NB), :] = tile_product(ahi, alo, at, both)
        for i in range(per_tile):
            j = a * per_tile + i
            mine = wpart_r.at[pl.ds(j * ch, ch)]

            @pl.when(j != c)
            def _():
                send(mine, wslot_r.at[c], 20, (r, j))

        return carry

    lax.fori_loop(0, tiles, first_product, 0)
    wslot_r[c] = wpart_r[pl.ds(c * ch, ch), :]
    gather_cols_wait(xr.at[0], 8)
    all_start(0, dot3(xr[0], wpart_r[...], TN), 26, over_rows, r)
    gather_rows_start(xc.at[1], 11)
    sum_wait(0, 3, 9)
    g_ref[...] = ar_res[0, 0]
    cholesky_blocks(g_ref, r0_ref, 0, CHOL_BLOCKS)
    gather_cols_wait(xr.at[1], 13)
    first = jnp.where(r == 1, xr[1, 0:NB], 0.0)
    second = jnp.where(r == 2, xr[1, 0:NB], 0.0)
    sum_start(1, [dot3(xr[0], xr[1], TN), first, second], 14, over_rows, r)
    all_mid(0, 26, over_cols, c)
    y_ref[...] = ar_res[0, 0] + exact(ar_res[0, 1], r0_ref[...], TN)
    inverse_blocks(y_ref, t_ref, 0, INV_BLOCKS // 2)

    wait(20, wslot_r.at[pl.ds(0, n - 1)])
    total = wslot_r[0]
    for j in range(1, n):
        total = total + wslot_r[j]
    wr[0, pl.ds(c * ch, ch), :] = total
    gather_cols_start(wr.at[0], 23)
    wch[0] = total

    @pl.when(r != c)
    def _():
        send(wch.at[0], wc.at[0, c // 2, lax.rem(c, 2)], 22, (c, r))

    @pl.when(r == c)
    def _():
        wc[0, level, parity] = total

    sum_mid(1, 3, 14, over_rows, r)
    all_late(0, 26, over_rows, r)
    gather_rows_mid(xc.at[1], 11)
    gather_rows_start(xc.at[2], 16)
    inverse_blocks(y_ref, t_ref, INV_BLOCKS // 2, INV_BLOCKS)
    lax.fori_loop(tiles // 2, tiles, to_flipped, 0)

    @pl.when(r != c)
    def _():
        wait_received(22, wc.at[0, level, parity])
        wait_sent(22, wch.at[0])

    gather_rows_start(wc.at[0], 24)
    sum_wait(1, 3, 14)
    r0 = r0_ref[...]
    z0 = y_ref[...]
    k0 = ar_res[1, 0]
    rz0 = exact(r0, z0)
    f01 = ar_res[0, 1] + r0
    f02 = ar_res[0, 2]
    known = known_part(r0, k0, ar_res[1, 1])
    c01 = exact(k0, z0, TN) + exact(ar_res[1, 1], rz0)
    all_wait(0, 26)
    b0 = core(z0, h_res[0] + known)
    c01 = c01 - exact(f01, b0)
    coef = jnp.concatenate([z0, rz0, -b0], axis=0)
    carried = exact(coef, f01, NT)
    last = carried[2 * NB :] + c01.T
    coef = jnp.concatenate(
        [coef, jnp.concatenate([carried[: 2 * NB], last], axis=0)], axis=1
    )

    def first_panel(f_ref, c_ref, x0, x1, w, index):
        f_ref[0] = x0

        @pl.when(index == 1)
        def _():
            f_ref[0, 0:NB, :] = f_ref[0, 0:NB, :] + r0

        out = dot3(jnp.concatenate([w, x1, f_ref[0]], axis=1), coef, NN)
        c_ref[0] = out[:, :NB]
        f_ref[1] = x1 - out[:, NB:]

        @pl.when(index == 0)
        def _():
            c_ref[0, 0:NB, :] = zero_tile

        @pl.when(index <= 1)
        def _():
            f_ref[1, 0:NB, :] = zero_tile

    gather_cols_wait(wr.at[0], 23)
    gather_cols_start(xr.at[2], 18)
    first_panel(panel_r, cor_r, xr[0], xr[1], wr[0], r)

    p1r = panel_r[1]
    first = jnp.where(r == 2, p1r[0:NB], 0.0)
    inner = dot3(p1r, jnp.concatenate([p1r, panel_r[0], cor_r[0]], axis=1), TN)
    sum_start(2, [inner[:, 0:NB], inner[:, NB : 2 * NB], inner[:, 2 * NB :], first], 30, over_rows, r)
    both = halves(p1r)

    def second_product(b, carry):
        at = pl.multiple_of(b * NB, NB)
        value = tile_product(thi, tlo, at, both).reshape(per_tile, ch, NB)
        for i in range(per_tile):
            j = b * per_tile + i
            wpart_c[j // 2, lax.rem(j, 2)] = value[i]
        return carry

    lax.fori_loop(0, tiles, second_product, 0)
    send(wpart_c.at[:, 1 - parity], wsib, 34, sibling)
    sum_mid(2, 4, 30, over_rows, r)
    wait(34, wsib)
    wsum[...] = wpart_c[:, parity] + wsib[...]

    def spread(k, carry):
        to = lax.rem(level + k, half)
        send(wsum.at[to], wslot_c.at[level], 35, (to * 2 + parity, c))
        return carry

    lax.fori_loop(1, half, spread, 0)
    wslot_c[level] = wsum[level]
    gather_rows_mid(xc.at[2], 16)
    gather_rows_mid(wc.at[0], 24)
    gather_rows_wait(xc.at[1], 11)
    gather_rows_wait(xc.at[2], 16)
    gather_rows_wait(wc.at[0], 24)
    first_panel(panel_c, cor_c, flat(xc.at[0]), flat(xc.at[1]), flat(wc.at[0]), c)
    p1c = panel_c[1]
    all_start(1, dot3(p1c, flat(wpart_c), TN), 36, over_cols, c)
    x2c = flat(xc.at[2])
    first = jnp.where(c == 2, x2c[0:NB], 0.0)
    inner = dot3(x2c, jnp.concatenate([flat(xc.at[0]), p1c], axis=1), TN)
    sum_start(3, [inner[:, 0:NB], inner[:, NB:], first], 32, over_cols, c)
    sum_wait(2, 4, 30)
    g_ref[...] = ar_res[2, 0]
    cholesky_blocks(g_ref, r1_ref, 0, CHOL_BLOCKS)
    all_mid(1, 36, over_rows, r)

    wait(35, wslot_c.at[pl.ds(0, half - 1)])
    total = wslot_c[0]
    for j in range(1, half):
        total = total + wslot_c[j]
    wc[1, level, parity] = total
    gather_rows_start(wc.at[1], 39)
    wch[1] = total

    @pl.when(r != c)
    def _():
        send(wch.at[1], wr.at[1, pl.ds(r * ch, ch)], 41, (c, r))

    @pl.when(r == c)
    def _():
        wr[1, pl.ds(c * ch, ch), :] = total

    sum_mid(3, 3, 32, over_cols, c)
    y_ref[...] = ar_res[2, 0] + exact(ar_res[2, 3], r1_ref[...], TN)
    inverse_blocks(y_ref, t_ref, 0, INV_BLOCKS // 2)
    all_late(1, 36, over_cols, c)
    inverse_blocks(y_ref, t_ref, INV_BLOCKS // 2, INV_BLOCKS)

    @pl.when(r != c)
    def _():
        wait_received(41, wr.at[1, pl.ds(c * ch, ch)])
        wait_sent(41, wch.at[1])

    gather_cols_start(wr.at[1], 42)
    keep_left(0, cor_r[0], panel_r[0])
    keep_right(0, panel_c[0], cor_c[0])
    apply_first()
    write_band(0, r0_ref)
    write_band(1, r1_ref)
    pltpu.make_async_copy(abuf, a_out, asem).start()
    gather_rows_mid(wc.at[1], 39)
    r1 = r1_ref[...]
    z1 = y_ref[...]
    j1t = ar_res[2, 1]
    j2t = ar_res[2, 2]
    rz1 = exact(r1, z1)
    sum_wait(3, 3, 32)
    c02 = exact(ar_res[3, 0], z0) + exact(ar_res[1, 2], rz0) - exact(f02, b0)
    cross = exact(j2t, j1t, NT)
    cf = exact(c02, f02, NT)
    k1 = ar_res[3, 1].T - exact(j2t, f02, NT) - exact(j1t, c02, NT)
    known = known_part(r1, k1, ar_res[3, 2] - cf - cf.T) - cross - cross.T
    fold1 = -exact(j1t, z1, TN) - exact(f02, rz1, TN)
    fold2 = -exact(j2t, z1, TN) - exact(c02, rz1, TN)
    all_wait(1, 36)
    b1 = core(z1, h_res[1] + known)
    coef = jnp.concatenate([z1, rz1, fold1, fold2, -b1], axis=0)

    def second_panel(f_ref, c_ref, x2, w, index):
        @pl.when(index == 2)
        def _():
            f_ref[1, 0:NB, :] = f_ref[1, 0:NB, :] + r1

        c_ref[1] = dot3(jnp.concatenate([w, x2, c_ref[0], f_ref[0], f_ref[1]], axis=1), coef, NN)

        @pl.when(index <= 1)
        def _():
            c_ref[1, 0:NB, :] = zero_tile

    gather_rows_wait(wc.at[1], 39)
    second_panel(panel_c, cor_c, flat(xc.at[2]), flat(wc.at[1]), c)
    keep_right(1, panel_c[1], cor_c[1])
    pltpu.make_async_copy(qh.at[1], qh_out, osem).start()
    pltpu.make_async_copy(ql.at[1], ql_out, osem2).start()
    gather_cols_wait(xr.at[2], 18)
    gather_cols_wait(wr.at[1], 42)
    second_panel(panel_r, cor_r, xr[2], wr[1], r)
    keep_left(1, cor_r[1], panel_r[1])
    last_high = pltpu.make_async_copy(lh.at[1], lh_out, osem3)
    last_low = pltpu.make_async_copy(ll.at[1], ll_out, osem4)
    last_high.start()
    last_low.start()
    pltpu.make_async_copy(abuf, a_out, asem).wait()
    pltpu.make_async_copy(qh.at[1], qh_out, osem).wait()
    pltpu.make_async_copy(ql.at[1], ql_out, osem2).wait()
    last_high.wait()
    last_low.wait()


def update_kernel(tiles, a_ref, lh, ll, qh, ql, o_ref):
    high = lh[...]
    low = ll[...]
    for b in range(0, tiles, 2):
        cols = slice(b * NB, (b + 2) * NB)
        change = mxu(high, qh[:, cols], NN) + (
            mxu(high, ql[:, cols], NN) + mxu(low, qh[:, cols], NN)
        )
        for k in range(high.shape[0] // NB):
            for j in range(2):
                spot = pl.ds(k * NB * tiles + b + j, NB, stride=tiles)
                part = change[k * NB : (k + 1) * NB, j * NB : (j + 1) * NB]
                o_ref[spot, :] = a_ref[spot, :] - part


def local(hamiltonian):
    tiles = hamiltonian.shape[0]
    n = lax.axis_size("row")
    rows = tiles * NB
    ch = rows // n
    pc = NB // n
    half = n // 2
    f32 = jnp.float32
    bf16 = jnp.bfloat16
    block = hamiltonian.reshape(rows * tiles, NB)
    shapes = [
        ((rows * tiles, NB), f32),
        ((rows, rows), bf16),
        ((rows, rows), bf16),
        ((rows, rows), bf16),
        ((rows, rows), bf16),
        ((rows, NB), f32),
        ((rows, NB), f32),
        ((3, rows, NB), f32),
        ((3, half, 2, ch, NB), f32),
        ((rows, NB), f32),
        ((n, ch, NB), f32),
        ((half, 2, ch, NB), f32),
        ((half, ch, NB), f32),
        ((half, ch, NB), f32),
        ((half, ch, NB), f32),
        ((2, ch, NB), f32),
        ((2, rows, NB), f32),
        ((2, half, 2, ch, NB), f32),
        ((2, rows, NB), f32),
        ((2, rows, NB), f32),
        ((2, rows, NB), f32),
        ((2, rows, NB), f32),
        ((2, rows, 2 * NB), bf16),
        ((2, rows, 2 * NB), bf16),
        ((2, 2 * NB, rows), bf16),
        ((2, 2 * NB, rows), bf16),
        ((4, 4, NB, NB), f32),
        ((4, n, 4, pc, NB), f32),
        ((4, 4, NB, NB), f32),
        ((2, NB, NB), f32),
        ((2, n, pc, NB), f32),
        ((2, pc, NB), f32),
        ((2, n, pc, NB), f32),
        ((2, NB, NB), f32),
    ] + [((NB, NB), f32)] * 5
    anywhere = pl.BlockSpec(memory_space=pl.ANY)
    left = jax.ShapeDtypeStruct((rows, 2 * NB), bf16)
    right = jax.ShapeDtypeStruct((2 * NB, rows), bf16)
    parts = pl.pallas_call(
        functools.partial(reduce_kernel, n, tiles),
        out_shape=[jax.ShapeDtypeStruct((rows * tiles, NB), f32), left, left, right, right],
        in_specs=[anywhere],
        out_specs=[anywhere] * 5,
        scratch_shapes=[pltpu.VMEM(*shape) for shape in shapes]
        + [pltpu.SemaphoreType.DMA] * 5
        + [pltpu.SemaphoreType.DMA((43,))] * 2,
        compiler_params=pltpu.CompilerParams(
            collective_id=0, has_side_effects=True, vmem_limit_bytes=VMEM_LIMIT
        ),
        name="reduce_panels",
    )(block)
    step = min(rows, 2 * NB)
    block_spec = pl.BlockSpec((step * tiles, NB), lambda i: (i, 0))
    left_spec = pl.BlockSpec((step, 2 * NB), lambda i: (i, 0))
    right_spec = pl.BlockSpec((2 * NB, rows), lambda i: (0, 0))
    result = pl.pallas_call(
        functools.partial(update_kernel, tiles),
        out_shape=jax.ShapeDtypeStruct((rows * tiles, NB), f32),
        grid=(rows // step,),
        in_specs=[block_spec, left_spec, left_spec, right_spec, right_spec],
        out_specs=block_spec,
        compiler_params=pltpu.CompilerParams(vmem_limit_bytes=VMEM_LIMIT),
        name="update_matrix",
    )(*parts)
    return result.reshape(hamiltonian.shape)


def solution(mesh):
    spec = P(None, "row", None, None, "col", None)
    return jax.shard_map(local, mesh=mesh, in_specs=(spec,), out_specs=spec, check_vma=False)
```

```python
import functools

import jax
import jax.numpy as jnp
from jax import lax
from jax.experimental import pallas as pl
from jax.experimental.pallas import tpu as pltpu
from jax.sharding import PartitionSpec as P

MESH = pl.DeviceIdType.MESH
NB = 128
NN = (((1,), (0,)), ((), ()))
NT = (((1,), (1,)), ((), ()))
TN = (((0,), (0,)), ((), ()))
TT = (((0,), (1,)), ((), ()))
VMEM_LIMIT = 56 << 20
CHOL_WIDTH = 32
INV_WIDTH = 16
CHOL_BLOCKS = NB // CHOL_WIDTH
INV_BLOCKS = NB // INV_WIDTH


def split(value):
    high = value.astype(jnp.bfloat16)
    low = (value - high.astype(jnp.float32)).astype(jnp.bfloat16)
    return high, low


def mxu(first, second, dims):
    return lax.dot_general(first, second, dims, preferred_element_type=jnp.float32)


def dot3(first, second, dims):
    fh, fl = split(first)
    sh, sl = split(second)
    return mxu(fh, sh, dims) + (mxu(fh, sl, dims) + mxu(fl, sh, dims))


def exact(first, second, dims=NN):
    return lax.dot_general(
        first, second, dims, precision=lax.Precision.HIGHEST, preferred_element_type=jnp.float32
    )


def iota(axis, shape):
    return lax.broadcasted_iota(jnp.int32, shape, axis)


def leading_columns(x, base, width):
    rolled = pltpu.roll(x, lax.rem(NB - base, NB), 1)
    return [jnp.broadcast_to(rolled[:, i : i + 1], (width, NB)) for i in range(width)]


def cholesky_blocks(g_ref, r_ref, first, last):
    width = CHOL_WIDTH
    sub = iota(0, (width, NB))
    lane = iota(1, (width, NB))

    def block(k, carry):
        base = pl.multiple_of(k * width, width)
        x = g_ref[pl.ds(base, width), :]
        cols = leading_columns(x, base, width)
        for i in range(width):
            scale = lax.rsqrt(cols[i][i : i + 1, :])
            column = cols[i] * scale
            below = jnp.where(sub > i, column, 0.0)
            row = x[i : i + 1, :] * scale
            x = jnp.where(sub == i, row, x - below * row)
            for m in range(i + 1, width):
                cols[m] = cols[m] - below * column[m : m + 1, :]
        x = jnp.where(lane >= base + sub, x, 0.0)
        r_ref[pl.ds(base, width), :] = x
        g_ref[...] -= exact(x, x, TN)
        return carry

    lax.fori_loop(first, last, block, 0)


def inverse_blocks(y_ref, t_ref, first, last):
    width = INV_WIDTH
    sub = iota(0, (width, NB))
    lane = iota(1, (width, NB))
    wide = iota(1, (NB, NB))

    def block(k, carry):
        base = pl.multiple_of(k * width, width)
        x = y_ref[pl.ds(base, width), :]
        cols = leading_columns(x, base, width)
        inside = (lane >= base) & (lane < base + width)
        x = jnp.where(inside, jnp.where(lane - base == sub, 1.0, 0.0), x)
        for i in range(width):
            scale = 1.0 / cols[i][i : i + 1, :]
            factor = jnp.where(sub == i, 0.0, cols[i])
            row = x[i : i + 1, :] * scale
            x = jnp.where(sub == i, row, x - factor * row)
            for m in range(i + 1, width):
                entry = cols[m][i : i + 1, :] * scale
                cols[m] = jnp.where(sub == i, entry, cols[m] - factor * entry)
        t_ref[pl.ds(base, width), :] = x
        y = y_ref[...]
        chosen = (wide >= base) & (wide < base + width)
        y_ref[...] = jnp.where(chosen, 0.0, y) - exact(jnp.where(chosen, y, 0.0), t_ref[...])
        y_ref[pl.ds(base, width), :] = x
        t_ref[pl.ds(base, width), :] = jnp.zeros((width, NB), jnp.float32)
        return carry

    lax.fori_loop(first, last, block, 0)


def reduce_kernel(n, tiles, *refs):
    rows = tiles * NB
    ch = rows // n
    pc = NB // n
    half = n // 2
    per_tile = NB // ch
    (
        a_hbm, a_out, lh_out, ll_out, qh_out, ql_out,
        abuf, ahi, alo, thi, tlo, stg_r, stg_c, xr, xc,
        wpart_r, wslot_r, wpart_c, wsib, wsum, wslot_c, wch, wr, wc,
        panel_r, panel_c, cor_r, cor_c, lh, ll, qh, ql,
        ar_src, ar_slot, ar_res, h_src, h_slot, h_piece, h_ex, h_res,
        g_ref, y_ref, t_ref, r0_ref, r1_ref, asem, osem, osem2, osem3, osem4, ss, rs,
    ) = refs
    r = lax.axis_index("row")
    c = lax.axis_index("col")
    parity = lax.rem(r, 2)
    level = r // 2
    sibling = (r + 1 - 2 * parity, c)

    load = pltpu.make_async_copy(a_hbm, abuf, asem)
    load.start()
    barrier = pltpu.get_barrier_semaphore()

    def greet(k, carry):
        pl.semaphore_signal(barrier, inc=1, device_id=(lax.rem(r + k, n), c), device_id_type=MESH)
        pl.semaphore_signal(barrier, inc=1, device_id=(r, lax.rem(c + k, n)), device_id_type=MESH)
        return carry

    lax.fori_loop(1, n, greet, 0)

    @pl.when(r != c)
    def _():
        pl.semaphore_signal(barrier, inc=1, device_id=(c, r), device_id_type=MESH)

    def send(src, dst, sem, device):
        pltpu.make_async_remote_copy(
            src, dst, ss.at[sem], rs.at[sem], device_id=device, device_id_type=MESH
        ).start()

    def over_cols(sem, src_of, dst_of):
        def one(k, carry):
            j = lax.rem(c + k, n)
            send(src_of(j), dst_of(j), sem, (r, j))
            return carry

        lax.fori_loop(1, n, one, 0)

    def over_rows(sem, src_of, dst_of):
        def one(k, carry):
            j = lax.rem(r + k, n)
            send(src_of(j), dst_of(j), sem, (j, c))
            return carry

        lax.fori_loop(1, n, one, 0)

    def wait_sent(sem, sent):
        pltpu.make_async_copy(sent, sent, ss.at[sem]).wait()

    def wait_received(sem, received):
        pltpu.make_async_copy(received, received, rs.at[sem]).wait()

    def wait(sem, part):
        wait_received(sem, part)
        wait_sent(sem, part)

    def scatter(t):
        @pl.when(c == t)
        def _():
            over_cols(
                t,
                lambda j: stg_r.at[pl.ds(j * ch, ch)],
                lambda j: xr.at[t, pl.ds(j * ch, ch)],
            )
            xr[t, pl.ds(t * ch, ch), :] = stg_r[pl.ds(t * ch, ch), :]

        @pl.when(r == t)
        def _():
            over_rows(
                3 + t,
                lambda j: stg_c.at[pl.ds(j * ch, ch)],
                lambda j: xc.at[t, j // 2, lax.rem(j, 2)],
            )
            xc[t, t // 2, t % 2] = stg_c[pl.ds(t * ch, ch), :]

    def scatter_wait(t):
        @pl.when(c == t)
        def _():
            wait_sent(t, stg_r.at[pl.ds(0, (n - 1) * ch)])

        @pl.when(c != t)
        def _():
            wait_received(t, xr.at[t, pl.ds(c * ch, ch)])

        @pl.when(r == t)
        def _():
            wait_sent(3 + t, stg_c.at[pl.ds(0, (n - 1) * ch)])

        @pl.when(r != t)
        def _():
            wait_received(3 + t, xc.at[t, level, parity])

    def gather_cols_start(buf, sem):
        mine = buf.at[pl.ds(c * ch, ch)]
        over_cols(sem, lambda j: mine, lambda j: mine)

    def gather_cols_wait(buf, sem):
        wait(sem, buf.at[pl.ds(0, (n - 1) * ch)])

    def gather_rows_start(buf, sem):
        mine = buf.at[level, parity]

        def one(k, carry):
            send(mine, mine, sem, (lax.rem(level + k, half) * 2 + parity, c))
            return carry

        lax.fori_loop(1, half, one, 0)

    def gather_rows_mid(buf, sem):
        wait(sem, buf.at[pl.ds(0, half - 1), 0])
        mine = buf.at[:, parity]
        send(mine, mine, sem + 1, sibling)

    def gather_rows_wait(buf, sem):
        wait(sem + 1, buf.at[:, 0])

    def sum_start(q, parts, sem, over, me):
        count = len(parts)
        for i, part in enumerate(parts):
            ar_src[q, i] = part
        over(
            sem,
            lambda j: ar_src.at[q, pl.ds(0, count), pl.ds(j * pc, pc)],
            lambda j: ar_slot.at[q, me, pl.ds(0, count)],
        )
        ar_slot[q, me, 0:count] = ar_src[q, 0:count, pl.ds(me * pc, pc), :]

    def sum_slots(q, count, sem):
        wait(sem, ar_slot.at[q, pl.ds(0, n - 1), pl.ds(0, count)])
        total = ar_slot[q, 0, 0:count]
        for j in range(1, n):
            total = total + ar_slot[q, j, 0:count]
        return total

    def sum_spread(q, count, sem, over, me):
        mine = (q, pl.ds(0, count), pl.ds(me * pc, pc))
        over(sem + 1, lambda j: ar_res.at[mine], lambda j: ar_res.at[mine])

    def sum_mid(q, count, sem, over, me):
        ar_res[q, 0:count, pl.ds(me * pc, pc), :] = sum_slots(q, count, sem)
        sum_spread(q, count, sem, over, me)

    def sum_wait(q, count, sem):
        wait(sem + 1, ar_res.at[q, pl.ds(0, count), pl.ds(0, (n - 1) * pc)])

    def all_start(p, part, sem, over, me):
        h_src[p] = part
        over(sem, lambda j: h_src.at[p, pl.ds(j * pc, pc)], lambda j: h_slot.at[p, me])
        h_slot[p, me] = h_src[p, pl.ds(me * pc, pc), :]

    def all_mid(p, sem, over, me):
        wait(sem, h_slot.at[p, pl.ds(0, n - 1)])
        total = h_slot[p, 0]
        for j in range(1, n):
            total = total + h_slot[p, j]
        h_piece[p] = total
        over(sem + 1, lambda j: h_piece.at[p], lambda j: h_ex.at[p, me])
        h_ex[p, me] = total

    def all_late(p, sem, over, me):
        wait(sem + 1, h_ex.at[p, pl.ds(0, n - 1)])
        total = h_ex[p, 0]
        for j in range(1, n):
            total = total + h_ex[p, j]
        h_res[p, pl.ds(me * pc, pc), :] = total
        mine = h_res.at[p, pl.ds(me * pc, pc)]
        over(sem + 2, lambda j: mine, lambda j: mine)

    def all_wait(p, sem):
        wait(sem + 2, h_res.at[p, pl.ds(0, (n - 1) * pc)])

    def tile_product(high_ref, low_ref, at, both):
        wide = mxu(high_ref[pl.ds(at, NB), :], both, NN)
        return wide[:, :NB] + (wide[:, NB:] + mxu(low_ref[pl.ds(at, NB), :], both[:, :NB], NN))

    def halves(panel):
        return jnp.concatenate(split(panel), axis=1)

    def flat(ref):
        return ref[...].reshape(rows, NB)

    def flip(value):
        return jnp.concatenate(
            [value[i * NB : (i + 1) * NB].T for i in range(tiles)], axis=1
        )

    def known_part(r_mat, k, corner):
        kr = exact(k, r_mat)
        return kr + kr.T + exact(exact(r_mat, corner, TN), r_mat)

    def core(z, inner_sum):
        return 0.5 * exact(exact(z, inner_sum, TN), z)

    zero_tile = jnp.zeros((NB, NB), jnp.float32)
    block_rows = min(rows, 2 * NB)

    def keep_left(p, first, second):
        for i, value in enumerate((first, second)):
            spot = slice(i * NB, (i + 1) * NB)
            lh[p, :, spot], ll[p, :, spot] = split(value)

    def keep_right(p, first, second):
        for i, value in enumerate((first, second)):
            spot = slice(i * NB, (i + 1) * NB)
            qh[p, spot, :], ql[p, spot, :] = split(flip(value))

    def apply_first():
        def one(i, carry):
            at = pl.multiple_of(i * block_rows, block_rows)
            high = lh[0, pl.ds(at, block_rows)]
            low = ll[0, pl.ds(at, block_rows)]
            for b in range(0, tiles, 2):
                cols = slice(b * NB, (b + 2) * NB)
                change = mxu(high, qh[0, :, cols], NN) + (
                    mxu(high, ql[0, :, cols], NN) + mxu(low, qh[0, :, cols], NN)
                )
                for k in range(block_rows // NB):
                    for j in range(2):
                        spot = pl.ds((at + k * NB) * tiles + b + j, NB, stride=tiles)
                        part = change[k * NB : (k + 1) * NB, j * NB : (j + 1) * NB]
                        abuf[spot, :] = abuf[spot, :] - part
            return carry

        lax.fori_loop(0, rows // block_rows, one, 0)

    def write_band(p, r_ref):
        @pl.when(c == p)
        def _():
            for a in range(tiles):
                spot = pl.ds(a * NB * tiles, NB, stride=tiles)

                @pl.when(a * n + r == p + 1)
                def _():
                    abuf[spot, :] = -r_ref[...]

                @pl.when(a * n + r > p + 1)
                def _():
                    abuf[spot, :] = zero_tile

        @pl.when(r == p)
        def _():
            for b in range(tiles):
                spot = pl.ds(b, NB, stride=tiles)

                @pl.when(b * n + c == p + 1)
                def _():
                    abuf[spot, :] = -r_ref[...].T

                @pl.when(b * n + c > p + 1)
                def _():
                    abuf[spot, :] = zero_tile

    load.wait()
    for t in range(3):

        @pl.when(c == t)
        def _():
            for a in range(tiles):
                stg_r[a * NB : (a + 1) * NB, :] = abuf[pl.ds(a * NB * tiles, NB, stride=tiles), :]

            @pl.when(r == 0)
            def _():
                stg_r[0:NB, :] = zero_tile

        @pl.when(r == t)
        def _():
            for b in range(tiles):
                stg_c[b * NB : (b + 1) * NB, :] = abuf[pl.ds(b, NB, stride=tiles), :].T

            @pl.when(c == 0)
            def _():
                stg_c[0:NB, :] = zero_tile

    pl.semaphore_wait(barrier, 2 * (n - 1) + jnp.where(r != c, 1, 0))
    scatter(0)

    def tile_start(sem, index, t, owner):
        @pl.when((r == t) & (c == owner))
        def _():
            over_cols(
                sem,
                lambda j: stg_c.at[pl.ds(j * pc, pc)],
                lambda j: ar_res.at[0, index, pl.ds(j * pc, pc)],
            )
            ar_res[0, index, pl.ds(c * pc, pc), :] = stg_c[pl.ds(c * pc, pc), :]

    def tile_wait(sem, index, t, owner):
        @pl.when((r == t) & (c == owner))
        def _():
            wait_sent(sem, stg_c.at[pl.ds(0, (n - 1) * pc)])

        @pl.when((r == t) & (c != owner))
        def _():
            wait_received(sem, ar_res.at[0, index, pl.ds(c * pc, pc)])

    def row_start(sem, t, first, count):
        mine = (0, pl.ds(first, count), pl.ds(c * pc, pc))

        @pl.when(r == t)
        def _():
            over_rows(sem, lambda j: ar_res.at[mine], lambda j: ar_res.at[mine])

    def row_wait(sem, t, first, count):
        @pl.when(r == t)
        def _():
            wait_sent(sem, ar_res.at[0, pl.ds(first, count), pl.ds(0, (n - 1) * pc)])

        @pl.when(r != t)
        def _():
            wait_received(sem, ar_res.at[0, pl.ds(first, count), pl.ds(c * pc, pc)])

    @pl.when(r == 0)
    def _():
        mine = stg_c[...]
        first = jnp.where(c == 1, mine[0:NB], 0.0)
        second = jnp.where(c == 2, mine[0:NB], 0.0)
        sum_start(0, [dot3(mine, mine, TN), first, second], 9, over_cols, c)

    t_ref[...] = zero_tile

    @pl.when(r == 0)
    def _():
        ar_res[0, 0:3, pl.ds(c * pc, pc), :] = sum_slots(0, 3, 9)

    row_start(19, 0, 0, 3)
    scatter_wait(0)
    gather_rows_start(xc.at[0], 6)
    gather_cols_start(xr.at[0], 8)
    scatter(1)
    tile_start(43, 3, 1, 1)
    tile_start(44, 4, 1, 2)
    scatter(2)
    tile_start(45, 5, 2, 2)

    def to_parts(a, carry):
        at = pl.multiple_of(a * NB, NB)
        for b in range(tiles):
            high, low = split(abuf[pl.ds(a * NB * tiles + b, NB, stride=tiles), :])
            ahi[pl.ds(at, NB), b * NB : (b + 1) * NB] = high
            alo[pl.ds(at, NB), b * NB : (b + 1) * NB] = low
        return carry

    lax.fori_loop(0, tiles, to_parts, 0)

    def to_flipped(b, carry):
        at = pl.multiple_of(b * NB, NB)
        for a in range(tiles):
            high, low = split(abuf[pl.ds(a * NB * tiles + b, NB, stride=tiles), :].T)
            thi[pl.ds(at, NB), a * NB : (a + 1) * NB] = high
            tlo[pl.ds(at, NB), a * NB : (a + 1) * NB] = low
        return carry

    lax.fori_loop(0, tiles // 2, to_flipped, 0)

    row_wait(19, 0, 0, 3)
    sum_spread(0, 3, 9, over_cols, c)
    tile_wait(43, 3, 1, 1)
    tile_wait(44, 4, 1, 2)
    tile_wait(45, 5, 2, 2)
    row_start(46, 1, 3, 2)
    row_start(47, 2, 5, 1)
    scatter_wait(1)
    gather_cols_start(xr.at[1], 13)
    scatter_wait(2)
    gather_rows_mid(xc.at[0], 6)
    gather_rows_wait(xc.at[0], 6)

    both = halves(flat(xc.at[0]))

    def first_product(a, carry):
        at = pl.multiple_of(a * NB, NB)
        wpart_r[pl.ds(at, NB), :] = tile_product(ahi, alo, at, both)
        for i in range(per_tile):
            j = a * per_tile + i
            mine = wpart_r.at[pl.ds(j * ch, ch)]

            @pl.when(j != c)
            def _():
                send(mine, wslot_r.at[c], 20, (r, j))

        return carry

    lax.fori_loop(0, tiles, first_product, 0)
    wslot_r[c] = wpart_r[pl.ds(c * ch, ch), :]
    gather_cols_wait(xr.at[0], 8)
    all_start(0, dot3(xr[0], wpart_r[...], TN), 26, over_rows, r)
    gather_rows_start(xc.at[1], 11)
    gather_cols_start(xr.at[2], 18)
    sum_wait(0, 3, 9)
    g_ref[...] = ar_res[0, 0]
    cholesky_blocks(g_ref, r0_ref, 0, CHOL_BLOCKS)
    all_mid(0, 26, over_cols, c)
    gather_cols_wait(xr.at[1], 13)
    sum_start(1, [dot3(xr[0], xr[1], TN)], 14, over_rows, r)
    gather_rows_start(xc.at[2], 16)
    y_ref[...] = ar_res[0, 0] + exact(ar_res[0, 1], r0_ref[...], TN)
    inverse_blocks(y_ref, t_ref, 0, INV_BLOCKS // 2)

    wait(20, wslot_r.at[pl.ds(0, n - 1)])
    total = wslot_r[0]
    for j in range(1, n):
        total = total + wslot_r[j]
    wr[0, pl.ds(c * ch, ch), :] = total
    wch[0] = total

    @pl.when(r != c)
    def _():
        send(wch.at[0], wc.at[0, c // 2, lax.rem(c, 2)], 22, (c, r))

    @pl.when(r == c)
    def _():
        wc[0, level, parity] = total

    gather_cols_start(wr.at[0], 23)
    all_late(0, 26, over_rows, r)
    sum_mid(1, 1, 14, over_rows, r)
    row_wait(46, 1, 3, 2)
    row_wait(47, 2, 5, 1)
    tiles_mine = (0, pl.ds(3, 3), pl.ds(c * pc, pc))
    over_cols(48, lambda j: ar_res.at[tiles_mine], lambda j: ar_res.at[tiles_mine])
    inverse_blocks(y_ref, t_ref, INV_BLOCKS // 2, INV_BLOCKS)
    lax.fori_loop(tiles // 2, tiles, to_flipped, 0)
    gather_rows_mid(xc.at[1], 11)

    @pl.when(r != c)
    def _():
        wait_received(22, wc.at[0, level, parity])
        wait_sent(22, wch.at[0])

    gather_rows_start(wc.at[0], 24)
    wait(48, ar_res.at[0, pl.ds(3, 3), pl.ds(0, (n - 1) * pc)])
    sum_wait(1, 1, 14)
    r0 = r0_ref[...]
    z0 = y_ref[...]
    k0 = ar_res[1, 0]
    rz0 = exact(r0, z0)
    f01 = ar_res[0, 1] + r0
    f02 = ar_res[0, 2]
    x11 = ar_res[0, 3]
    x12 = ar_res[0, 4]
    x22 = ar_res[0, 5]
    known = known_part(r0, k0, x11)
    c01 = exact(k0, z0, TN) + exact(x11, rz0)
    all_wait(0, 26)
    b0 = core(z0, h_res[0] + known)
    c01 = c01 - exact(f01, b0)
    coef = jnp.concatenate([z0, rz0, -b0], axis=0)
    carried = exact(coef, f01, NT)
    last = carried[2 * NB :] + c01.T
    coef = jnp.concatenate(
        [coef, jnp.concatenate([carried[: 2 * NB], last], axis=0)], axis=1
    )

    def first_panel(f_ref, c_ref, x0, x1, w, index):
        f_ref[0] = x0

        @pl.when(index == 1)
        def _():
            f_ref[0, 0:NB, :] = f_ref[0, 0:NB, :] + r0

        out = dot3(jnp.concatenate([w, x1, f_ref[0]], axis=1), coef, NN)
        c_ref[0] = out[:, :NB]
        f_ref[1] = x1 - out[:, NB:]

        @pl.when(index == 0)
        def _():
            c_ref[0, 0:NB, :] = zero_tile

        @pl.when(index <= 1)
        def _():
            f_ref[1, 0:NB, :] = zero_tile

    gather_cols_wait(wr.at[0], 23)
    first_panel(panel_r, cor_r, xr[0], xr[1], wr[0], r)

    p1r = panel_r[1]
    sum_start(2, [dot3(p1r, p1r, TN)], 30, over_rows, r)
    both = halves(p1r)

    def second_product(b, carry):
        at = pl.multiple_of(b * NB, NB)
        value = tile_product(thi, tlo, at, both).reshape(per_tile, ch, NB)
        for i in range(per_tile):
            j = b * per_tile + i
            wpart_c[j // 2, lax.rem(j, 2)] = value[i]
        return carry

    lax.fori_loop(0, tiles, second_product, 0)
    send(wpart_c.at[:, 1 - parity], wsib, 34, sibling)
    gather_cols_wait(xr.at[2], 18)
    sum_mid(2, 1, 30, over_rows, r)
    wait(34, wsib)
    wsum[...] = wpart_c[:, parity] + wsib[...]

    def spread(k, carry):
        to = lax.rem(level + k, half)
        send(wsum.at[to], wslot_c.at[level], 35, (to * 2 + parity, c))
        return carry

    lax.fori_loop(1, half, spread, 0)
    wslot_c[level] = wsum[level]
    gather_rows_mid(xc.at[2], 16)
    gather_rows_mid(wc.at[0], 24)
    gather_rows_wait(xc.at[1], 11)
    gather_rows_wait(xc.at[2], 16)
    gather_rows_wait(wc.at[0], 24)
    first_panel(panel_c, cor_c, flat(xc.at[0]), flat(xc.at[1]), flat(wc.at[0]), c)
    p1c = panel_c[1]
    all_start(1, dot3(p1c, flat(wpart_c), TN), 36, over_cols, c)
    x2c = flat(xc.at[2])
    inner = dot3(p1c, jnp.concatenate([x2c, panel_c[0], cor_c[0]], axis=1), TN)
    sum_start(3, [inner[:, 0:NB], inner[:, NB : 2 * NB], inner[:, 2 * NB :]], 32, over_cols, c)
    sum_start(4, [dot3(xr[2], xr[0], TN)], 49, over_rows, r)
    keep_left(0, cor_r[0], panel_r[0])
    keep_right(0, panel_c[0], cor_c[0])
    sum_wait(2, 1, 30)
    g_ref[...] = ar_res[2, 0]
    cholesky_blocks(g_ref, r1_ref, 0, CHOL_BLOCKS // 2)
    all_mid(1, 36, over_rows, r)
    sum_mid(4, 1, 49, over_rows, r)

    wait(35, wslot_c.at[pl.ds(0, half - 1)])
    total = wslot_c[0]
    for j in range(1, half):
        total = total + wslot_c[j]
    wch[1] = total

    @pl.when(r != c)
    def _():
        send(wch.at[1], wr.at[1, pl.ds(r * ch, ch)], 41, (c, r))

    @pl.when(r == c)
    def _():
        wr[1, pl.ds(c * ch, ch), :] = total

    wc[1, level, parity] = total
    gather_rows_start(wc.at[1], 39)
    cholesky_blocks(g_ref, r1_ref, CHOL_BLOCKS // 2, CHOL_BLOCKS)
    sum_mid(3, 3, 32, over_cols, c)
    all_late(1, 36, over_cols, c)
    sum_wait(4, 1, 49)
    c02 = exact(ar_res[4, 0], z0) + exact(x12, rz0) - exact(f02, b0)
    top = x12 - exact(c02, f01, NT) - exact(f02, c01, NT)
    y_ref[...] = ar_res[2, 0] + exact(top, r1_ref[...], TN)
    inverse_blocks(y_ref, t_ref, 0, INV_BLOCKS // 2)

    @pl.when(r != c)
    def _():
        wait_received(41, wr.at[1, pl.ds(c * ch, ch)])
        wait_sent(41, wch.at[1])

    gather_cols_start(wr.at[1], 42)
    inverse_blocks(y_ref, t_ref, INV_BLOCKS // 2, INV_BLOCKS)
    gather_rows_mid(wc.at[1], 39)
    r1 = r1_ref[...]
    z1 = y_ref[...]
    rz1 = exact(r1, z1)
    sum_wait(3, 3, 32)
    j1t = ar_res[3, 1]
    j2t = ar_res[3, 2]
    cross = exact(j2t, j1t, NT)
    cf = exact(c02, f02, NT)
    k1 = ar_res[3, 0] - exact(j2t, f02, NT) - exact(j1t, c02, NT)
    known = known_part(r1, k1, x22 - cf - cf.T) - cross - cross.T
    fold1 = -exact(j1t, z1, TN) - exact(f02, rz1, TN)
    fold2 = -exact(j2t, z1, TN) - exact(c02, rz1, TN)
    apply_first()
    write_band(0, r0_ref)
    write_band(1, r1_ref)
    pltpu.make_async_copy(abuf, a_out, asem).start()
    all_wait(1, 36)
    b1 = core(z1, h_res[1] + known)
    coef = jnp.concatenate([z1, rz1, fold1, fold2, -b1], axis=0)

    def second_panel(f_ref, c_ref, x2, w, index):
        @pl.when(index == 2)
        def _():
            f_ref[1, 0:NB, :] = f_ref[1, 0:NB, :] + r1

        c_ref[1] = dot3(jnp.concatenate([w, x2, c_ref[0], f_ref[0], f_ref[1]], axis=1), coef, NN)

        @pl.when(index <= 1)
        def _():
            c_ref[1, 0:NB, :] = zero_tile

    gather_rows_wait(wc.at[1], 39)
    second_panel(panel_c, cor_c, flat(xc.at[2]), flat(wc.at[1]), c)
    keep_right(1, panel_c[1], cor_c[1])
    pltpu.make_async_copy(qh.at[1], qh_out, osem).start()
    pltpu.make_async_copy(ql.at[1], ql_out, osem2).start()
    gather_cols_wait(wr.at[1], 42)
    second_panel(panel_r, cor_r, xr[2], wr[1], r)
    keep_left(1, cor_r[1], panel_r[1])
    last_high = pltpu.make_async_copy(lh.at[1], lh_out, osem3)
    last_low = pltpu.make_async_copy(ll.at[1], ll_out, osem4)
    last_high.start()
    last_low.start()
    pltpu.make_async_copy(abuf, a_out, asem).wait()
    pltpu.make_async_copy(qh.at[1], qh_out, osem).wait()
    pltpu.make_async_copy(ql.at[1], ql_out, osem2).wait()
    last_high.wait()
    last_low.wait()


def update_kernel(tiles, a_ref, lh, ll, qh, ql, o_ref):
    high = lh[...]
    low = ll[...]
    for b in range(0, tiles, 2):
        cols = slice(b * NB, (b + 2) * NB)
        change = mxu(high, qh[:, cols], NN) + (
            mxu(high, ql[:, cols], NN) + mxu(low, qh[:, cols], NN)
        )
        for k in range(high.shape[0] // NB):
            for j in range(2):
                spot = pl.ds(k * NB * tiles + b + j, NB, stride=tiles)
                part = change[k * NB : (k + 1) * NB, j * NB : (j + 1) * NB]
                o_ref[spot, :] = a_ref[spot, :] - part


def local(hamiltonian):
    tiles = hamiltonian.shape[0]
    n = lax.axis_size("row")
    rows = tiles * NB
    ch = rows // n
    pc = NB // n
    half = n // 2
    f32 = jnp.float32
    bf16 = jnp.bfloat16
    block = hamiltonian.reshape(rows * tiles, NB)
    shapes = [
        ((rows * tiles, NB), f32),
        ((rows, rows), bf16),
        ((rows, rows), bf16),
        ((rows, rows), bf16),
        ((rows, rows), bf16),
        ((rows, NB), f32),
        ((rows, NB), f32),
        ((3, rows, NB), f32),
        ((3, half, 2, ch, NB), f32),
        ((rows, NB), f32),
        ((n, ch, NB), f32),
        ((half, 2, ch, NB), f32),
        ((half, ch, NB), f32),
        ((half, ch, NB), f32),
        ((half, ch, NB), f32),
        ((2, ch, NB), f32),
        ((2, rows, NB), f32),
        ((2, half, 2, ch, NB), f32),
        ((2, rows, NB), f32),
        ((2, rows, NB), f32),
        ((2, rows, NB), f32),
        ((2, rows, NB), f32),
        ((2, rows, 2 * NB), bf16),
        ((2, rows, 2 * NB), bf16),
        ((2, 2 * NB, rows), bf16),
        ((2, 2 * NB, rows), bf16),
        ((5, 3, NB, NB), f32),
        ((5, n, 3, pc, NB), f32),
        ((5, 6, NB, NB), f32),
        ((2, NB, NB), f32),
        ((2, n, pc, NB), f32),
        ((2, pc, NB), f32),
        ((2, n, pc, NB), f32),
        ((2, NB, NB), f32),
    ] + [((NB, NB), f32)] * 5
    anywhere = pl.BlockSpec(memory_space=pl.ANY)
    left = jax.ShapeDtypeStruct((rows, 2 * NB), bf16)
    right = jax.ShapeDtypeStruct((2 * NB, rows), bf16)
    parts = pl.pallas_call(
        functools.partial(reduce_kernel, n, tiles),
        out_shape=[jax.ShapeDtypeStruct((rows * tiles, NB), f32), left, left, right, right],
        in_specs=[anywhere],
        out_specs=[anywhere] * 5,
        scratch_shapes=[pltpu.VMEM(*shape) for shape in shapes]
        + [pltpu.SemaphoreType.DMA] * 5
        + [pltpu.SemaphoreType.DMA((51,))] * 2,
        compiler_params=pltpu.CompilerParams(
            collective_id=0, has_side_effects=True, vmem_limit_bytes=VMEM_LIMIT
        ),
        name="reduce_panels",
    )(block)
    step = min(rows, 2 * NB)
    block_spec = pl.BlockSpec((step * tiles, NB), lambda i: (i, 0))
    left_spec = pl.BlockSpec((step, 2 * NB), lambda i: (i, 0))
    right_spec = pl.BlockSpec((2 * NB, rows), lambda i: (0, 0))
    result = pl.pallas_call(
        functools.partial(update_kernel, tiles),
        out_shape=jax.ShapeDtypeStruct((rows * tiles, NB), f32),
        grid=(rows // step,),
        in_specs=[block_spec, left_spec, left_spec, right_spec, right_spec],
        out_specs=block_spec,
        compiler_params=pltpu.CompilerParams(vmem_limit_bytes=VMEM_LIMIT),
        name="update_matrix",
    )(*parts)
    return result.reshape(hamiltonian.shape)


def solution(mesh):
    spec = P(None, "row", None, None, "col", None)
    return jax.shard_map(local, mesh=mesh, in_specs=(spec,), out_specs=spec, check_vma=False)
```

```python
import functools

import jax
import jax.numpy as jnp
from jax import lax
from jax.experimental import pallas as pl
from jax.experimental.pallas import tpu as pltpu
from jax.sharding import PartitionSpec as P

MESH = pl.DeviceIdType.MESH
NB = 128
NN = (((1,), (0,)), ((), ()))
NT = (((1,), (1,)), ((), ()))
TN = (((0,), (0,)), ((), ()))
TT = (((0,), (1,)), ((), ()))
VMEM_LIMIT = 56 << 20
CHOL_WIDTH = 32
INV_WIDTH = 16
CHOL_BLOCKS = NB // CHOL_WIDTH
INV_BLOCKS = NB // INV_WIDTH


def split(value):
    high = value.astype(jnp.bfloat16)
    low = (value - high.astype(jnp.float32)).astype(jnp.bfloat16)
    return high, low


def mxu(first, second, dims):
    return lax.dot_general(first, second, dims, preferred_element_type=jnp.float32)


def dot3(first, second, dims):
    fh, fl = split(first)
    sh, sl = split(second)
    return mxu(fh, sh, dims) + (mxu(fh, sl, dims) + mxu(fl, sh, dims))


def exact(first, second, dims=NN):
    return lax.dot_general(
        first, second, dims, precision=lax.Precision.HIGHEST, preferred_element_type=jnp.float32
    )


def iota(axis, shape):
    return lax.broadcasted_iota(jnp.int32, shape, axis)


def leading_columns(x, base, width):
    rolled = pltpu.roll(x, lax.rem(NB - base, NB), 1)
    return [jnp.broadcast_to(rolled[:, i : i + 1], (width, NB)) for i in range(width)]


def cholesky_blocks(g_ref, r_ref, first, last):
    width = CHOL_WIDTH
    sub = iota(0, (width, NB))
    lane = iota(1, (width, NB))

    def block(k, carry):
        base = pl.multiple_of(k * width, width)
        x = g_ref[pl.ds(base, width), :]
        cols = leading_columns(x, base, width)
        for i in range(width):
            scale = lax.rsqrt(cols[i][i : i + 1, :])
            column = cols[i] * scale
            below = jnp.where(sub > i, column, 0.0)
            row = x[i : i + 1, :] * scale
            x = jnp.where(sub == i, row, x - below * row)
            for m in range(i + 1, width):
                cols[m] = cols[m] - below * column[m : m + 1, :]
        x = jnp.where(lane >= base + sub, x, 0.0)
        r_ref[pl.ds(base, width), :] = x
        g_ref[...] -= exact(x, x, TN)
        return carry

    lax.fori_loop(first, last, block, 0)


def inverse_blocks(y_ref, t_ref, first, last):
    width = INV_WIDTH
    sub = iota(0, (width, NB))
    lane = iota(1, (width, NB))
    wide = iota(1, (NB, NB))

    def block(k, carry):
        base = pl.multiple_of(k * width, width)
        x = y_ref[pl.ds(base, width), :]
        cols = leading_columns(x, base, width)
        inside = (lane >= base) & (lane < base + width)
        x = jnp.where(inside, jnp.where(lane - base == sub, 1.0, 0.0), x)
        for i in range(width):
            scale = 1.0 / cols[i][i : i + 1, :]
            factor = jnp.where(sub == i, 0.0, cols[i])
            row = x[i : i + 1, :] * scale
            x = jnp.where(sub == i, row, x - factor * row)
            for m in range(i + 1, width):
                entry = cols[m][i : i + 1, :] * scale
                cols[m] = jnp.where(sub == i, entry, cols[m] - factor * entry)
        t_ref[pl.ds(base, width), :] = x
        y = y_ref[...]
        chosen = (wide >= base) & (wide < base + width)
        y_ref[...] = jnp.where(chosen, 0.0, y) - exact(jnp.where(chosen, y, 0.0), t_ref[...])
        y_ref[pl.ds(base, width), :] = x
        t_ref[pl.ds(base, width), :] = jnp.zeros((width, NB), jnp.float32)
        return carry

    lax.fori_loop(first, last, block, 0)


def reduce_kernel(n, tiles, *refs):
    rows = tiles * NB
    ch = rows // n
    pc = NB // n
    half = n // 2
    per_tile = NB // ch
    (
        a_hbm, a_out, lh_out, ll_out, qh_out, ql_out,
        abuf, ahi, alo, thi, tlo, stg_r, stg_c, xr, xc,
        wpart_r, wslot_r, wpart_c, wsib, wsum, wslot_c, wch, wr, wc,
        panel_r, panel_c, cor_r, cor_c, lh, ll, qh, ql,
        ar_src, ar_slot, ar_res, h_src, h_slot, h_piece, h_ex, h_res,
        g_ref, y_ref, t_ref, r0_ref, r1_ref, asem, osem, osem2, osem3, osem4, ss, rs,
    ) = refs
    r = lax.axis_index("row")
    c = lax.axis_index("col")
    parity = lax.rem(r, 2)
    level = r // 2
    sibling = (r + 1 - 2 * parity, c)

    load = pltpu.make_async_copy(a_hbm, abuf, asem)
    load.start()
    barrier = pltpu.get_barrier_semaphore()

    def greet(k, carry):
        pl.semaphore_signal(barrier, inc=1, device_id=(lax.rem(r + k, n), c), device_id_type=MESH)
        pl.semaphore_signal(barrier, inc=1, device_id=(r, lax.rem(c + k, n)), device_id_type=MESH)
        return carry

    lax.fori_loop(1, n, greet, 0)

    @pl.when(r != c)
    def _():
        pl.semaphore_signal(barrier, inc=1, device_id=(c, r), device_id_type=MESH)

    def send(src, dst, sem, device):
        pltpu.make_async_remote_copy(
            src, dst, ss.at[sem], rs.at[sem], device_id=device, device_id_type=MESH
        ).start()

    def over_cols(sem, src_of, dst_of):
        def one(k, carry):
            j = lax.rem(c + k, n)
            send(src_of(j), dst_of(j), sem, (r, j))
            return carry

        lax.fori_loop(1, n, one, 0)

    def over_rows(sem, src_of, dst_of):
        def one(k, carry):
            j = lax.rem(r + k, n)
            send(src_of(j), dst_of(j), sem, (j, c))
            return carry

        lax.fori_loop(1, n, one, 0)

    def wait_sent(sem, sent):
        pltpu.make_async_copy(sent, sent, ss.at[sem]).wait()

    def wait_received(sem, received):
        pltpu.make_async_copy(received, received, rs.at[sem]).wait()

    def wait(sem, part):
        wait_received(sem, part)
        wait_sent(sem, part)

    def scatter(t):
        @pl.when(c == t)
        def _():
            over_cols(
                t,
                lambda j: stg_r.at[pl.ds(j * ch, ch)],
                lambda j: xr.at[t, pl.ds(j * ch, ch)],
            )
            xr[t, pl.ds(t * ch, ch), :] = stg_r[pl.ds(t * ch, ch), :]

        @pl.when(r == t)
        def _():
            over_rows(
                3 + t,
                lambda j: stg_c.at[pl.ds(j * ch, ch)],
                lambda j: xc.at[t, j // 2, lax.rem(j, 2)],
            )
            xc[t, t // 2, t % 2] = stg_c[pl.ds(t * ch, ch), :]

    def scatter_wait(t):
        @pl.when(c == t)
        def _():
            wait_sent(t, stg_r.at[pl.ds(0, (n - 1) * ch)])

        @pl.when(c != t)
        def _():
            wait_received(t, xr.at[t, pl.ds(c * ch, ch)])

        @pl.when(r == t)
        def _():
            wait_sent(3 + t, stg_c.at[pl.ds(0, (n - 1) * ch)])

        @pl.when(r != t)
        def _():
            wait_received(3 + t, xc.at[t, level, parity])

    def gather_cols_start(buf, sem):
        mine = buf.at[pl.ds(c * ch, ch)]
        over_cols(sem, lambda j: mine, lambda j: mine)

    def gather_cols_wait(buf, sem):
        wait(sem, buf.at[pl.ds(0, (n - 1) * ch)])

    def gather_rows_start(buf, sem):
        mine = buf.at[level, parity]

        def one(k, carry):
            send(mine, mine, sem, (lax.rem(level + k, half) * 2 + parity, c))
            return carry

        lax.fori_loop(1, half, one, 0)

    def gather_rows_mid(buf, sem):
        wait(sem, buf.at[pl.ds(0, half - 1), 0])
        mine = buf.at[:, parity]
        send(mine, mine, sem + 1, sibling)

    def gather_rows_wait(buf, sem):
        wait(sem + 1, buf.at[:, 0])

    def sum_start(q, parts, sem, over, me):
        count = len(parts)
        for i, part in enumerate(parts):
            ar_src[q, i] = part
        over(
            sem,
            lambda j: ar_src.at[q, pl.ds(0, count), pl.ds(j * pc, pc)],
            lambda j: ar_slot.at[q, me, pl.ds(0, count)],
        )
        ar_slot[q, me, 0:count] = ar_src[q, 0:count, pl.ds(me * pc, pc), :]

    def sum_slots(q, count, sem):
        wait(sem, ar_slot.at[q, pl.ds(0, n - 1), pl.ds(0, count)])
        total = ar_slot[q, 0, 0:count]
        for j in range(1, n):
            total = total + ar_slot[q, j, 0:count]
        return total

    def sum_spread(q, count, sem, over, me):
        mine = (q, pl.ds(0, count), pl.ds(me * pc, pc))
        over(sem + 1, lambda j: ar_res.at[mine], lambda j: ar_res.at[mine])

    def sum_mid(q, count, sem, over, me):
        ar_res[q, 0:count, pl.ds(me * pc, pc), :] = sum_slots(q, count, sem)
        sum_spread(q, count, sem, over, me)

    def sum_wait(q, count, sem):
        wait(sem + 1, ar_res.at[q, pl.ds(0, count), pl.ds(0, (n - 1) * pc)])

    def all_start(p, part, sem, over, me):
        h_src[p] = part
        over(sem, lambda j: h_src.at[p, pl.ds(j * pc, pc)], lambda j: h_slot.at[p, me])
        h_slot[p, me] = h_src[p, pl.ds(me * pc, pc), :]

    def all_mid(p, sem, over, me):
        wait(sem, h_slot.at[p, pl.ds(0, n - 1)])
        total = h_slot[p, 0]
        for j in range(1, n):
            total = total + h_slot[p, j]
        h_piece[p] = total
        over(sem + 1, lambda j: h_piece.at[p], lambda j: h_ex.at[p, me])
        h_ex[p, me] = total

    def all_late(p, sem, over, me):
        wait(sem + 1, h_ex.at[p, pl.ds(0, n - 1)])
        total = h_ex[p, 0]
        for j in range(1, n):
            total = total + h_ex[p, j]
        h_res[p, pl.ds(me * pc, pc), :] = total
        mine = h_res.at[p, pl.ds(me * pc, pc)]
        over(sem + 2, lambda j: mine, lambda j: mine)

    def all_wait(p, sem):
        wait(sem + 2, h_res.at[p, pl.ds(0, (n - 1) * pc)])

    def tile_product(high_ref, low_ref, at, both):
        wide = mxu(high_ref[pl.ds(at, NB), :], both, NN)
        return wide[:, :NB] + (wide[:, NB:] + mxu(low_ref[pl.ds(at, NB), :], both[:, :NB], NN))

    def halves(panel):
        return jnp.concatenate(split(panel), axis=1)

    def flat(ref):
        return ref[...].reshape(rows, NB)

    def flip(value):
        return jnp.concatenate(
            [value[i * NB : (i + 1) * NB].T for i in range(tiles)], axis=1
        )

    def known_part(r_mat, k, corner):
        kr = exact(k, r_mat)
        return kr + kr.T + exact(exact(r_mat, corner, TN), r_mat)

    def core(z, inner_sum):
        return 0.5 * exact(exact(z, inner_sum, TN), z)

    zero_tile = jnp.zeros((NB, NB), jnp.float32)
    block_rows = min(rows, 2 * NB)

    def keep_left(p, first, second):
        for i, value in enumerate((first, second)):
            spot = slice(i * NB, (i + 1) * NB)
            lh[p, :, spot], ll[p, :, spot] = split(value)

    def keep_right(p, first, second):
        for i, value in enumerate((first, second)):
            spot = slice(i * NB, (i + 1) * NB)
            qh[p, spot, :], ql[p, spot, :] = split(flip(value))

    def apply_first():
        def one(i, carry):
            at = pl.multiple_of(i * block_rows, block_rows)
            high = lh[0, pl.ds(at, block_rows)]
            low = ll[0, pl.ds(at, block_rows)]
            for b in range(0, tiles, 2):
                cols = slice(b * NB, (b + 2) * NB)
                change = mxu(high, qh[0, :, cols], NN) + (
                    mxu(high, ql[0, :, cols], NN) + mxu(low, qh[0, :, cols], NN)
                )
                for k in range(block_rows // NB):
                    for j in range(2):
                        spot = pl.ds((at + k * NB) * tiles + b + j, NB, stride=tiles)
                        part = change[k * NB : (k + 1) * NB, j * NB : (j + 1) * NB]
                        abuf[spot, :] = abuf[spot, :] - part
            return carry

        lax.fori_loop(0, rows // block_rows, one, 0)

    def write_band(p, r_ref):
        @pl.when(c == p)
        def _():
            for a in range(tiles):
                spot = pl.ds(a * NB * tiles, NB, stride=tiles)

                @pl.when(a * n + r == p + 1)
                def _():
                    abuf[spot, :] = -r_ref[...]

                @pl.when(a * n + r > p + 1)
                def _():
                    abuf[spot, :] = zero_tile

        @pl.when(r == p)
        def _():
            for b in range(tiles):
                spot = pl.ds(b, NB, stride=tiles)

                @pl.when(b * n + c == p + 1)
                def _():
                    abuf[spot, :] = -r_ref[...].T

                @pl.when(b * n + c > p + 1)
                def _():
                    abuf[spot, :] = zero_tile

    load.wait()
    for t in range(3):

        @pl.when(c == t)
        def _():
            for a in range(tiles):
                stg_r[a * NB : (a + 1) * NB, :] = abuf[pl.ds(a * NB * tiles, NB, stride=tiles), :]

            @pl.when(r == 0)
            def _():
                stg_r[0:NB, :] = zero_tile

        @pl.when(r == t)
        def _():
            for b in range(tiles):
                stg_c[b * NB : (b + 1) * NB, :] = abuf[pl.ds(b, NB, stride=tiles), :].T

            @pl.when(c == 0)
            def _():
                stg_c[0:NB, :] = zero_tile

    pl.semaphore_wait(barrier, 2 * (n - 1) + jnp.where(r != c, 1, 0))
    scatter(0)

    def tile_start(sem, index, t, owner):
        @pl.when((r == t) & (c == owner))
        def _():
            over_cols(
                sem,
                lambda j: stg_c.at[pl.ds(j * pc, pc)],
                lambda j: ar_res.at[0, index, pl.ds(j * pc, pc)],
            )
            ar_res[0, index, pl.ds(c * pc, pc), :] = stg_c[pl.ds(c * pc, pc), :]

    def tile_wait(sem, index, t, owner):
        @pl.when((r == t) & (c == owner))
        def _():
            wait_sent(sem, stg_c.at[pl.ds(0, (n - 1) * pc)])

        @pl.when((r == t) & (c != owner))
        def _():
            wait_received(sem, ar_res.at[0, index, pl.ds(c * pc, pc)])

    def row_start(sem, t, first, count):
        mine = (0, pl.ds(first, count), pl.ds(c * pc, pc))

        @pl.when(r == t)
        def _():
            over_rows(sem, lambda j: ar_res.at[mine], lambda j: ar_res.at[mine])

    def row_wait(sem, t, first, count):
        @pl.when(r == t)
        def _():
            wait_sent(sem, ar_res.at[0, pl.ds(first, count), pl.ds(0, (n - 1) * pc)])

        @pl.when(r != t)
        def _():
            wait_received(sem, ar_res.at[0, pl.ds(first, count), pl.ds(c * pc, pc)])

    @pl.when(r == 0)
    def _():
        mine = stg_c[...]
        first = jnp.where(c == 1, mine[0:NB], 0.0)
        second = jnp.where(c == 2, mine[0:NB], 0.0)
        sum_start(0, [dot3(mine, mine, TN), first, second], 9, over_cols, c)

    t_ref[...] = zero_tile

    @pl.when(r == 0)
    def _():
        ar_res[0, 0:3, pl.ds(c * pc, pc), :] = sum_slots(0, 3, 9)

    row_start(19, 0, 0, 3)
    scatter_wait(0)
    gather_rows_start(xc.at[0], 6)
    gather_cols_start(xr.at[0], 8)
    scatter(1)
    tile_start(43, 3, 1, 1)
    tile_start(44, 4, 1, 2)
    scatter(2)
    tile_start(45, 5, 2, 2)

    def to_parts(a, carry):
        at = pl.multiple_of(a * NB, NB)
        for b in range(tiles):
            high, low = split(abuf[pl.ds(a * NB * tiles + b, NB, stride=tiles), :])
            ahi[pl.ds(at, NB), b * NB : (b + 1) * NB] = high
            alo[pl.ds(at, NB), b * NB : (b + 1) * NB] = low
        return carry

    lax.fori_loop(0, tiles, to_parts, 0)

    def to_flipped(b, carry):
        at = pl.multiple_of(b * NB, NB)
        for a in range(tiles):
            high, low = split(abuf[pl.ds(a * NB * tiles + b, NB, stride=tiles), :].T)
            thi[pl.ds(at, NB), a * NB : (a + 1) * NB] = high
            tlo[pl.ds(at, NB), a * NB : (a + 1) * NB] = low
        return carry

    lax.fori_loop(0, tiles // 2, to_flipped, 0)

    row_wait(19, 0, 0, 3)
    sum_spread(0, 3, 9, over_cols, c)
    scatter_wait(1)
    gather_cols_start(xr.at[1], 13)
    gather_rows_mid(xc.at[0], 6)
    tile_wait(43, 3, 1, 1)
    tile_wait(44, 4, 1, 2)
    tile_wait(45, 5, 2, 2)
    row_start(46, 1, 3, 2)
    row_start(47, 2, 5, 1)
    scatter_wait(2)
    gather_rows_wait(xc.at[0], 6)

    both = halves(flat(xc.at[0]))

    def first_product(a, carry):
        at = pl.multiple_of(a * NB, NB)
        wpart_r[pl.ds(at, NB), :] = tile_product(ahi, alo, at, both)
        for i in range(per_tile):
            j = a * per_tile + i
            mine = wpart_r.at[pl.ds(j * ch, ch)]

            @pl.when(j != c)
            def _():
                send(mine, wslot_r.at[c], 20, (r, j))

        return carry

    lax.fori_loop(0, tiles, first_product, 0)
    wslot_r[c] = wpart_r[pl.ds(c * ch, ch), :]
    gather_cols_wait(xr.at[0], 8)
    all_start(0, dot3(xr[0], wpart_r[...], TN), 26, over_rows, r)
    gather_rows_start(xc.at[1], 11)
    sum_wait(0, 3, 9)
    g_ref[...] = ar_res[0, 0]
    cholesky_blocks(g_ref, r0_ref, 0, CHOL_BLOCKS)
    all_mid(0, 26, over_cols, c)
    gather_cols_wait(xr.at[1], 13)
    sum_start(1, [dot3(xr[0], xr[1], TN)], 14, over_rows, r)
    y_ref[...] = ar_res[0, 0] + exact(ar_res[0, 1], r0_ref[...], TN)
    inverse_blocks(y_ref, t_ref, 0, INV_BLOCKS // 2)

    wait(20, wslot_r.at[pl.ds(0, n - 1)])
    total = wslot_r[0]
    for j in range(1, n):
        total = total + wslot_r[j]
    wr[0, pl.ds(c * ch, ch), :] = total
    gather_cols_start(wr.at[0], 23)
    wch[0] = total

    @pl.when(r != c)
    def _():
        send(wch.at[0], wc.at[0, c // 2, lax.rem(c, 2)], 22, (c, r))

    @pl.when(r == c)
    def _():
        wc[0, level, parity] = total

    all_late(0, 26, over_rows, r)
    sum_mid(1, 1, 14, over_rows, r)
    row_wait(46, 1, 3, 2)
    row_wait(47, 2, 5, 1)
    tiles_mine = (0, pl.ds(3, 3), pl.ds(c * pc, pc))
    over_cols(48, lambda j: ar_res.at[tiles_mine], lambda j: ar_res.at[tiles_mine])
    inverse_blocks(y_ref, t_ref, INV_BLOCKS // 2, INV_BLOCKS)
    lax.fori_loop(tiles // 2, tiles, to_flipped, 0)
    gather_rows_mid(xc.at[1], 11)

    @pl.when(r != c)
    def _():
        wait_received(22, wc.at[0, level, parity])
        wait_sent(22, wch.at[0])

    gather_rows_start(wc.at[0], 24)
    wait(48, ar_res.at[0, pl.ds(3, 3), pl.ds(0, (n - 1) * pc)])
    sum_wait(1, 1, 14)
    r0 = r0_ref[...]
    z0 = y_ref[...]
    k0 = ar_res[1, 0]
    rz0 = exact(r0, z0)
    f01 = ar_res[0, 1] + r0
    f02 = ar_res[0, 2]
    x11 = ar_res[0, 3]
    x12 = ar_res[0, 4]
    x22 = ar_res[0, 5]
    known = known_part(r0, k0, x11)
    c01 = exact(k0, z0, TN) + exact(x11, rz0)
    all_wait(0, 26)
    b0 = core(z0, h_res[0] + known)
    c01 = c01 - exact(f01, b0)
    coef = jnp.concatenate([z0, rz0, -b0], axis=0)
    carried = exact(coef, f01, NT)
    last = carried[2 * NB :] + c01.T
    coef = jnp.concatenate(
        [coef, jnp.concatenate([carried[: 2 * NB], last], axis=0)], axis=1
    )

    def first_panel(f_ref, c_ref, x0, x1, index):
        f_ref[0] = x0

        @pl.when(index == 1)
        def _():
            f_ref[0, 0:NB, :] = f_ref[0, 0:NB, :] + r0

        out = dot3(jnp.concatenate([x1, f_ref[0]], axis=1), coef[NB:], NN)
        c_ref[0] = out[:, :NB]
        f_ref[1] = x1 - out[:, NB:]

    def first_panel_product(f_ref, c_ref, w, index):
        out = dot3(w, coef[:NB], NN)
        c_ref[0] = c_ref[0] + out[:, :NB]
        f_ref[1] = f_ref[1] - out[:, NB:]

        @pl.when(index == 0)
        def _():
            c_ref[0, 0:NB, :] = zero_tile

        @pl.when(index <= 1)
        def _():
            f_ref[1, 0:NB, :] = zero_tile

    first_panel(panel_r, cor_r, xr[0], xr[1], r)
    gather_cols_wait(wr.at[0], 23)
    gather_cols_start(xr.at[2], 18)
    first_panel_product(panel_r, cor_r, wr[0], r)

    p1r = panel_r[1]
    sum_start(2, [dot3(p1r, p1r, TN)], 30, over_rows, r)
    both = halves(p1r)

    def second_product(b, carry):
        at = pl.multiple_of(b * NB, NB)
        value = tile_product(thi, tlo, at, both).reshape(per_tile, ch, NB)
        for i in range(per_tile):
            j = b * per_tile + i
            wpart_c[j // 2, lax.rem(j, 2)] = value[i]
        return carry

    lax.fori_loop(0, tiles, second_product, 0)
    send(wpart_c.at[:, 1 - parity], wsib, 34, sibling)
    sum_mid(2, 1, 30, over_rows, r)
    wait(34, wsib)
    wsum[...] = wpart_c[:, parity] + wsib[...]

    def spread(k, carry):
        to = lax.rem(level + k, half)
        send(wsum.at[to], wslot_c.at[level], 35, (to * 2 + parity, c))
        return carry

    lax.fori_loop(1, half, spread, 0)
    wslot_c[level] = wsum[level]
    gather_rows_mid(wc.at[0], 24)
    gather_rows_start(xc.at[2], 16)
    gather_rows_wait(xc.at[1], 11)
    first_panel(panel_c, cor_c, flat(xc.at[0]), flat(xc.at[1]), c)
    gather_cols_wait(xr.at[2], 18)
    inner = dot3(xr[2], jnp.concatenate([xr[0], panel_r[1]], axis=1), TN)
    sum_start(4, [inner[:, 0:NB], inner[:, NB:]], 49, over_rows, r)
    gather_rows_wait(wc.at[0], 24)
    first_panel_product(panel_c, cor_c, flat(wc.at[0]), c)
    p1c = panel_c[1]
    all_start(1, dot3(p1c, flat(wpart_c), TN), 36, over_cols, c)
    inner = dot3(p1c, jnp.concatenate([panel_c[0], cor_c[0]], axis=1), TN)
    sum_start(3, [inner[:, 0:NB], inner[:, NB:]], 32, over_cols, c)
    keep_left(0, cor_r[0], panel_r[0])
    keep_right(0, panel_c[0], cor_c[0])
    sum_wait(2, 1, 30)
    g_ref[...] = ar_res[2, 0]
    cholesky_blocks(g_ref, r1_ref, 0, CHOL_BLOCKS // 2)
    all_mid(1, 36, over_rows, r)
    sum_mid(4, 2, 49, over_rows, r)

    wait(35, wslot_c.at[pl.ds(0, half - 1)])
    total = wslot_c[0]
    for j in range(1, half):
        total = total + wslot_c[j]
    wch[1] = total

    @pl.when(r != c)
    def _():
        send(wch.at[1], wr.at[1, pl.ds(r * ch, ch)], 41, (c, r))

    @pl.when(r == c)
    def _():
        wr[1, pl.ds(c * ch, ch), :] = total

    wc[1, level, parity] = total
    gather_rows_start(wc.at[1], 39)
    cholesky_blocks(g_ref, r1_ref, CHOL_BLOCKS // 2, CHOL_BLOCKS)
    sum_mid(3, 2, 32, over_cols, c)
    gather_rows_mid(xc.at[2], 16)
    all_late(1, 36, over_cols, c)
    sum_wait(4, 2, 49)
    c02 = exact(ar_res[4, 0], z0) + exact(x12, rz0) - exact(f02, b0)
    top = x12 - exact(c02, f01, NT) - exact(f02, c01, NT)
    y_ref[...] = ar_res[2, 0] + exact(top, r1_ref[...], TN)
    inverse_blocks(y_ref, t_ref, 0, INV_BLOCKS // 2)

    @pl.when(r != c)
    def _():
        wait_received(41, wr.at[1, pl.ds(c * ch, ch)])
        wait_sent(41, wch.at[1])

    gather_cols_start(wr.at[1], 42)
    inverse_blocks(y_ref, t_ref, INV_BLOCKS // 2, INV_BLOCKS)
    gather_rows_mid(wc.at[1], 39)
    r1 = r1_ref[...]
    z1 = y_ref[...]
    rz1 = exact(r1, z1)
    sum_wait(3, 2, 32)
    j1t = ar_res[3, 0]
    j2t = ar_res[3, 1]
    cross = exact(j2t, j1t, NT)
    cf = exact(c02, f02, NT)
    k1 = ar_res[4, 1].T - exact(j2t, f02, NT) - exact(j1t, c02, NT)
    known = known_part(r1, k1, x22 - cf - cf.T) - cross - cross.T
    fold1 = -exact(j1t, z1, TN) - exact(f02, rz1, TN)
    fold2 = -exact(j2t, z1, TN) - exact(c02, rz1, TN)
    apply_first()
    write_band(0, r0_ref)
    write_band(1, r1_ref)
    pltpu.make_async_copy(abuf, a_out, asem).start()
    all_wait(1, 36)
    b1 = core(z1, h_res[1] + known)
    coef = jnp.concatenate([z1, rz1, fold1, fold2, -b1], axis=0)

    def second_panel(f_ref, c_ref, x2, index):
        @pl.when(index == 2)
        def _():
            f_ref[1, 0:NB, :] = f_ref[1, 0:NB, :] + r1

        c_ref[1] = dot3(
            jnp.concatenate([x2, c_ref[0], f_ref[0], f_ref[1]], axis=1), coef[NB:], NN
        )

    def second_panel_product(c_ref, w, index):
        c_ref[1] = c_ref[1] + dot3(w, coef[:NB], NN)

        @pl.when(index <= 1)
        def _():
            c_ref[1, 0:NB, :] = zero_tile

    second_panel(panel_r, cor_r, xr[2], r)
    gather_rows_wait(xc.at[2], 16)
    second_panel(panel_c, cor_c, flat(xc.at[2]), c)
    gather_rows_wait(wc.at[1], 39)
    second_panel_product(cor_c, flat(wc.at[1]), c)
    keep_right(1, panel_c[1], cor_c[1])
    pltpu.make_async_copy(qh.at[1], qh_out, osem).start()
    pltpu.make_async_copy(ql.at[1], ql_out, osem2).start()
    gather_cols_wait(wr.at[1], 42)
    second_panel_product(cor_r, wr[1], r)
    keep_left(1, cor_r[1], panel_r[1])
    last_high = pltpu.make_async_copy(lh.at[1], lh_out, osem3)
    last_low = pltpu.make_async_copy(ll.at[1], ll_out, osem4)
    last_high.start()
    last_low.start()
    pltpu.make_async_copy(abuf, a_out, asem).wait()
    pltpu.make_async_copy(qh.at[1], qh_out, osem).wait()
    pltpu.make_async_copy(ql.at[1], ql_out, osem2).wait()
    last_high.wait()
    last_low.wait()


def update_kernel(tiles, a_ref, lh, ll, qh, ql, o_ref):
    high = lh[...]
    low = ll[...]
    for b in range(0, tiles, 2):
        cols = slice(b * NB, (b + 2) * NB)
        change = mxu(high, qh[:, cols], NN) + (
            mxu(high, ql[:, cols], NN) + mxu(low, qh[:, cols], NN)
        )
        for k in range(high.shape[0] // NB):
            for j in range(2):
                spot = pl.ds(k * NB * tiles + b + j, NB, stride=tiles)
                part = change[k * NB : (k + 1) * NB, j * NB : (j + 1) * NB]
                o_ref[spot, :] = a_ref[spot, :] - part


def local(hamiltonian):
    tiles = hamiltonian.shape[0]
    n = lax.axis_size("row")
    rows = tiles * NB
    ch = rows // n
    pc = NB // n
    half = n // 2
    f32 = jnp.float32
    bf16 = jnp.bfloat16
    block = hamiltonian.reshape(rows * tiles, NB)
    shapes = [
        ((rows * tiles, NB), f32),
        ((rows, rows), bf16),
        ((rows, rows), bf16),
        ((rows, rows), bf16),
        ((rows, rows), bf16),
        ((rows, NB), f32),
        ((rows, NB), f32),
        ((3, rows, NB), f32),
        ((3, half, 2, ch, NB), f32),
        ((rows, NB), f32),
        ((n, ch, NB), f32),
        ((half, 2, ch, NB), f32),
        ((half, ch, NB), f32),
        ((half, ch, NB), f32),
        ((half, ch, NB), f32),
        ((2, ch, NB), f32),
        ((2, rows, NB), f32),
        ((2, half, 2, ch, NB), f32),
        ((2, rows, NB), f32),
        ((2, rows, NB), f32),
        ((2, rows, NB), f32),
        ((2, rows, NB), f32),
        ((2, rows, 2 * NB), bf16),
        ((2, rows, 2 * NB), bf16),
        ((2, 2 * NB, rows), bf16),
        ((2, 2 * NB, rows), bf16),
        ((5, 3, NB, NB), f32),
        ((5, n, 3, pc, NB), f32),
        ((5, 6, NB, NB), f32),
        ((2, NB, NB), f32),
        ((2, n, pc, NB), f32),
        ((2, pc, NB), f32),
        ((2, n, pc, NB), f32),
        ((2, NB, NB), f32),
    ] + [((NB, NB), f32)] * 5
    anywhere = pl.BlockSpec(memory_space=pl.ANY)
    left = jax.ShapeDtypeStruct((rows, 2 * NB), bf16)
    right = jax.ShapeDtypeStruct((2 * NB, rows), bf16)
    parts = pl.pallas_call(
        functools.partial(reduce_kernel, n, tiles),
        out_shape=[jax.ShapeDtypeStruct((rows * tiles, NB), f32), left, left, right, right],
        in_specs=[anywhere],
        out_specs=[anywhere] * 5,
        scratch_shapes=[pltpu.VMEM(*shape) for shape in shapes]
        + [pltpu.SemaphoreType.DMA] * 5
        + [pltpu.SemaphoreType.DMA((51,))] * 2,
        compiler_params=pltpu.CompilerParams(
            collective_id=0, has_side_effects=True, vmem_limit_bytes=VMEM_LIMIT
        ),
        name="reduce_panels",
    )(block)
    step = min(rows, 2 * NB)
    block_spec = pl.BlockSpec((step * tiles, NB), lambda i: (i, 0))
    left_spec = pl.BlockSpec((step, 2 * NB), lambda i: (i, 0))
    right_spec = pl.BlockSpec((2 * NB, rows), lambda i: (0, 0))
    result = pl.pallas_call(
        functools.partial(update_kernel, tiles),
        out_shape=jax.ShapeDtypeStruct((rows * tiles, NB), f32),
        grid=(rows // step,),
        in_specs=[block_spec, left_spec, left_spec, right_spec, right_spec],
        out_specs=block_spec,
        compiler_params=pltpu.CompilerParams(vmem_limit_bytes=VMEM_LIMIT),
        name="update_matrix",
    )(*parts)
    return result.reshape(hamiltonian.shape)


def solution(mesh):
    spec = P(None, "row", None, None, "col", None)
    return jax.shard_map(local, mesh=mesh, in_specs=(spec,), out_specs=spec, check_vma=False)
```

```python
import functools

import jax
import jax.numpy as jnp
from jax import lax
from jax.experimental import pallas as pl
from jax.experimental.pallas import tpu as pltpu
from jax.sharding import PartitionSpec as P

MESH = pl.DeviceIdType.MESH
NB = 128
NN = (((1,), (0,)), ((), ()))
NT = (((1,), (1,)), ((), ()))
TN = (((0,), (0,)), ((), ()))
TT = (((0,), (1,)), ((), ()))
VMEM_LIMIT = 56 << 20
CHOL_WIDTH = 32
INV_WIDTH = 16
CHOL_BLOCKS = NB // CHOL_WIDTH
INV_BLOCKS = NB // INV_WIDTH


def split(value):
    high = value.astype(jnp.bfloat16)
    low = (value - high.astype(jnp.float32)).astype(jnp.bfloat16)
    return high, low


def mxu(first, second, dims):
    return lax.dot_general(first, second, dims, preferred_element_type=jnp.float32)


def dot3(first, second, dims):
    fh, fl = split(first)
    sh, sl = split(second)
    return mxu(fh, sh, dims) + (mxu(fh, sl, dims) + mxu(fl, sh, dims))


def exact(first, second, dims=NN):
    return lax.dot_general(
        first, second, dims, precision=lax.Precision.HIGHEST, preferred_element_type=jnp.float32
    )


def iota(axis, shape):
    return lax.broadcasted_iota(jnp.int32, shape, axis)


def leading_columns(x, base, width):
    rolled = pltpu.roll(x, lax.rem(NB - base, NB), 1)
    return [jnp.broadcast_to(rolled[:, i : i + 1], (width, NB)) for i in range(width)]


def cholesky_blocks(g_ref, r_ref, first, last):
    width = CHOL_WIDTH
    sub = iota(0, (width, NB))
    lane = iota(1, (width, NB))

    def block(k, carry):
        base = pl.multiple_of(k * width, width)
        x = g_ref[pl.ds(base, width), :]
        cols = leading_columns(x, base, width)
        for i in range(width):
            scale = lax.rsqrt(cols[i][i : i + 1, :])
            column = cols[i] * scale
            below = jnp.where(sub > i, column, 0.0)
            row = x[i : i + 1, :] * scale
            x = jnp.where(sub == i, row, x - below * row)
            for m in range(i + 1, width):
                cols[m] = cols[m] - below * column[m : m + 1, :]
        x = jnp.where(lane >= base + sub, x, 0.0)
        r_ref[pl.ds(base, width), :] = x
        g_ref[...] -= exact(x, x, TN)
        return carry

    lax.fori_loop(first, last, block, 0)


def inverse_blocks(y_ref, t_ref, first, last):
    width = INV_WIDTH
    sub = iota(0, (width, NB))
    lane = iota(1, (width, NB))
    wide = iota(1, (NB, NB))

    def block(k, carry):
        base = pl.multiple_of(k * width, width)
        x = y_ref[pl.ds(base, width), :]
        cols = leading_columns(x, base, width)
        inside = (lane >= base) & (lane < base + width)
        x = jnp.where(inside, jnp.where(lane - base == sub, 1.0, 0.0), x)
        for i in range(width):
            scale = 1.0 / cols[i][i : i + 1, :]
            factor = jnp.where(sub == i, 0.0, cols[i])
            row = x[i : i + 1, :] * scale
            x = jnp.where(sub == i, row, x - factor * row)
            for m in range(i + 1, width):
                entry = cols[m][i : i + 1, :] * scale
                cols[m] = jnp.where(sub == i, entry, cols[m] - factor * entry)
        t_ref[pl.ds(base, width), :] = x
        y = y_ref[...]
        chosen = (wide >= base) & (wide < base + width)
        y_ref[...] = jnp.where(chosen, 0.0, y) - exact(jnp.where(chosen, y, 0.0), t_ref[...])
        y_ref[pl.ds(base, width), :] = x
        t_ref[pl.ds(base, width), :] = jnp.zeros((width, NB), jnp.float32)
        return carry

    lax.fori_loop(first, last, block, 0)


def reduce_kernel(n, tiles, *refs):
    rows = tiles * NB
    ch = rows // n
    pc = NB // n
    half = n // 2
    per_tile = NB // ch
    (
        a_hbm, a_out, lh_out, ll_out, qh_out, ql_out,
        abuf, ahi, alo, thi, tlo, stg_r, stg_c, xr, xc,
        wpart_r, wslot_r, wpart_c, wsib, wsum, wslot_c, wch, wr, wc,
        panel_r, panel_c, cor_r, cor_c, lh, ll, qh, ql,
        ar_src, ar_slot, ar_res, h_src, h_slot, h_piece, h_ex, h_res,
        g_ref, y_ref, t_ref, r0_ref, r1_ref, asem, osem, osem2, osem3, osem4, ss, rs,
    ) = refs
    r = lax.axis_index("row")
    c = lax.axis_index("col")
    parity = lax.rem(r, 2)
    level = r // 2
    sibling = (r + 1 - 2 * parity, c)

    load = pltpu.make_async_copy(a_hbm, abuf, asem)
    load.start()
    barrier = pltpu.get_barrier_semaphore()

    def greet(k, carry):
        pl.semaphore_signal(barrier, inc=1, device_id=(lax.rem(r + k, n), c), device_id_type=MESH)
        pl.semaphore_signal(barrier, inc=1, device_id=(r, lax.rem(c + k, n)), device_id_type=MESH)
        return carry

    lax.fori_loop(1, n, greet, 0)

    @pl.when(r != c)
    def _():
        pl.semaphore_signal(barrier, inc=1, device_id=(c, r), device_id_type=MESH)

    def send(src, dst, sem, device):
        pltpu.make_async_remote_copy(
            src, dst, ss.at[sem], rs.at[sem], device_id=device, device_id_type=MESH
        ).start()

    def over_cols(sem, src_of, dst_of):
        def one(k, carry):
            j = lax.rem(c + k, n)
            send(src_of(j), dst_of(j), sem, (r, j))
            return carry

        lax.fori_loop(1, n, one, 0)

    def over_rows(sem, src_of, dst_of):
        def one(k, carry):
            j = lax.rem(r + k, n)
            send(src_of(j), dst_of(j), sem, (j, c))
            return carry

        lax.fori_loop(1, n, one, 0)

    def wait_sent(sem, sent):
        pltpu.make_async_copy(sent, sent, ss.at[sem]).wait()

    def wait_received(sem, received):
        pltpu.make_async_copy(received, received, rs.at[sem]).wait()

    def wait(sem, part):
        wait_received(sem, part)
        wait_sent(sem, part)

    def scatter(t):
        @pl.when(c == t)
        def _():
            over_cols(
                t,
                lambda j: stg_r.at[pl.ds(j * ch, ch)],
                lambda j: xr.at[t, pl.ds(j * ch, ch)],
            )
            xr[t, pl.ds(t * ch, ch), :] = stg_r[pl.ds(t * ch, ch), :]

        @pl.when(r == t)
        def _():
            over_rows(
                3 + t,
                lambda j: stg_c.at[pl.ds(j * ch, ch)],
                lambda j: xc.at[t, j // 2, lax.rem(j, 2)],
            )
            xc[t, t // 2, t % 2] = stg_c[pl.ds(t * ch, ch), :]

    def scatter_wait(t):
        @pl.when(c == t)
        def _():
            wait_sent(t, stg_r.at[pl.ds(0, (n - 1) * ch)])

        @pl.when(c != t)
        def _():
            wait_received(t, xr.at[t, pl.ds(c * ch, ch)])

        @pl.when(r == t)
        def _():
            wait_sent(3 + t, stg_c.at[pl.ds(0, (n - 1) * ch)])

        @pl.when(r != t)
        def _():
            wait_received(3 + t, xc.at[t, level, parity])

    def gather_cols_start(buf, sem):
        mine = buf.at[pl.ds(c * ch, ch)]
        over_cols(sem, lambda j: mine, lambda j: mine)

    def gather_cols_wait(buf, sem):
        wait(sem, buf.at[pl.ds(0, (n - 1) * ch)])

    def gather_rows_start(buf, sem):
        mine = buf.at[level, parity]

        def one(k, carry):
            send(mine, mine, sem, (lax.rem(level + k, half) * 2 + parity, c))
            return carry

        lax.fori_loop(1, half, one, 0)

    def gather_rows_mid(buf, sem):
        wait(sem, buf.at[pl.ds(0, half - 1), 0])
        mine = buf.at[:, parity]
        send(mine, mine, sem + 1, sibling)

    def gather_rows_wait(buf, sem):
        wait(sem + 1, buf.at[:, 0])

    def sum_start(q, parts, sem, over, me):
        count = len(parts)
        for i, part in enumerate(parts):
            ar_src[q, i] = part
        over(
            sem,
            lambda j: ar_src.at[q, pl.ds(0, count), pl.ds(j * pc, pc)],
            lambda j: ar_slot.at[q, me, pl.ds(0, count)],
        )
        ar_slot[q, me, 0:count] = ar_src[q, 0:count, pl.ds(me * pc, pc), :]

    def sum_slots(q, count, sem):
        wait(sem, ar_slot.at[q, pl.ds(0, n - 1), pl.ds(0, count)])
        total = ar_slot[q, 0, 0:count]
        for j in range(1, n):
            total = total + ar_slot[q, j, 0:count]
        return total

    def sum_spread(q, count, sem, over, me):
        mine = (q, pl.ds(0, count), pl.ds(me * pc, pc))
        over(sem + 1, lambda j: ar_res.at[mine], lambda j: ar_res.at[mine])

    def sum_mid(q, count, sem, over, me):
        ar_res[q, 0:count, pl.ds(me * pc, pc), :] = sum_slots(q, count, sem)
        sum_spread(q, count, sem, over, me)

    def sum_wait(q, count, sem):
        wait(sem + 1, ar_res.at[q, pl.ds(0, count), pl.ds(0, (n - 1) * pc)])

    def all_start(p, part, sem, over, me):
        h_src[p] = part
        over(sem, lambda j: h_src.at[p, pl.ds(j * pc, pc)], lambda j: h_slot.at[p, me])
        h_slot[p, me] = h_src[p, pl.ds(me * pc, pc), :]

    def all_mid(p, sem, over, me):
        wait(sem, h_slot.at[p, pl.ds(0, n - 1)])
        total = h_slot[p, 0]
        for j in range(1, n):
            total = total + h_slot[p, j]
        h_piece[p] = total
        over(sem + 1, lambda j: h_piece.at[p], lambda j: h_ex.at[p, me])
        h_ex[p, me] = total

    def all_late(p, sem, over, me):
        wait(sem + 1, h_ex.at[p, pl.ds(0, n - 1)])
        total = h_ex[p, 0]
        for j in range(1, n):
            total = total + h_ex[p, j]
        h_res[p, pl.ds(me * pc, pc), :] = total
        mine = h_res.at[p, pl.ds(me * pc, pc)]
        over(sem + 2, lambda j: mine, lambda j: mine)

    def all_wait(p, sem):
        wait(sem + 2, h_res.at[p, pl.ds(0, (n - 1) * pc)])

    def tile_product(high_ref, low_ref, at, both):
        wide = mxu(high_ref[pl.ds(at, NB), :], both, NN)
        return wide[:, :NB] + (wide[:, NB:] + mxu(low_ref[pl.ds(at, NB), :], both[:, :NB], NN))

    def halves(panel):
        return jnp.concatenate(split(panel), axis=1)

    def flat(ref):
        return ref[...].reshape(rows, NB)

    def flip(value):
        return jnp.concatenate(
            [value[i * NB : (i + 1) * NB].T for i in range(tiles)], axis=1
        )

    def known_part(r_mat, k, corner):
        kr = exact(k, r_mat)
        return kr + kr.T + exact(exact(r_mat, corner, TN), r_mat)

    def core(z, inner_sum):
        return 0.5 * exact(exact(z, inner_sum, TN), z)

    zero_tile = jnp.zeros((NB, NB), jnp.float32)
    block_rows = min(rows, 2 * NB)

    def keep_left(p, first, second):
        for i, value in enumerate((first, second)):
            spot = slice(i * NB, (i + 1) * NB)
            lh[p, :, spot], ll[p, :, spot] = split(value)

    def keep_right(p, first, second):
        for i, value in enumerate((first, second)):
            spot = slice(i * NB, (i + 1) * NB)
            qh[p, spot, :], ql[p, spot, :] = split(flip(value))

    def apply_first():
        def one(i, carry):
            at = pl.multiple_of(i * block_rows, block_rows)
            high = lh[0, pl.ds(at, block_rows)]
            low = ll[0, pl.ds(at, block_rows)]
            for b in range(0, tiles, 2):
                cols = slice(b * NB, (b + 2) * NB)
                change = mxu(high, qh[0, :, cols], NN) + (
                    mxu(high, ql[0, :, cols], NN) + mxu(low, qh[0, :, cols], NN)
                )
                for k in range(block_rows // NB):
                    for j in range(2):
                        spot = pl.ds((at + k * NB) * tiles + b + j, NB, stride=tiles)
                        part = change[k * NB : (k + 1) * NB, j * NB : (j + 1) * NB]
                        abuf[spot, :] = abuf[spot, :] - part
            return carry

        lax.fori_loop(0, rows // block_rows, one, 0)

    def write_band(p, r_ref):
        @pl.when(c == p)
        def _():
            for a in range(tiles):
                spot = pl.ds(a * NB * tiles, NB, stride=tiles)

                @pl.when(a * n + r == p + 1)
                def _():
                    abuf[spot, :] = -r_ref[...]

                @pl.when(a * n + r > p + 1)
                def _():
                    abuf[spot, :] = zero_tile

        @pl.when(r == p)
        def _():
            for b in range(tiles):
                spot = pl.ds(b, NB, stride=tiles)

                @pl.when(b * n + c == p + 1)
                def _():
                    abuf[spot, :] = -r_ref[...].T

                @pl.when(b * n + c > p + 1)
                def _():
                    abuf[spot, :] = zero_tile

    load.wait()
    for t in range(3):

        @pl.when(c == t)
        def _():
            for a in range(tiles):
                stg_r[a * NB : (a + 1) * NB, :] = abuf[pl.ds(a * NB * tiles, NB, stride=tiles), :]

            @pl.when(r == 0)
            def _():
                stg_r[0:NB, :] = zero_tile

        @pl.when(r == t)
        def _():
            for b in range(tiles):
                stg_c[b * NB : (b + 1) * NB, :] = abuf[pl.ds(b, NB, stride=tiles), :].T

            @pl.when(c == 0)
            def _():
                stg_c[0:NB, :] = zero_tile

    pl.semaphore_wait(barrier, 2 * (n - 1) + jnp.where(r != c, 1, 0))
    scatter(0)

    def tile_start(sem, index, t, owner):
        @pl.when((r == t) & (c == owner))
        def _():
            over_cols(
                sem,
                lambda j: stg_c.at[pl.ds(j * pc, pc)],
                lambda j: ar_res.at[0, index, pl.ds(j * pc, pc)],
            )
            ar_res[0, index, pl.ds(c * pc, pc), :] = stg_c[pl.ds(c * pc, pc), :]

    def tile_wait(sem, index, t, owner):
        @pl.when((r == t) & (c == owner))
        def _():
            wait_sent(sem, stg_c.at[pl.ds(0, (n - 1) * pc)])

        @pl.when((r == t) & (c != owner))
        def _():
            wait_received(sem, ar_res.at[0, index, pl.ds(c * pc, pc)])

    def row_start(sem, t, first, count):
        mine = (0, pl.ds(first, count), pl.ds(c * pc, pc))

        @pl.when(r == t)
        def _():
            over_rows(sem, lambda j: ar_res.at[mine], lambda j: ar_res.at[mine])

    def row_wait(sem, t, first, count):
        @pl.when(r == t)
        def _():
            wait_sent(sem, ar_res.at[0, pl.ds(first, count), pl.ds(0, (n - 1) * pc)])

        @pl.when(r != t)
        def _():
            wait_received(sem, ar_res.at[0, pl.ds(first, count), pl.ds(c * pc, pc)])

    @pl.when(r == 0)
    def _():
        mine = stg_c[...]
        first = jnp.where(c == 1, mine[0:NB], 0.0)
        second = jnp.where(c == 2, mine[0:NB], 0.0)
        sum_start(0, [dot3(mine, mine, TN), first, second], 9, over_cols, c)

    t_ref[...] = zero_tile

    @pl.when(r == 0)
    def _():
        ar_res[0, 0:3, pl.ds(c * pc, pc), :] = sum_slots(0, 3, 9)

    row_start(19, 0, 0, 3)
    scatter_wait(0)
    gather_rows_start(xc.at[0], 6)
    gather_cols_start(xr.at[0], 8)
    scatter(1)
    tile_start(43, 3, 1, 1)
    tile_start(44, 4, 1, 2)
    scatter(2)
    tile_start(45, 5, 2, 2)

    def to_parts(a, carry):
        at = pl.multiple_of(a * NB, NB)
        for b in range(tiles):
            high, low = split(abuf[pl.ds(a * NB * tiles + b, NB, stride=tiles), :])
            ahi[pl.ds(at, NB), b * NB : (b + 1) * NB] = high
            alo[pl.ds(at, NB), b * NB : (b + 1) * NB] = low
        return carry

    lax.fori_loop(0, tiles, to_parts, 0)

    def to_flipped(b, carry):
        at = pl.multiple_of(b * NB, NB)
        for a in range(tiles):
            high, low = split(abuf[pl.ds(a * NB * tiles + b, NB, stride=tiles), :].T)
            thi[pl.ds(at, NB), a * NB : (a + 1) * NB] = high
            tlo[pl.ds(at, NB), a * NB : (a + 1) * NB] = low
        return carry

    lax.fori_loop(0, tiles // 2, to_flipped, 0)

    row_wait(19, 0, 0, 3)
    sum_spread(0, 3, 9, over_cols, c)
    scatter_wait(1)
    gather_cols_start(xr.at[1], 13)
    gather_rows_mid(xc.at[0], 6)
    tile_wait(43, 3, 1, 1)
    tile_wait(44, 4, 1, 2)
    tile_wait(45, 5, 2, 2)
    row_start(46, 1, 3, 2)
    row_start(47, 2, 5, 1)
    scatter_wait(2)
    gather_rows_wait(xc.at[0], 6)

    both = halves(flat(xc.at[0]))

    def first_product(a, carry):
        at = pl.multiple_of(a * NB, NB)
        wpart_r[pl.ds(at, NB), :] = tile_product(ahi, alo, at, both)
        for i in range(per_tile):
            j = a * per_tile + i
            mine = wpart_r.at[pl.ds(j * ch, ch)]

            @pl.when(j != c)
            def _():
                send(mine, wslot_r.at[c], 20, (r, j))

        return carry

    lax.fori_loop(0, tiles, first_product, 0)
    wslot_r[c] = wpart_r[pl.ds(c * ch, ch), :]
    gather_cols_wait(xr.at[0], 8)
    all_start(0, dot3(xr[0], wpart_r[...], TN), 26, over_rows, r)
    gather_rows_start(xc.at[1], 11)
    sum_wait(0, 3, 9)
    g_ref[...] = ar_res[0, 0]
    cholesky_blocks(g_ref, r0_ref, 0, CHOL_BLOCKS)
    all_mid(0, 26, over_cols, c)
    gather_cols_wait(xr.at[1], 13)
    sum_start(1, [dot3(xr[0], xr[1], TN)], 14, over_rows, r)
    all_start(2, dot3(xr[2, pl.ds(c * ch, ch), :], xr[0, pl.ds(c * ch, ch), :], TN), 49, over_cols, c)
    y_ref[...] = ar_res[0, 0] + exact(ar_res[0, 1], r0_ref[...], TN)
    inverse_blocks(y_ref, t_ref, 0, INV_BLOCKS // 2)

    wait(20, wslot_r.at[pl.ds(0, n - 1)])
    total = wslot_r[0]
    for j in range(1, n):
        total = total + wslot_r[j]
    wr[0, pl.ds(c * ch, ch), :] = total
    gather_cols_start(wr.at[0], 23)
    wch[0] = total

    @pl.when(r != c)
    def _():
        send(wch.at[0], wc.at[0, c // 2, lax.rem(c, 2)], 22, (c, r))

    @pl.when(r == c)
    def _():
        wc[0, level, parity] = total

    all_late(0, 26, over_rows, r)
    sum_mid(1, 1, 14, over_rows, r)
    row_wait(46, 1, 3, 2)
    row_wait(47, 2, 5, 1)
    tiles_mine = (0, pl.ds(3, 3), pl.ds(c * pc, pc))
    over_cols(48, lambda j: ar_res.at[tiles_mine], lambda j: ar_res.at[tiles_mine])
    inverse_blocks(y_ref, t_ref, INV_BLOCKS // 2, INV_BLOCKS)
    lax.fori_loop(tiles // 2, tiles, to_flipped, 0)
    gather_rows_mid(xc.at[1], 11)
    all_mid(2, 49, over_rows, r)

    @pl.when(r != c)
    def _():
        wait_received(22, wc.at[0, level, parity])
        wait_sent(22, wch.at[0])

    gather_rows_start(wc.at[0], 24)
    wait(48, ar_res.at[0, pl.ds(3, 3), pl.ds(0, (n - 1) * pc)])
    sum_wait(1, 1, 14)
    r0 = r0_ref[...]
    z0 = y_ref[...]
    k0 = ar_res[1, 0]
    rz0 = exact(r0, z0)
    f01 = ar_res[0, 1] + r0
    f02 = ar_res[0, 2]
    x11 = ar_res[0, 3]
    x12 = ar_res[0, 4]
    x22 = ar_res[0, 5]
    known = known_part(r0, k0, x11)
    c01 = exact(k0, z0, TN) + exact(x11, rz0)
    all_wait(0, 26)
    b0 = core(z0, h_res[0] + known)
    c01 = c01 - exact(f01, b0)
    coef = jnp.concatenate([z0, rz0, -b0], axis=0)
    carried = exact(coef, f01, NT)
    last = carried[2 * NB :] + c01.T
    coef = jnp.concatenate(
        [coef, jnp.concatenate([carried[: 2 * NB], last], axis=0)], axis=1
    )

    def first_panel(f_ref, c_ref, x0, x1, index):
        f_ref[0] = x0

        @pl.when(index == 1)
        def _():
            f_ref[0, 0:NB, :] = f_ref[0, 0:NB, :] + r0

        out = dot3(jnp.concatenate([x1, f_ref[0]], axis=1), coef[NB:], NN)
        c_ref[0] = out[:, :NB]
        f_ref[1] = x1 - out[:, NB:]

    def first_panel_product(f_ref, c_ref, w, index):
        out = dot3(w, coef[:NB], NN)
        c_ref[0] = c_ref[0] + out[:, :NB]
        f_ref[1] = f_ref[1] - out[:, NB:]

        @pl.when(index == 0)
        def _():
            c_ref[0, 0:NB, :] = zero_tile

        @pl.when(index <= 1)
        def _():
            f_ref[1, 0:NB, :] = zero_tile

    first_panel(panel_r, cor_r, xr[0], xr[1], r)
    gather_cols_wait(wr.at[0], 23)
    first_panel_product(panel_r, cor_r, wr[0], r)

    p1r = panel_r[1]
    sum_start(2, [dot3(p1r, p1r, TN)], 30, over_rows, r)
    both = halves(p1r)

    def second_product(b, carry):
        at = pl.multiple_of(b * NB, NB)
        value = tile_product(thi, tlo, at, both).reshape(per_tile, ch, NB)
        for i in range(per_tile):
            j = b * per_tile + i
            wpart_c[j // 2, lax.rem(j, 2)] = value[i]
        return carry

    lax.fori_loop(0, tiles, second_product, 0)
    send(wpart_c.at[:, 1 - parity], wsib, 34, sibling)
    all_late(2, 49, over_cols, c)
    sum_mid(2, 1, 30, over_rows, r)
    wait(34, wsib)
    wsum[...] = wpart_c[:, parity] + wsib[...]

    def spread(k, carry):
        to = lax.rem(level + k, half)
        send(wsum.at[to], wslot_c.at[level], 35, (to * 2 + parity, c))
        return carry

    lax.fori_loop(1, half, spread, 0)
    wslot_c[level] = wsum[level]
    gather_rows_mid(wc.at[0], 24)
    all_start(3, dot3(xr[2, pl.ds(c * ch, ch), :], panel_r[1, pl.ds(c * ch, ch), :], TN), 52, over_cols, c)
    gather_rows_wait(xc.at[1], 11)
    first_panel(panel_c, cor_c, flat(xc.at[0]), flat(xc.at[1]), c)
    gather_rows_wait(wc.at[0], 24)
    first_panel_product(panel_c, cor_c, flat(wc.at[0]), c)
    p1c = panel_c[1]
    all_start(1, dot3(p1c, flat(wpart_c), TN), 36, over_cols, c)
    inner = dot3(p1c, jnp.concatenate([panel_c[0], cor_c[0]], axis=1), TN)
    sum_start(3, [inner[:, 0:NB], inner[:, NB:]], 32, over_cols, c)
    keep_left(0, cor_r[0], panel_r[0])
    keep_right(0, panel_c[0], cor_c[0])
    sum_wait(2, 1, 30)
    g_ref[...] = ar_res[2, 0]
    cholesky_blocks(g_ref, r1_ref, 0, CHOL_BLOCKS)
    all_mid(1, 36, over_rows, r)
    all_mid(3, 52, over_rows, r)
    sum_mid(3, 2, 32, over_cols, c)
    wait(35, wslot_c.at[pl.ds(0, half - 1)])
    total = wslot_c[0]
    for j in range(1, half):
        total = total + wslot_c[j]
    total = total + exact(xc[2, level, parity], r1_ref[...])
    wch[1] = total

    @pl.when(r != c)
    def _():
        send(wch.at[1], wr.at[1, pl.ds(r * ch, ch)], 41, (c, r))

    @pl.when(r == c)
    def _():
        wr[1, pl.ds(c * ch, ch), :] = total

    wc[1, level, parity] = total
    gather_rows_start(wc.at[1], 39)
    all_wait(2, 49)
    c02 = exact(h_res[2], z0) + exact(x12, rz0) - exact(f02, b0)
    top = x12 - exact(c02, f01, NT) - exact(f02, c01, NT)
    y_ref[...] = ar_res[2, 0] + exact(top, r1_ref[...], TN)
    inverse_blocks(y_ref, t_ref, 0, INV_BLOCKS // 2)

    @pl.when(r != c)
    def _():
        wait_received(41, wr.at[1, pl.ds(c * ch, ch)])
        wait_sent(41, wch.at[1])

    all_late(1, 36, over_cols, c)
    all_late(3, 52, over_cols, c)
    gather_cols_start(wr.at[1], 42)
    inverse_blocks(y_ref, t_ref, INV_BLOCKS // 2, INV_BLOCKS)
    gather_rows_mid(wc.at[1], 39)
    r1 = r1_ref[...]
    z1 = y_ref[...]
    rz1 = exact(r1, z1)
    sum_wait(3, 2, 32)
    all_wait(3, 52)
    j1t = ar_res[3, 0]
    j2t = ar_res[3, 1]
    cross = exact(j2t, j1t, NT)
    cf = exact(c02, f02, NT)
    k1 = h_res[3].T - exact(j2t, f02, NT) - exact(j1t, c02, NT)
    known = known_part(r1, k1, x22 - cf - cf.T) - cross - cross.T
    fold1 = -exact(j1t, z1, TN) - exact(f02, rz1, TN)
    fold2 = -exact(j2t, z1, TN) - exact(c02, rz1, TN)
    apply_first()
    write_band(0, r0_ref)
    write_band(1, r1_ref)
    pltpu.make_async_copy(abuf, a_out, asem).start()
    all_wait(1, 36)
    b1 = core(z1, h_res[1] + known)
    coef = jnp.concatenate([z1, fold1, fold2, -b1], axis=0)

    def second_panel(f_ref, c_ref, index):
        @pl.when(index == 2)
        def _():
            f_ref[1, 0:NB, :] = f_ref[1, 0:NB, :] + r1

        c_ref[1] = dot3(
            jnp.concatenate([c_ref[0], f_ref[0], f_ref[1]], axis=1), coef[NB:], NN
        )

    def second_panel_product(c_ref, w, index):
        c_ref[1] = c_ref[1] + dot3(w, coef[:NB], NN)

        @pl.when(index <= 1)
        def _():
            c_ref[1, 0:NB, :] = zero_tile

    second_panel(panel_r, cor_r, r)
    second_panel(panel_c, cor_c, c)
    gather_rows_wait(wc.at[1], 39)
    second_panel_product(cor_c, flat(wc.at[1]), c)
    keep_right(1, panel_c[1], cor_c[1])
    pltpu.make_async_copy(qh.at[1], qh_out, osem).start()
    pltpu.make_async_copy(ql.at[1], ql_out, osem2).start()
    gather_cols_wait(wr.at[1], 42)
    second_panel_product(cor_r, wr[1], r)
    keep_left(1, cor_r[1], panel_r[1])
    last_high = pltpu.make_async_copy(lh.at[1], lh_out, osem3)
    last_low = pltpu.make_async_copy(ll.at[1], ll_out, osem4)
    last_high.start()
    last_low.start()
    pltpu.make_async_copy(abuf, a_out, asem).wait()
    pltpu.make_async_copy(qh.at[1], qh_out, osem).wait()
    pltpu.make_async_copy(ql.at[1], ql_out, osem2).wait()
    last_high.wait()
    last_low.wait()


def update_kernel(tiles, a_ref, lh, ll, qh, ql, o_ref):
    high = lh[...]
    low = ll[...]
    for b in range(0, tiles, 2):
        cols = slice(b * NB, (b + 2) * NB)
        change = mxu(high, qh[:, cols], NN) + (
            mxu(high, ql[:, cols], NN) + mxu(low, qh[:, cols], NN)
        )
        for k in range(high.shape[0] // NB):
            for j in range(2):
                spot = pl.ds(k * NB * tiles + b + j, NB, stride=tiles)
                part = change[k * NB : (k + 1) * NB, j * NB : (j + 1) * NB]
                o_ref[spot, :] = a_ref[spot, :] - part


def local(hamiltonian):
    tiles = hamiltonian.shape[0]
    n = lax.axis_size("row")
    rows = tiles * NB
    ch = rows // n
    pc = NB // n
    half = n // 2
    f32 = jnp.float32
    bf16 = jnp.bfloat16
    block = hamiltonian.reshape(rows * tiles, NB)
    shapes = [
        ((rows * tiles, NB), f32),
        ((rows, rows), bf16),
        ((rows, rows), bf16),
        ((rows, rows), bf16),
        ((rows, rows), bf16),
        ((rows, NB), f32),
        ((rows, NB), f32),
        ((3, rows, NB), f32),
        ((3, half, 2, ch, NB), f32),
        ((rows, NB), f32),
        ((n, ch, NB), f32),
        ((half, 2, ch, NB), f32),
        ((half, ch, NB), f32),
        ((half, ch, NB), f32),
        ((half, ch, NB), f32),
        ((2, ch, NB), f32),
        ((2, rows, NB), f32),
        ((2, half, 2, ch, NB), f32),
        ((2, rows, NB), f32),
        ((2, rows, NB), f32),
        ((2, rows, NB), f32),
        ((2, rows, NB), f32),
        ((2, rows, 2 * NB), bf16),
        ((2, rows, 2 * NB), bf16),
        ((2, 2 * NB, rows), bf16),
        ((2, 2 * NB, rows), bf16),
        ((4, 3, NB, NB), f32),
        ((4, n, 3, pc, NB), f32),
        ((4, 6, NB, NB), f32),
        ((4, NB, NB), f32),
        ((4, n, pc, NB), f32),
        ((4, pc, NB), f32),
        ((4, n, pc, NB), f32),
        ((4, NB, NB), f32),
    ] + [((NB, NB), f32)] * 5
    anywhere = pl.BlockSpec(memory_space=pl.ANY)
    left = jax.ShapeDtypeStruct((rows, 2 * NB), bf16)
    right = jax.ShapeDtypeStruct((2 * NB, rows), bf16)
    parts = pl.pallas_call(
        functools.partial(reduce_kernel, n, tiles),
        out_shape=[jax.ShapeDtypeStruct((rows * tiles, NB), f32), left, left, right, right],
        in_specs=[anywhere],
        out_specs=[anywhere] * 5,
        scratch_shapes=[pltpu.VMEM(*shape) for shape in shapes]
        + [pltpu.SemaphoreType.DMA] * 5
        + [pltpu.SemaphoreType.DMA((55,))] * 2,
        compiler_params=pltpu.CompilerParams(
            collective_id=0, has_side_effects=True, vmem_limit_bytes=VMEM_LIMIT
        ),
        name="reduce_panels",
    )(block)
    step = min(rows, 2 * NB)
    block_spec = pl.BlockSpec((step * tiles, NB), lambda i: (i, 0))
    left_spec = pl.BlockSpec((step, 2 * NB), lambda i: (i, 0))
    right_spec = pl.BlockSpec((2 * NB, rows), lambda i: (0, 0))
    result = pl.pallas_call(
        functools.partial(update_kernel, tiles),
        out_shape=jax.ShapeDtypeStruct((rows * tiles, NB), f32),
        grid=(rows // step,),
        in_specs=[block_spec, left_spec, left_spec, right_spec, right_spec],
        out_specs=block_spec,
        compiler_params=pltpu.CompilerParams(vmem_limit_bytes=VMEM_LIMIT),
        name="update_matrix",
    )(*parts)
    return result.reshape(hamiltonian.shape)


def solution(mesh):
    spec = P(None, "row", None, None, "col", None)
    return jax.shard_map(local, mesh=mesh, in_specs=(spec,), out_specs=spec, check_vma=False)
```

```python
import functools

import jax
import jax.numpy as jnp
from jax import lax
from jax.experimental import pallas as pl
from jax.experimental.pallas import tpu as pltpu
from jax.sharding import PartitionSpec as P

MESH = pl.DeviceIdType.MESH
NB = 128
NN = (((1,), (0,)), ((), ()))
NT = (((1,), (1,)), ((), ()))
TN = (((0,), (0,)), ((), ()))
TT = (((0,), (1,)), ((), ()))
VMEM_LIMIT = 56 << 20
CHOL_WIDTH = 32
INV_WIDTH = 16
CHOL_BLOCKS = NB // CHOL_WIDTH
INV_BLOCKS = NB // INV_WIDTH


def split(value):
    high = value.astype(jnp.bfloat16)
    low = (value - high.astype(jnp.float32)).astype(jnp.bfloat16)
    return high, low


def mxu(first, second, dims):
    return lax.dot_general(first, second, dims, preferred_element_type=jnp.float32)


def dot3(first, second, dims):
    fh, fl = split(first)
    sh, sl = split(second)
    return mxu(fh, sh, dims) + (mxu(fh, sl, dims) + mxu(fl, sh, dims))


def exact(first, second, dims=NN):
    return lax.dot_general(
        first, second, dims, precision=lax.Precision.HIGHEST, preferred_element_type=jnp.float32
    )


def iota(axis, shape):
    return lax.broadcasted_iota(jnp.int32, shape, axis)


def leading_columns(x, base, width):
    rolled = pltpu.roll(x, lax.rem(NB - base, NB), 1)
    return [jnp.broadcast_to(rolled[:, i : i + 1], (width, NB)) for i in range(width)]


def cholesky_blocks(g_ref, r_ref, first, last):
    width = CHOL_WIDTH
    sub = iota(0, (width, NB))
    lane = iota(1, (width, NB))

    def block(k, carry):
        base = pl.multiple_of(k * width, width)
        x = g_ref[pl.ds(base, width), :]
        cols = leading_columns(x, base, width)
        for i in range(width):
            scale = lax.rsqrt(cols[i][i : i + 1, :])
            column = cols[i] * scale
            below = jnp.where(sub > i, column, 0.0)
            row = x[i : i + 1, :] * scale
            x = jnp.where(sub == i, row, x - below * row)
            for m in range(i + 1, width):
                cols[m] = cols[m] - below * column[m : m + 1, :]
        x = jnp.where(lane >= base + sub, x, 0.0)
        r_ref[pl.ds(base, width), :] = x
        g_ref[...] -= exact(x, x, TN)
        return carry

    lax.fori_loop(first, last, block, 0)


def inverse_blocks(y_ref, t_ref, first, last):
    width = INV_WIDTH
    sub = iota(0, (width, NB))
    lane = iota(1, (width, NB))
    wide = iota(1, (NB, NB))

    def block(k, carry):
        base = pl.multiple_of(k * width, width)
        x = y_ref[pl.ds(base, width), :]
        cols = leading_columns(x, base, width)
        inside = (lane >= base) & (lane < base + width)
        x = jnp.where(inside, jnp.where(lane - base == sub, 1.0, 0.0), x)
        for i in range(width):
            scale = 1.0 / cols[i][i : i + 1, :]
            factor = jnp.where(sub == i, 0.0, cols[i])
            row = x[i : i + 1, :] * scale
            x = jnp.where(sub == i, row, x - factor * row)
            for m in range(i + 1, width):
                entry = cols[m][i : i + 1, :] * scale
                cols[m] = jnp.where(sub == i, entry, cols[m] - factor * entry)
        t_ref[pl.ds(base, width), :] = x
        y = y_ref[...]
        chosen = (wide >= base) & (wide < base + width)
        y_ref[...] = jnp.where(chosen, 0.0, y) - exact(jnp.where(chosen, y, 0.0), t_ref[...])
        y_ref[pl.ds(base, width), :] = x
        t_ref[pl.ds(base, width), :] = jnp.zeros((width, NB), jnp.float32)
        return carry

    lax.fori_loop(first, last, block, 0)


def reduce_kernel(n, tiles, *refs):
    rows = tiles * NB
    ch = rows // n
    pc = NB // n
    half = n // 2
    per_tile = NB // ch
    (
        a_hbm, a_out, lh_out, ll_out, qh_out, ql_out,
        abuf, ahi, alo, thi, tlo, stg_r, stg_c, xr, xc,
        wpart_r, wslot_r, wpart_c, wsib, wsum, wslot_c, wch, wr, wc,
        panel_r, panel_c, cor_r, cor_c, lh, ll, qh, ql,
        ar_src, ar_slot, ar_res, h_src, h_slot, h_piece, h_ex, h_res,
        g_ref, y_ref, t_ref, r0_ref, r1_ref, asem, osem, osem2, osem3, osem4, ss, rs,
    ) = refs
    r = lax.axis_index("row")
    c = lax.axis_index("col")
    parity = lax.rem(r, 2)
    level = r // 2
    sibling = (r + 1 - 2 * parity, c)

    load = pltpu.make_async_copy(a_hbm, abuf, asem)
    load.start()
    barrier = pltpu.get_barrier_semaphore()

    def greet(k, carry):
        pl.semaphore_signal(barrier, inc=1, device_id=(lax.rem(r + k, n), c), device_id_type=MESH)
        pl.semaphore_signal(barrier, inc=1, device_id=(r, lax.rem(c + k, n)), device_id_type=MESH)
        return carry

    lax.fori_loop(1, n, greet, 0)

    @pl.when(r != c)
    def _():
        pl.semaphore_signal(barrier, inc=1, device_id=(c, r), device_id_type=MESH)

    def send(src, dst, sem, device):
        pltpu.make_async_remote_copy(
            src, dst, ss.at[sem], rs.at[sem], device_id=device, device_id_type=MESH
        ).start()

    def over_cols(sem, src_of, dst_of):
        def one(k, carry):
            j = lax.rem(c + k, n)
            send(src_of(j), dst_of(j), sem, (r, j))
            return carry

        lax.fori_loop(1, n, one, 0)

    def over_rows(sem, src_of, dst_of):
        def one(k, carry):
            j = lax.rem(r + k, n)
            send(src_of(j), dst_of(j), sem, (j, c))
            return carry

        lax.fori_loop(1, n, one, 0)

    def wait_sent(sem, sent):
        pltpu.make_async_copy(sent, sent, ss.at[sem]).wait()

    def wait_received(sem, received):
        pltpu.make_async_copy(received, received, rs.at[sem]).wait()

    def wait(sem, part):
        wait_received(sem, part)
        wait_sent(sem, part)

    def scatter(t):
        @pl.when(c == t)
        def _():
            over_cols(
                t,
                lambda j: stg_r.at[pl.ds(j * ch, ch)],
                lambda j: xr.at[t, pl.ds(j * ch, ch)],
            )
            xr[t, pl.ds(t * ch, ch), :] = stg_r[pl.ds(t * ch, ch), :]

        @pl.when(r == t)
        def _():
            over_rows(
                3 + t,
                lambda j: stg_c.at[pl.ds(j * ch, ch)],
                lambda j: xc.at[t, j // 2, lax.rem(j, 2)],
            )
            xc[t, t // 2, t % 2] = stg_c[pl.ds(t * ch, ch), :]

    def scatter_wait(t):
        @pl.when(c == t)
        def _():
            wait_sent(t, stg_r.at[pl.ds(0, (n - 1) * ch)])

        @pl.when(c != t)
        def _():
            wait_received(t, xr.at[t, pl.ds(c * ch, ch)])

        @pl.when(r == t)
        def _():
            wait_sent(3 + t, stg_c.at[pl.ds(0, (n - 1) * ch)])

        @pl.when(r != t)
        def _():
            wait_received(3 + t, xc.at[t, level, parity])

    def gather_cols_start(buf, sem):
        mine = buf.at[pl.ds(c * ch, ch)]
        over_cols(sem, lambda j: mine, lambda j: mine)

    def gather_cols_wait(buf, sem):
        wait(sem, buf.at[pl.ds(0, (n - 1) * ch)])

    def gather_rows_start(buf, sem):
        mine = buf.at[level, parity]

        def one(k, carry):
            send(mine, mine, sem, (lax.rem(level + k, half) * 2 + parity, c))
            return carry

        lax.fori_loop(1, half, one, 0)

    def gather_rows_mid(buf, sem):
        wait(sem, buf.at[pl.ds(0, half - 1), 0])
        mine = buf.at[:, parity]
        send(mine, mine, sem + 1, sibling)

    def gather_rows_wait(buf, sem):
        wait(sem + 1, buf.at[:, 0])

    def sum_start(q, parts, sem, over, me):
        count = len(parts)
        for i, part in enumerate(parts):
            ar_src[q, i] = part
        over(
            sem,
            lambda j: ar_src.at[q, pl.ds(0, count), pl.ds(j * pc, pc)],
            lambda j: ar_slot.at[q, me, pl.ds(0, count)],
        )
        ar_slot[q, me, 0:count] = ar_src[q, 0:count, pl.ds(me * pc, pc), :]

    def sum_slots(q, count, sem):
        wait(sem, ar_slot.at[q, pl.ds(0, n - 1), pl.ds(0, count)])
        total = ar_slot[q, 0, 0:count]
        for j in range(1, n):
            total = total + ar_slot[q, j, 0:count]
        return total

    def sum_spread(q, count, sem, over, me):
        mine = (q, pl.ds(0, count), pl.ds(me * pc, pc))
        over(sem + 1, lambda j: ar_res.at[mine], lambda j: ar_res.at[mine])

    def sum_mid(q, count, sem, over, me):
        ar_res[q, 0:count, pl.ds(me * pc, pc), :] = sum_slots(q, count, sem)
        sum_spread(q, count, sem, over, me)

    def sum_wait(q, count, sem):
        wait(sem + 1, ar_res.at[q, pl.ds(0, count), pl.ds(0, (n - 1) * pc)])

    def all_start(p, part, sem, over, me):
        h_src[p] = part
        over(sem, lambda j: h_src.at[p, pl.ds(j * pc, pc)], lambda j: h_slot.at[p, me])
        h_slot[p, me] = h_src[p, pl.ds(me * pc, pc), :]

    def all_mid(p, sem, over, me):
        wait(sem, h_slot.at[p, pl.ds(0, n - 1)])
        total = h_slot[p, 0]
        for j in range(1, n):
            total = total + h_slot[p, j]
        h_piece[p] = total
        over(sem + 1, lambda j: h_piece.at[p], lambda j: h_ex.at[p, me])
        h_ex[p, me] = total

    def all_late(p, sem, over, me):
        wait(sem + 1, h_ex.at[p, pl.ds(0, n - 1)])
        total = h_ex[p, 0]
        for j in range(1, n):
            total = total + h_ex[p, j]
        h_res[p, pl.ds(me * pc, pc), :] = total
        mine = h_res.at[p, pl.ds(me * pc, pc)]
        over(sem + 2, lambda j: mine, lambda j: mine)

    def all_wait(p, sem):
        wait(sem + 2, h_res.at[p, pl.ds(0, (n - 1) * pc)])

    def tile_product(high_ref, low_ref, at, both):
        wide = mxu(high_ref[pl.ds(at, NB), :], both, NN)
        return wide[:, :NB] + (wide[:, NB:] + mxu(low_ref[pl.ds(at, NB), :], both[:, :NB], NN))

    def halves(panel):
        return jnp.concatenate(split(panel), axis=1)

    def flat(ref):
        return ref[...].reshape(rows, NB)

    def flip(value):
        return jnp.concatenate(
            [value[i * NB : (i + 1) * NB].T for i in range(tiles)], axis=1
        )

    def known_part(r_mat, k, corner):
        kr = exact(k, r_mat)
        return kr + kr.T + exact(exact(r_mat, corner, TN), r_mat)

    def core(z, inner_sum):
        return 0.5 * exact(exact(z, inner_sum, TN), z)

    zero_tile = jnp.zeros((NB, NB), jnp.float32)
    block_rows = min(rows, 2 * NB)

    def keep_left(p, first, second):
        for i, value in enumerate((first, second)):
            spot = slice(i * NB, (i + 1) * NB)
            lh[p, :, spot], ll[p, :, spot] = split(value)

    def keep_right(p, first, second):
        for i, value in enumerate((first, second)):
            spot = slice(i * NB, (i + 1) * NB)
            qh[p, spot, :], ql[p, spot, :] = split(flip(value))

    def apply_first():
        def one(i, carry):
            at = pl.multiple_of(i * block_rows, block_rows)
            high = lh[0, pl.ds(at, block_rows)]
            low = ll[0, pl.ds(at, block_rows)]
            for b in range(0, tiles, 2):
                cols = slice(b * NB, (b + 2) * NB)
                change = mxu(high, qh[0, :, cols], NN) + (
                    mxu(high, ql[0, :, cols], NN) + mxu(low, qh[0, :, cols], NN)
                )
                for k in range(block_rows // NB):
                    for j in range(2):
                        spot = pl.ds((at + k * NB) * tiles + b + j, NB, stride=tiles)
                        part = change[k * NB : (k + 1) * NB, j * NB : (j + 1) * NB]
                        abuf[spot, :] = abuf[spot, :] - part
            return carry

        lax.fori_loop(0, rows // block_rows, one, 0)

    def write_band(p, r_ref):
        @pl.when(c == p)
        def _():
            for a in range(tiles):
                spot = pl.ds(a * NB * tiles, NB, stride=tiles)

                @pl.when(a * n + r == p + 1)
                def _():
                    abuf[spot, :] = -r_ref[...]

                @pl.when(a * n + r > p + 1)
                def _():
                    abuf[spot, :] = zero_tile

        @pl.when(r == p)
        def _():
            for b in range(tiles):
                spot = pl.ds(b, NB, stride=tiles)

                @pl.when(b * n + c == p + 1)
                def _():
                    abuf[spot, :] = -r_ref[...].T

                @pl.when(b * n + c > p + 1)
                def _():
                    abuf[spot, :] = zero_tile

    load.wait()
    for t in range(3):

        @pl.when(c == t)
        def _():
            for a in range(tiles):
                stg_r[a * NB : (a + 1) * NB, :] = abuf[pl.ds(a * NB * tiles, NB, stride=tiles), :]

            @pl.when(r == 0)
            def _():
                stg_r[0:NB, :] = zero_tile

        @pl.when(r == t)
        def _():
            for b in range(tiles):
                stg_c[b * NB : (b + 1) * NB, :] = abuf[pl.ds(b, NB, stride=tiles), :].T

            @pl.when(c == 0)
            def _():
                stg_c[0:NB, :] = zero_tile

    pl.semaphore_wait(barrier, 2 * (n - 1) + jnp.where(r != c, 1, 0))
    scatter(0)

    def tile_start(sem, index, t, owner):
        @pl.when((r == t) & (c == owner))
        def _():
            over_cols(
                sem,
                lambda j: stg_c.at[pl.ds(j * pc, pc)],
                lambda j: ar_res.at[0, index, pl.ds(j * pc, pc)],
            )
            ar_res[0, index, pl.ds(c * pc, pc), :] = stg_c[pl.ds(c * pc, pc), :]

    def tile_wait(sem, index, t, owner):
        @pl.when((r == t) & (c == owner))
        def _():
            wait_sent(sem, stg_c.at[pl.ds(0, (n - 1) * pc)])

        @pl.when((r == t) & (c != owner))
        def _():
            wait_received(sem, ar_res.at[0, index, pl.ds(c * pc, pc)])

    def row_start(sem, t, first, count):
        mine = (0, pl.ds(first, count), pl.ds(c * pc, pc))

        @pl.when(r == t)
        def _():
            over_rows(sem, lambda j: ar_res.at[mine], lambda j: ar_res.at[mine])

    def row_wait(sem, t, first, count):
        @pl.when(r == t)
        def _():
            wait_sent(sem, ar_res.at[0, pl.ds(first, count), pl.ds(0, (n - 1) * pc)])

        @pl.when(r != t)
        def _():
            wait_received(sem, ar_res.at[0, pl.ds(first, count), pl.ds(c * pc, pc)])

    @pl.when(r == 0)
    def _():
        mine = stg_c[...]
        first = jnp.where(c == 1, mine[0:NB], 0.0)
        second = jnp.where(c == 2, mine[0:NB], 0.0)
        sum_start(0, [dot3(mine, mine, TN), first, second], 9, over_cols, c)

    t_ref[...] = zero_tile

    @pl.when(r == 0)
    def _():
        ar_res[0, 0:3, pl.ds(c * pc, pc), :] = sum_slots(0, 3, 9)

    row_start(19, 0, 0, 3)
    scatter_wait(0)
    gather_rows_start(xc.at[0], 6)
    gather_cols_start(xr.at[0], 8)
    scatter(1)
    tile_start(43, 3, 1, 1)
    tile_start(44, 4, 1, 2)
    scatter(2)
    tile_start(45, 5, 2, 2)

    def to_parts(a, carry):
        at = pl.multiple_of(a * NB, NB)
        for b in range(tiles):
            high, low = split(abuf[pl.ds(a * NB * tiles + b, NB, stride=tiles), :])
            ahi[pl.ds(at, NB), b * NB : (b + 1) * NB] = high
            alo[pl.ds(at, NB), b * NB : (b + 1) * NB] = low
        return carry

    lax.fori_loop(0, tiles, to_parts, 0)

    def to_flipped(b, carry):
        at = pl.multiple_of(b * NB, NB)
        for a in range(tiles):
            high, low = split(abuf[pl.ds(a * NB * tiles + b, NB, stride=tiles), :].T)
            thi[pl.ds(at, NB), a * NB : (a + 1) * NB] = high
            tlo[pl.ds(at, NB), a * NB : (a + 1) * NB] = low
        return carry

    lax.fori_loop(0, tiles // 2, to_flipped, 0)

    row_wait(19, 0, 0, 3)
    sum_spread(0, 3, 9, over_cols, c)
    scatter_wait(1)
    gather_cols_start(xr.at[1], 13)
    gather_rows_mid(xc.at[0], 6)
    tile_wait(43, 3, 1, 1)
    tile_wait(44, 4, 1, 2)
    tile_wait(45, 5, 2, 2)
    row_start(46, 1, 3, 2)
    row_start(47, 2, 5, 1)
    scatter_wait(2)
    gather_rows_wait(xc.at[0], 6)

    both = halves(flat(xc.at[0]))

    def first_product(a, carry):
        at = pl.multiple_of(a * NB, NB)
        wpart_r[pl.ds(at, NB), :] = tile_product(ahi, alo, at, both)
        for i in range(per_tile):
            j = a * per_tile + i
            mine = wpart_r.at[pl.ds(j * ch, ch)]

            @pl.when(j != c)
            def _():
                send(mine, wslot_r.at[c], 20, (r, j))

        return carry

    lax.fori_loop(0, tiles, first_product, 0)
    wslot_r[c] = wpart_r[pl.ds(c * ch, ch), :]
    gather_cols_wait(xr.at[0], 8)
    all_start(0, dot3(xr[0], wpart_r[...], TN), 26, over_rows, r)
    gather_rows_start(xc.at[1], 11)
    sum_wait(0, 3, 9)
    g_ref[...] = ar_res[0, 0]
    cholesky_blocks(g_ref, r0_ref, 0, CHOL_BLOCKS)
    all_mid(0, 26, over_cols, c)
    gather_cols_wait(xr.at[1], 13)
    sum_start(1, [dot3(xr[0], xr[1], TN)], 14, over_rows, r)
    all_start(2, dot3(xr[2, pl.ds(c * ch, ch), :], xr[0, pl.ds(c * ch, ch), :], TN), 49, over_cols, c)
    y_ref[...] = ar_res[0, 0] + exact(ar_res[0, 1], r0_ref[...], TN)
    inverse_blocks(y_ref, t_ref, 0, INV_BLOCKS // 2)

    wait(20, wslot_r.at[pl.ds(0, n - 1)])
    total = wslot_r[0]
    for j in range(1, n):
        total = total + wslot_r[j]
    wr[0, pl.ds(c * ch, ch), :] = total
    gather_cols_start(wr.at[0], 23)
    wch[0] = total

    @pl.when(r != c)
    def _():
        send(wch.at[0], wc.at[0, c // 2, lax.rem(c, 2)], 22, (c, r))

    @pl.when(r == c)
    def _():
        wc[0, level, parity] = total

    all_late(0, 26, over_rows, r)
    sum_mid(1, 1, 14, over_rows, r)
    row_wait(46, 1, 3, 2)
    row_wait(47, 2, 5, 1)
    tiles_mine = (0, pl.ds(3, 3), pl.ds(c * pc, pc))
    over_cols(48, lambda j: ar_res.at[tiles_mine], lambda j: ar_res.at[tiles_mine])
    inverse_blocks(y_ref, t_ref, INV_BLOCKS // 2, INV_BLOCKS)
    lax.fori_loop(tiles // 2, tiles, to_flipped, 0)
    gather_rows_mid(xc.at[1], 11)
    all_mid(2, 49, over_rows, r)

    wait(48, ar_res.at[0, pl.ds(3, 3), pl.ds(0, (n - 1) * pc)])
    sum_wait(1, 1, 14)
    r0 = r0_ref[...]
    z0 = y_ref[...]
    k0 = ar_res[1, 0]
    rz0 = exact(r0, z0)
    f01 = ar_res[0, 1] + r0
    f02 = ar_res[0, 2]
    x11 = ar_res[0, 3]
    x12 = ar_res[0, 4]
    x22 = ar_res[0, 5]
    known = known_part(r0, k0, x11)
    c01 = exact(k0, z0, TN) + exact(x11, rz0)
    all_wait(0, 26)
    b0 = core(z0, h_res[0] + known)
    c01 = c01 - exact(f01, b0)
    coef = jnp.concatenate([z0, rz0, -b0], axis=0)
    carried = exact(coef, f01, NT)
    last = carried[2 * NB :] + c01.T
    coef = jnp.concatenate(
        [coef, jnp.concatenate([carried[: 2 * NB], last], axis=0)], axis=1
    )

    def first_panel(f_ref, c_ref, x0, x1, index):
        f_ref[0] = x0

        @pl.when(index == 1)
        def _():
            f_ref[0, 0:NB, :] = f_ref[0, 0:NB, :] + r0

        out = dot3(jnp.concatenate([x1, f_ref[0]], axis=1), coef[NB:], NN)
        c_ref[0] = out[:, :NB]
        f_ref[1] = x1 - out[:, NB:]

    def first_panel_product(f_ref, c_ref, w, index):
        out = dot3(w, coef[:NB], NN)
        c_ref[0] = c_ref[0] + out[:, :NB]
        f_ref[1] = f_ref[1] - out[:, NB:]

        @pl.when(index == 0)
        def _():
            c_ref[0, 0:NB, :] = zero_tile

        @pl.when(index <= 1)
        def _():
            f_ref[1, 0:NB, :] = zero_tile

    all_late(2, 49, over_cols, c)
    first_panel(panel_r, cor_r, xr[0], xr[1], r)
    gather_cols_wait(wr.at[0], 23)
    first_panel_product(panel_r, cor_r, wr[0], r)

    p1r = panel_r[1]
    sum_start(2, [dot3(p1r, p1r, TN)], 30, over_rows, r)

    @pl.when(r != c)
    def _():
        wait_received(22, wc.at[0, level, parity])
        wait_sent(22, wch.at[0])

    gather_rows_start(wc.at[0], 24)
    both = halves(p1r)

    def second_product(b, carry):
        at = pl.multiple_of(b * NB, NB)
        value = tile_product(thi, tlo, at, both).reshape(per_tile, ch, NB)
        for i in range(per_tile):
            j = b * per_tile + i
            wpart_c[j // 2, lax.rem(j, 2)] = value[i]
        return carry

    lax.fori_loop(0, tiles, second_product, 0)
    send(wpart_c.at[:, 1 - parity], wsib, 34, sibling)
    sum_mid(2, 1, 30, over_rows, r)
    wait(34, wsib)
    wsum[...] = wpart_c[:, parity] + wsib[...]

    def spread(k, carry):
        to = lax.rem(level + k, half)
        send(wsum.at[to], wslot_c.at[level], 35, (to * 2 + parity, c))
        return carry

    lax.fori_loop(1, half, spread, 0)
    wslot_c[level] = wsum[level]
    all_wait(2, 49)
    c02 = exact(h_res[2], z0) + exact(x12, rz0) - exact(f02, b0)
    top = x12 - exact(c02, f01, NT) - exact(f02, c01, NT)
    cf = exact(c02, f02, NT)
    keep_left(0, cor_r[0], panel_r[0])
    gather_rows_mid(wc.at[0], 24)
    all_start(3, dot3(xr[2, pl.ds(c * ch, ch), :], panel_r[1, pl.ds(c * ch, ch), :], TN), 52, over_cols, c)
    gather_rows_wait(xc.at[1], 11)
    first_panel(panel_c, cor_c, flat(xc.at[0]), flat(xc.at[1]), c)
    gather_rows_wait(wc.at[0], 24)
    first_panel_product(panel_c, cor_c, flat(wc.at[0]), c)
    p1c = panel_c[1]
    all_start(1, dot3(p1c, flat(wpart_c), TN), 36, over_cols, c)
    inner = dot3(p1c, jnp.concatenate([panel_c[0], cor_c[0]], axis=1), TN)
    sum_start(3, [inner[:, 0:NB], inner[:, NB:]], 32, over_cols, c)
    sum_wait(2, 1, 30)
    g_ref[...] = ar_res[2, 0]
    cholesky_blocks(g_ref, r1_ref, 0, CHOL_BLOCKS)
    all_mid(1, 36, over_rows, r)
    all_mid(3, 52, over_rows, r)
    sum_mid(3, 2, 32, over_cols, c)
    wait(35, wslot_c.at[pl.ds(0, half - 1)])
    total = wslot_c[0]
    for j in range(1, half):
        total = total + wslot_c[j]
    total = total + exact(xc[2, level, parity], r1_ref[...])
    wch[1] = total

    @pl.when(r != c)
    def _():
        send(wch.at[1], wr.at[1, pl.ds(r * ch, ch)], 41, (c, r))

    @pl.when(r == c)
    def _():
        wr[1, pl.ds(c * ch, ch), :] = total

    wc[1, level, parity] = total
    gather_rows_start(wc.at[1], 39)
    y_ref[...] = ar_res[2, 0] + exact(top, r1_ref[...], TN)
    inverse_blocks(y_ref, t_ref, 0, INV_BLOCKS // 2)

    @pl.when(r != c)
    def _():
        wait_received(41, wr.at[1, pl.ds(c * ch, ch)])
        wait_sent(41, wch.at[1])

    all_late(1, 36, over_cols, c)
    all_late(3, 52, over_cols, c)
    gather_cols_start(wr.at[1], 42)
    inverse_blocks(y_ref, t_ref, INV_BLOCKS // 2, INV_BLOCKS)
    gather_rows_mid(wc.at[1], 39)
    r1 = r1_ref[...]
    z1 = y_ref[...]
    rz1 = exact(r1, z1)
    sum_wait(3, 2, 32)
    all_wait(3, 52)
    j1t = ar_res[3, 0]
    j2t = ar_res[3, 1]
    cross = exact(j2t, j1t, NT)
    k1 = h_res[3].T - exact(j2t, f02, NT) - exact(j1t, c02, NT)
    known = known_part(r1, k1, x22 - cf - cf.T) - cross - cross.T
    fold1 = -exact(j1t, z1, TN) - exact(f02, rz1, TN)
    fold2 = -exact(j2t, z1, TN) - exact(c02, rz1, TN)
    keep_right(0, panel_c[0], cor_c[0])
    apply_first()
    write_band(0, r0_ref)
    write_band(1, r1_ref)
    pltpu.make_async_copy(abuf, a_out, asem).start()
    all_wait(1, 36)
    b1 = core(z1, h_res[1] + known)
    coef = jnp.concatenate([z1, fold1, fold2, -b1], axis=0)

    def second_panel(f_ref, c_ref, index):
        @pl.when(index == 2)
        def _():
            f_ref[1, 0:NB, :] = f_ref[1, 0:NB, :] + r1

        c_ref[1] = dot3(
            jnp.concatenate([c_ref[0], f_ref[0], f_ref[1]], axis=1), coef[NB:], NN
        )

    def second_panel_product(c_ref, w, index):
        c_ref[1] = c_ref[1] + dot3(w, coef[:NB], NN)

        @pl.when(index <= 1)
        def _():
            c_ref[1, 0:NB, :] = zero_tile

    second_panel(panel_r, cor_r, r)
    second_panel(panel_c, cor_c, c)
    gather_rows_wait(wc.at[1], 39)
    second_panel_product(cor_c, flat(wc.at[1]), c)
    keep_right(1, panel_c[1], cor_c[1])
    pltpu.make_async_copy(qh.at[1], qh_out, osem).start()
    pltpu.make_async_copy(ql.at[1], ql_out, osem2).start()
    gather_cols_wait(wr.at[1], 42)
    second_panel_product(cor_r, wr[1], r)
    keep_left(1, cor_r[1], panel_r[1])
    last_high = pltpu.make_async_copy(lh.at[1], lh_out, osem3)
    last_low = pltpu.make_async_copy(ll.at[1], ll_out, osem4)
    last_high.start()
    last_low.start()
    pltpu.make_async_copy(abuf, a_out, asem).wait()
    pltpu.make_async_copy(qh.at[1], qh_out, osem).wait()
    pltpu.make_async_copy(ql.at[1], ql_out, osem2).wait()
    last_high.wait()
    last_low.wait()


def update_kernel(tiles, a_ref, lh, ll, qh, ql, o_ref):
    high = lh[...]
    low = ll[...]
    for b in range(0, tiles, 2):
        cols = slice(b * NB, (b + 2) * NB)
        change = mxu(high, qh[:, cols], NN) + (
            mxu(high, ql[:, cols], NN) + mxu(low, qh[:, cols], NN)
        )
        for k in range(high.shape[0] // NB):
            for j in range(2):
                spot = pl.ds(k * NB * tiles + b + j, NB, stride=tiles)
                part = change[k * NB : (k + 1) * NB, j * NB : (j + 1) * NB]
                o_ref[spot, :] = a_ref[spot, :] - part


def local(hamiltonian):
    tiles = hamiltonian.shape[0]
    n = lax.axis_size("row")
    rows = tiles * NB
    ch = rows // n
    pc = NB // n
    half = n // 2
    f32 = jnp.float32
    bf16 = jnp.bfloat16
    block = hamiltonian.reshape(rows * tiles, NB)
    shapes = [
        ((rows * tiles, NB), f32),
        ((rows, rows), bf16),
        ((rows, rows), bf16),
        ((rows, rows), bf16),
        ((rows, rows), bf16),
        ((rows, NB), f32),
        ((rows, NB), f32),
        ((3, rows, NB), f32),
        ((3, half, 2, ch, NB), f32),
        ((rows, NB), f32),
        ((n, ch, NB), f32),
        ((half, 2, ch, NB), f32),
        ((half, ch, NB), f32),
        ((half, ch, NB), f32),
        ((half, ch, NB), f32),
        ((2, ch, NB), f32),
        ((2, rows, NB), f32),
        ((2, half, 2, ch, NB), f32),
        ((2, rows, NB), f32),
        ((2, rows, NB), f32),
        ((2, rows, NB), f32),
        ((2, rows, NB), f32),
        ((2, rows, 2 * NB), bf16),
        ((2, rows, 2 * NB), bf16),
        ((2, 2 * NB, rows), bf16),
        ((2, 2 * NB, rows), bf16),
        ((4, 3, NB, NB), f32),
        ((4, n, 3, pc, NB), f32),
        ((4, 6, NB, NB), f32),
        ((4, NB, NB), f32),
        ((4, n, pc, NB), f32),
        ((4, pc, NB), f32),
        ((4, n, pc, NB), f32),
        ((4, NB, NB), f32),
    ] + [((NB, NB), f32)] * 5
    anywhere = pl.BlockSpec(memory_space=pl.ANY)
    left = jax.ShapeDtypeStruct((rows, 2 * NB), bf16)
    right = jax.ShapeDtypeStruct((2 * NB, rows), bf16)
    parts = pl.pallas_call(
        functools.partial(reduce_kernel, n, tiles),
        out_shape=[jax.ShapeDtypeStruct((rows * tiles, NB), f32), left, left, right, right],
        in_specs=[anywhere],
        out_specs=[anywhere] * 5,
        scratch_shapes=[pltpu.VMEM(*shape) for shape in shapes]
        + [pltpu.SemaphoreType.DMA] * 5
        + [pltpu.SemaphoreType.DMA((55,))] * 2,
        compiler_params=pltpu.CompilerParams(
            collective_id=0, has_side_effects=True, vmem_limit_bytes=VMEM_LIMIT
        ),
        name="reduce_panels",
    )(block)
    step = min(rows, 2 * NB)
    block_spec = pl.BlockSpec((step * tiles, NB), lambda i: (i, 0))
    left_spec = pl.BlockSpec((step, 2 * NB), lambda i: (i, 0))
    right_spec = pl.BlockSpec((2 * NB, rows), lambda i: (0, 0))
    result = pl.pallas_call(
        functools.partial(update_kernel, tiles),
        out_shape=jax.ShapeDtypeStruct((rows * tiles, NB), f32),
        grid=(rows // step,),
        in_specs=[block_spec, left_spec, left_spec, right_spec, right_spec],
        out_specs=block_spec,
        compiler_params=pltpu.CompilerParams(vmem_limit_bytes=VMEM_LIMIT),
        name="update_matrix",
    )(*parts)
    return result.reshape(hamiltonian.shape)


def solution(mesh):
    spec = P(None, "row", None, None, "col", None)
    return jax.shard_map(local, mesh=mesh, in_specs=(spec,), out_specs=spec, check_vma=False)
```

```python
import functools

import jax
import jax.numpy as jnp
from jax import lax
from jax.experimental import pallas as pl
from jax.experimental.pallas import tpu as pltpu
from jax.sharding import PartitionSpec as P

MESH = pl.DeviceIdType.MESH
NB = 128
NN = (((1,), (0,)), ((), ()))
NT = (((1,), (1,)), ((), ()))
TN = (((0,), (0,)), ((), ()))
TT = (((0,), (1,)), ((), ()))
VMEM_LIMIT = 56 << 20
CHOL_WIDTH = 32
INV_WIDTH = 16
CHOL_BLOCKS = NB // CHOL_WIDTH
INV_BLOCKS = NB // INV_WIDTH


def split(value):
    high = value.astype(jnp.bfloat16)
    low = (value - high.astype(jnp.float32)).astype(jnp.bfloat16)
    return high, low


def mxu(first, second, dims):
    return lax.dot_general(first, second, dims, preferred_element_type=jnp.float32)


def dot3(first, second, dims):
    fh, fl = split(first)
    sh, sl = split(second)
    return mxu(fh, sh, dims) + (mxu(fh, sl, dims) + mxu(fl, sh, dims))


def exact(first, second, dims=NN):
    return lax.dot_general(
        first, second, dims, precision=lax.Precision.HIGHEST, preferred_element_type=jnp.float32
    )


def iota(axis, shape):
    return lax.broadcasted_iota(jnp.int32, shape, axis)


def leading_columns(x, base, width):
    rolled = pltpu.roll(x, lax.rem(NB - base, NB), 1)
    return [jnp.broadcast_to(rolled[:, i : i + 1], (width, NB)) for i in range(width)]


def cholesky_blocks(g_ref, r_ref, first, last):
    width = CHOL_WIDTH
    sub = iota(0, (width, NB))
    lane = iota(1, (width, NB))

    def block(k, carry):
        base = pl.multiple_of(k * width, width)
        x = g_ref[pl.ds(base, width), :]
        cols = leading_columns(x, base, width)
        for i in range(width):
            scale = lax.rsqrt(cols[i][i : i + 1, :])
            column = cols[i] * scale
            below = jnp.where(sub > i, column, 0.0)
            row = x[i : i + 1, :] * scale
            x = jnp.where(sub == i, row, x - below * row)
            for m in range(i + 1, width):
                cols[m] = cols[m] - below * column[m : m + 1, :]
        x = jnp.where(lane >= base + sub, x, 0.0)
        r_ref[pl.ds(base, width), :] = x
        g_ref[...] -= exact(x, x, TN)
        return carry

    lax.fori_loop(first, last, block, 0)


def inverse_blocks(y_ref, t_ref, first, last):
    width = INV_WIDTH
    sub = iota(0, (width, NB))
    lane = iota(1, (width, NB))
    wide = iota(1, (NB, NB))

    def block(k, carry):
        base = pl.multiple_of(k * width, width)
        x = y_ref[pl.ds(base, width), :]
        cols = leading_columns(x, base, width)
        inside = (lane >= base) & (lane < base + width)
        x = jnp.where(inside, jnp.where(lane - base == sub, 1.0, 0.0), x)
        for i in range(width):
            scale = 1.0 / cols[i][i : i + 1, :]
            factor = jnp.where(sub == i, 0.0, cols[i])
            row = x[i : i + 1, :] * scale
            x = jnp.where(sub == i, row, x - factor * row)
            for m in range(i + 1, width):
                entry = cols[m][i : i + 1, :] * scale
                cols[m] = jnp.where(sub == i, entry, cols[m] - factor * entry)
        t_ref[pl.ds(base, width), :] = x
        y = y_ref[...]
        chosen = (wide >= base) & (wide < base + width)
        y_ref[...] = jnp.where(chosen, 0.0, y) - exact(jnp.where(chosen, y, 0.0), t_ref[...])
        y_ref[pl.ds(base, width), :] = x
        t_ref[pl.ds(base, width), :] = jnp.zeros((width, NB), jnp.float32)
        return carry

    lax.fori_loop(first, last, block, 0)


def reduce_kernel(n, tiles, *refs):
    rows = tiles * NB
    ch = rows // n
    pc = NB // n
    half = n // 2
    per_tile = NB // ch
    (
        a_hbm, a_out, lh_out, ll_out, qh_out, ql_out,
        abuf, ahi, alo, thi, tlo, stg_r, stg_c, xr, xc,
        wpart_r, wslot_r, wpart_c, wsib, wsum, wslot_c, wch, wr, wc,
        panel_r, panel_c, cor_r, cor_c, lh, ll, qh, ql,
        ar_src, ar_slot, ar_res, h_src, h_slot, h_piece, h_ex, h_res,
        g_ref, y_ref, t_ref, r0_ref, r1_ref, asem, osem, osem2, osem3, osem4, ss, rs,
    ) = refs
    r = lax.axis_index("row")
    c = lax.axis_index("col")
    parity = lax.rem(r, 2)
    level = r // 2
    sibling = (r + 1 - 2 * parity, c)

    load = pltpu.make_async_copy(a_hbm, abuf, asem)
    load.start()
    barrier = pltpu.get_barrier_semaphore()

    def greet(k, carry):
        pl.semaphore_signal(barrier, inc=1, device_id=(lax.rem(r + k, n), c), device_id_type=MESH)
        pl.semaphore_signal(barrier, inc=1, device_id=(r, lax.rem(c + k, n)), device_id_type=MESH)
        return carry

    lax.fori_loop(1, n, greet, 0)

    @pl.when(r != c)
    def _():
        pl.semaphore_signal(barrier, inc=1, device_id=(c, r), device_id_type=MESH)

    def send(src, dst, sem, device):
        pltpu.make_async_remote_copy(
            src, dst, ss.at[sem], rs.at[sem], device_id=device, device_id_type=MESH
        ).start()

    def over_cols(sem, src_of, dst_of):
        def one(k, carry):
            j = lax.rem(c + k, n)
            send(src_of(j), dst_of(j), sem, (r, j))
            return carry

        lax.fori_loop(1, n, one, 0)

    def over_rows(sem, src_of, dst_of):
        def one(k, carry):
            j = lax.rem(r + k, n)
            send(src_of(j), dst_of(j), sem, (j, c))
            return carry

        lax.fori_loop(1, n, one, 0)

    def wait_sent(sem, sent):
        pltpu.make_async_copy(sent, sent, ss.at[sem]).wait()

    def wait_received(sem, received):
        pltpu.make_async_copy(received, received, rs.at[sem]).wait()

    def wait(sem, part):
        wait_received(sem, part)
        wait_sent(sem, part)

    def scatter(t):
        @pl.when(c == t)
        def _():
            over_cols(
                t,
                lambda j: stg_r.at[pl.ds(j * ch, ch)],
                lambda j: xr.at[t, pl.ds(j * ch, ch)],
            )
            xr[t, pl.ds(t * ch, ch), :] = stg_r[pl.ds(t * ch, ch), :]

        @pl.when(r == t)
        def _():
            over_rows(
                3 + t,
                lambda j: stg_c.at[pl.ds(j * ch, ch)],
                lambda j: xc.at[t, j // 2, lax.rem(j, 2)],
            )
            xc[t, t // 2, t % 2] = stg_c[pl.ds(t * ch, ch), :]

    def scatter_wait(t):
        @pl.when(c == t)
        def _():
            wait_sent(t, stg_r.at[pl.ds(0, (n - 1) * ch)])

        @pl.when(c != t)
        def _():
            wait_received(t, xr.at[t, pl.ds(c * ch, ch)])

        @pl.when(r == t)
        def _():
            wait_sent(3 + t, stg_c.at[pl.ds(0, (n - 1) * ch)])

        @pl.when(r != t)
        def _():
            wait_received(3 + t, xc.at[t, level, parity])

    def gather_cols_start(buf, sem):
        mine = buf.at[pl.ds(c * ch, ch)]
        over_cols(sem, lambda j: mine, lambda j: mine)

    def gather_cols_wait(buf, sem):
        wait(sem, buf.at[pl.ds(0, (n - 1) * ch)])

    def gather_rows_start(buf, sem):
        mine = buf.at[level, parity]

        def one(k, carry):
            send(mine, mine, sem, (lax.rem(level + k, half) * 2 + parity, c))
            return carry

        lax.fori_loop(1, half, one, 0)

    def gather_rows_mid(buf, sem):
        wait(sem, buf.at[pl.ds(0, half - 1), 0])
        mine = buf.at[:, parity]
        send(mine, mine, sem + 1, sibling)

    def gather_rows_wait(buf, sem):
        wait(sem + 1, buf.at[:, 0])

    def sum_start(q, parts, sem, over, me):
        count = len(parts)
        for i, part in enumerate(parts):
            ar_src[q, i] = part
        over(
            sem,
            lambda j: ar_src.at[q, pl.ds(0, count), pl.ds(j * pc, pc)],
            lambda j: ar_slot.at[q, me, pl.ds(0, count)],
        )
        ar_slot[q, me, 0:count] = ar_src[q, 0:count, pl.ds(me * pc, pc), :]

    def sum_slots(q, count, sem):
        wait(sem, ar_slot.at[q, pl.ds(0, n - 1), pl.ds(0, count)])
        total = ar_slot[q, 0, 0:count]
        for j in range(1, n):
            total = total + ar_slot[q, j, 0:count]
        return total

    def sum_spread(q, count, sem, over, me):
        mine = (q, pl.ds(0, count), pl.ds(me * pc, pc))
        over(sem + 1, lambda j: ar_res.at[mine], lambda j: ar_res.at[mine])

    def sum_mid(q, count, sem, over, me):
        ar_res[q, 0:count, pl.ds(me * pc, pc), :] = sum_slots(q, count, sem)
        sum_spread(q, count, sem, over, me)

    def sum_wait(q, count, sem):
        wait(sem + 1, ar_res.at[q, pl.ds(0, count), pl.ds(0, (n - 1) * pc)])

    def all_start(p, part, sem, over, me):
        h_src[p] = part
        over(sem, lambda j: h_src.at[p, pl.ds(j * pc, pc)], lambda j: h_slot.at[p, me])
        h_slot[p, me] = h_src[p, pl.ds(me * pc, pc), :]

    def all_mid(p, sem, over, me):
        wait(sem, h_slot.at[p, pl.ds(0, n - 1)])
        total = h_slot[p, 0]
        for j in range(1, n):
            total = total + h_slot[p, j]
        h_piece[p] = total
        over(sem + 1, lambda j: h_piece.at[p], lambda j: h_ex.at[p, me])
        h_ex[p, me] = total

    def all_late(p, sem, over, me):
        wait(sem + 1, h_ex.at[p, pl.ds(0, n - 1)])
        total = h_ex[p, 0]
        for j in range(1, n):
            total = total + h_ex[p, j]
        h_res[p, pl.ds(me * pc, pc), :] = total
        mine = h_res.at[p, pl.ds(me * pc, pc)]
        over(sem + 2, lambda j: mine, lambda j: mine)

    def all_wait(p, sem):
        wait(sem + 2, h_res.at[p, pl.ds(0, (n - 1) * pc)])

    def tile_product(high_ref, low_ref, at, both):
        wide = mxu(high_ref[pl.ds(at, NB), :], both, NN)
        return wide[:, :NB] + (wide[:, NB:] + mxu(low_ref[pl.ds(at, NB), :], both[:, :NB], NN))

    def halves(panel):
        return jnp.concatenate(split(panel), axis=1)

    def flat(ref):
        return ref[...].reshape(rows, NB)

    def flip(value):
        return jnp.concatenate(
            [value[i * NB : (i + 1) * NB].T for i in range(tiles)], axis=1
        )

    def known_part(r_mat, k, corner):
        kr = exact(k, r_mat)
        return kr + kr.T + exact(exact(r_mat, corner, TN), r_mat)

    def core(z, inner_sum):
        return 0.5 * exact(exact(z, inner_sum, TN), z)

    zero_tile = jnp.zeros((NB, NB), jnp.float32)
    block_rows = min(rows, 2 * NB)

    def keep_left(p, first, second):
        for i, value in enumerate((first, second)):
            spot = slice(i * NB, (i + 1) * NB)
            lh[p, :, spot], ll[p, :, spot] = split(value)

    def keep_right(p, first, second):
        for i, value in enumerate((first, second)):
            spot = slice(i * NB, (i + 1) * NB)
            qh[p, spot, :], ql[p, spot, :] = split(flip(value))

    def apply_first():
        def one(i, carry):
            at = pl.multiple_of(i * block_rows, block_rows)
            high = lh[0, pl.ds(at, block_rows)]
            low = ll[0, pl.ds(at, block_rows)]
            for b in range(0, tiles, 2):
                cols = slice(b * NB, (b + 2) * NB)
                change = mxu(high, qh[0, :, cols], NN) + (
                    mxu(high, ql[0, :, cols], NN) + mxu(low, qh[0, :, cols], NN)
                )
                for k in range(block_rows // NB):
                    for j in range(2):
                        spot = pl.ds((at + k * NB) * tiles + b + j, NB, stride=tiles)
                        part = change[k * NB : (k + 1) * NB, j * NB : (j + 1) * NB]
                        abuf[spot, :] = abuf[spot, :] - part
            return carry

        lax.fori_loop(0, rows // block_rows, one, 0)

    def write_band(p, r_ref):
        @pl.when(c == p)
        def _():
            for a in range(tiles):
                spot = pl.ds(a * NB * tiles, NB, stride=tiles)

                @pl.when(a * n + r == p + 1)
                def _():
                    abuf[spot, :] = -r_ref[...]

                @pl.when(a * n + r > p + 1)
                def _():
                    abuf[spot, :] = zero_tile

        @pl.when(r == p)
        def _():
            for b in range(tiles):
                spot = pl.ds(b, NB, stride=tiles)

                @pl.when(b * n + c == p + 1)
                def _():
                    abuf[spot, :] = -r_ref[...].T

                @pl.when(b * n + c > p + 1)
                def _():
                    abuf[spot, :] = zero_tile

    load.wait()
    for t in range(3):

        @pl.when(c == t)
        def _():
            for a in range(tiles):
                stg_r[a * NB : (a + 1) * NB, :] = abuf[pl.ds(a * NB * tiles, NB, stride=tiles), :]

            @pl.when(r == 0)
            def _():
                stg_r[0:NB, :] = zero_tile

        @pl.when(r == t)
        def _():
            for b in range(tiles):
                stg_c[b * NB : (b + 1) * NB, :] = abuf[pl.ds(b, NB, stride=tiles), :].T

            @pl.when(c == 0)
            def _():
                stg_c[0:NB, :] = zero_tile

    pl.semaphore_wait(barrier, 2 * (n - 1) + jnp.where(r != c, 1, 0))
    scatter(0)

    def tile_start(sem, index, t, owner):
        @pl.when((r == t) & (c == owner))
        def _():
            over_cols(
                sem,
                lambda j: stg_c.at[pl.ds(j * pc, pc)],
                lambda j: ar_res.at[0, index, pl.ds(j * pc, pc)],
            )
            ar_res[0, index, pl.ds(c * pc, pc), :] = stg_c[pl.ds(c * pc, pc), :]

    def tile_wait(sem, index, t, owner):
        @pl.when((r == t) & (c == owner))
        def _():
            wait_sent(sem, stg_c.at[pl.ds(0, (n - 1) * pc)])

        @pl.when((r == t) & (c != owner))
        def _():
            wait_received(sem, ar_res.at[0, index, pl.ds(c * pc, pc)])

    def row_start(sem, t, first, count):
        mine = (0, pl.ds(first, count), pl.ds(c * pc, pc))

        @pl.when(r == t)
        def _():
            over_rows(sem, lambda j: ar_res.at[mine], lambda j: ar_res.at[mine])

    def row_wait(sem, t, first, count):
        @pl.when(r == t)
        def _():
            wait_sent(sem, ar_res.at[0, pl.ds(first, count), pl.ds(0, (n - 1) * pc)])

        @pl.when(r != t)
        def _():
            wait_received(sem, ar_res.at[0, pl.ds(first, count), pl.ds(c * pc, pc)])

    @pl.when(r == 0)
    def _():
        mine = stg_c[...]
        first = jnp.where(c == 1, mine[0:NB], 0.0)
        second = jnp.where(c == 2, mine[0:NB], 0.0)
        sum_start(0, [dot3(mine, mine, TN), first, second], 9, over_cols, c)

    t_ref[...] = zero_tile

    @pl.when(r == 0)
    def _():
        ar_res[0, 0:3, pl.ds(c * pc, pc), :] = sum_slots(0, 3, 9)

    row_start(19, 0, 0, 3)
    scatter_wait(0)
    gather_rows_start(xc.at[0], 6)
    gather_cols_start(xr.at[0], 8)
    scatter(1)
    tile_start(43, 3, 1, 1)
    tile_start(44, 4, 1, 2)
    scatter(2)
    tile_start(45, 5, 2, 2)

    def to_parts(a, carry):
        at = pl.multiple_of(a * NB, NB)
        for b in range(tiles):
            high, low = split(abuf[pl.ds(a * NB * tiles + b, NB, stride=tiles), :])
            ahi[pl.ds(at, NB), b * NB : (b + 1) * NB] = high
            alo[pl.ds(at, NB), b * NB : (b + 1) * NB] = low
        return carry

    lax.fori_loop(0, tiles, to_parts, 0)

    def to_flipped(b, carry):
        at = pl.multiple_of(b * NB, NB)
        for a in range(tiles):
            high, low = split(abuf[pl.ds(a * NB * tiles + b, NB, stride=tiles), :].T)
            thi[pl.ds(at, NB), a * NB : (a + 1) * NB] = high
            tlo[pl.ds(at, NB), a * NB : (a + 1) * NB] = low
        return carry

    lax.fori_loop(0, tiles // 2, to_flipped, 0)

    row_wait(19, 0, 0, 3)
    sum_spread(0, 3, 9, over_cols, c)
    scatter_wait(1)
    gather_cols_start(xr.at[1], 13)
    gather_rows_mid(xc.at[0], 6)
    tile_wait(43, 3, 1, 1)
    tile_wait(44, 4, 1, 2)
    tile_wait(45, 5, 2, 2)
    row_start(46, 1, 3, 2)
    row_start(47, 2, 5, 1)
    scatter_wait(2)
    gather_rows_wait(xc.at[0], 6)

    both = halves(flat(xc.at[0]))

    def first_product(a, carry):
        at = pl.multiple_of(a * NB, NB)
        wpart_r[pl.ds(at, NB), :] = tile_product(ahi, alo, at, both)
        for i in range(per_tile):
            j = a * per_tile + i
            mine = wpart_r.at[pl.ds(j * ch, ch)]

            @pl.when(j != c)
            def _():
                send(mine, wslot_r.at[c], 20, (r, j))

        return carry

    lax.fori_loop(0, tiles, first_product, 0)
    wslot_r[c] = wpart_r[pl.ds(c * ch, ch), :]
    gather_cols_wait(xr.at[0], 8)
    all_start(0, dot3(xr[0], wpart_r[...], TN), 26, over_rows, r)
    gather_rows_start(xc.at[1], 11)
    sum_wait(0, 3, 9)
    g_ref[...] = ar_res[0, 0]
    cholesky_blocks(g_ref, r0_ref, 0, CHOL_BLOCKS)
    all_mid(0, 26, over_cols, c)
    gather_cols_wait(xr.at[1], 13)
    sum_start(1, [dot3(xr[0], xr[1], TN)], 14, over_rows, r)
    all_start(2, dot3(xr[2, pl.ds(c * ch, ch), :], xr[0, pl.ds(c * ch, ch), :], TN), 49, over_cols, c)
    y_ref[...] = ar_res[0, 0] + exact(ar_res[0, 1], r0_ref[...], TN)
    inverse_blocks(y_ref, t_ref, 0, INV_BLOCKS // 2)

    wait(20, wslot_r.at[pl.ds(0, n - 1)])
    total = wslot_r[0]
    for j in range(1, n):
        total = total + wslot_r[j]
    wr[0, pl.ds(c * ch, ch), :] = total
    wch[0] = total

    @pl.when(r != c)
    def _():
        send(wch.at[0], wc.at[0, c // 2, lax.rem(c, 2)], 22, (c, r))

    @pl.when(r == c)
    def _():
        wc[0, level, parity] = total

    gather_cols_start(wr.at[0], 23)
    all_late(0, 26, over_rows, r)
    sum_mid(1, 1, 14, over_rows, r)
    row_wait(46, 1, 3, 2)
    row_wait(47, 2, 5, 1)
    tiles_mine = (0, pl.ds(3, 3), pl.ds(c * pc, pc))
    over_cols(48, lambda j: ar_res.at[tiles_mine], lambda j: ar_res.at[tiles_mine])
    inverse_blocks(y_ref, t_ref, INV_BLOCKS // 2, INV_BLOCKS)
    lax.fori_loop(tiles // 2, tiles, to_flipped, 0)
    gather_rows_mid(xc.at[1], 11)
    all_mid(2, 49, over_rows, r)

    @pl.when(r != c)
    def _():
        wait_received(22, wc.at[0, level, parity])
        wait_sent(22, wch.at[0])

    gather_rows_start(wc.at[0], 24)
    wait(48, ar_res.at[0, pl.ds(3, 3), pl.ds(0, (n - 1) * pc)])
    sum_wait(1, 1, 14)
    r0 = r0_ref[...]
    z0 = y_ref[...]
    k0 = ar_res[1, 0]
    rz0 = exact(r0, z0)
    f01 = ar_res[0, 1] + r0
    f02 = ar_res[0, 2]
    x11 = ar_res[0, 3]
    x12 = ar_res[0, 4]
    x22 = ar_res[0, 5]
    known = known_part(r0, k0, x11)
    c01 = exact(k0, z0, TN) + exact(x11, rz0)
    all_wait(0, 26)
    b0 = core(z0, h_res[0] + known)
    c01 = c01 - exact(f01, b0)
    coef = jnp.concatenate([z0, rz0, -b0], axis=0)
    carried = exact(coef, f01, NT)
    last = carried[2 * NB :] + c01.T
    coef = jnp.concatenate(
        [coef, jnp.concatenate([carried[: 2 * NB], last], axis=0)], axis=1
    )

    def first_panel(f_ref, c_ref, x0, x1, index):
        f_ref[0] = x0

        @pl.when(index == 1)
        def _():
            f_ref[0, 0:NB, :] = f_ref[0, 0:NB, :] + r0

        out = dot3(jnp.concatenate([x1, f_ref[0]], axis=1), coef[NB:], NN)
        c_ref[0] = out[:, :NB]
        f_ref[1] = x1 - out[:, NB:]

    def first_panel_product(f_ref, c_ref, w, index):
        out = dot3(w, coef[:NB], NN)
        c_ref[0] = c_ref[0] + out[:, :NB]
        f_ref[1] = f_ref[1] - out[:, NB:]

        @pl.when(index == 0)
        def _():
            c_ref[0, 0:NB, :] = zero_tile

        @pl.when(index <= 1)
        def _():
            f_ref[1, 0:NB, :] = zero_tile

    all_late(2, 49, over_cols, c)
    first_panel(panel_r, cor_r, xr[0], xr[1], r)
    gather_cols_wait(wr.at[0], 23)
    first_panel_product(panel_r, cor_r, wr[0], r)

    p1r = panel_r[1]
    sum_start(2, [dot3(p1r, p1r, TN)], 30, over_rows, r)
    both = halves(p1r)

    def second_product(b, carry):
        at = pl.multiple_of(b * NB, NB)
        value = tile_product(thi, tlo, at, both).reshape(per_tile, ch, NB)
        for i in range(per_tile):
            j = b * per_tile + i
            wpart_c[j // 2, lax.rem(j, 2)] = value[i]
        return carry

    lax.fori_loop(0, tiles, second_product, 0)
    send(wpart_c.at[:, 1 - parity], wsib, 34, sibling)
    sum_mid(2, 1, 30, over_rows, r)
    wait(34, wsib)
    wsum[...] = wpart_c[:, parity] + wsib[...]

    def spread(k, carry):
        to = lax.rem(level + k, half)
        send(wsum.at[to], wslot_c.at[level], 35, (to * 2 + parity, c))
        return carry

    lax.fori_loop(1, half, spread, 0)
    wslot_c[level] = wsum[level]
    all_wait(2, 49)
    c02 = exact(h_res[2], z0) + exact(x12, rz0) - exact(f02, b0)
    top = x12 - exact(c02, f01, NT) - exact(f02, c01, NT)
    cf = exact(c02, f02, NT)
    keep_left(0, cor_r[0], panel_r[0])
    gather_rows_mid(wc.at[0], 24)
    all_start(3, dot3(xr[2, pl.ds(c * ch, ch), :], panel_r[1, pl.ds(c * ch, ch), :], TN), 52, over_cols, c)
    gather_rows_wait(xc.at[1], 11)
    first_panel(panel_c, cor_c, flat(xc.at[0]), flat(xc.at[1]), c)
    gather_rows_wait(wc.at[0], 24)
    first_panel_product(panel_c, cor_c, flat(wc.at[0]), c)
    p1c = panel_c[1]
    all_start(1, dot3(p1c, flat(wpart_c), TN), 36, over_cols, c)
    inner = dot3(p1c, jnp.concatenate([panel_c[0], cor_c[0]], axis=1), TN)
    sum_start(3, [inner[:, 0:NB], inner[:, NB:]], 32, over_cols, c)
    sum_wait(2, 1, 30)
    g_ref[...] = ar_res[2, 0]
    cholesky_blocks(g_ref, r1_ref, 0, CHOL_BLOCKS)
    all_mid(1, 36, over_rows, r)
    all_mid(3, 52, over_rows, r)
    sum_mid(3, 2, 32, over_cols, c)
    wait(35, wslot_c.at[pl.ds(0, half - 1)])
    total = wslot_c[0]
    for j in range(1, half):
        total = total + wslot_c[j]
    total = total + exact(xc[2, level, parity], r1_ref[...])
    wch[1] = total

    @pl.when(r != c)
    def _():
        send(wch.at[1], wr.at[1, pl.ds(r * ch, ch)], 41, (c, r))

    @pl.when(r == c)
    def _():
        wr[1, pl.ds(c * ch, ch), :] = total

    wc[1, level, parity] = total
    gather_rows_start(wc.at[1], 39)
    y_ref[...] = ar_res[2, 0] + exact(top, r1_ref[...], TN)
    inverse_blocks(y_ref, t_ref, 0, INV_BLOCKS // 2)

    @pl.when(r != c)
    def _():
        wait_received(41, wr.at[1, pl.ds(c * ch, ch)])
        wait_sent(41, wch.at[1])

    all_late(1, 36, over_cols, c)
    all_late(3, 52, over_cols, c)
    gather_cols_start(wr.at[1], 42)
    inverse_blocks(y_ref, t_ref, INV_BLOCKS // 2, INV_BLOCKS)
    gather_rows_mid(wc.at[1], 39)
    r1 = r1_ref[...]
    z1 = y_ref[...]
    rz1 = exact(r1, z1)
    sum_wait(3, 2, 32)
    all_wait(3, 52)
    j1t = ar_res[3, 0]
    j2t = ar_res[3, 1]
    cross = exact(j2t, j1t, NT)
    k1 = h_res[3].T - exact(j2t, f02, NT) - exact(j1t, c02, NT)
    known = known_part(r1, k1, x22 - cf - cf.T) - cross - cross.T
    fold1 = -exact(j1t, z1, TN) - exact(f02, rz1, TN)
    fold2 = -exact(j2t, z1, TN) - exact(c02, rz1, TN)
    keep_right(0, panel_c[0], cor_c[0])
    apply_first()
    write_band(0, r0_ref)
    write_band(1, r1_ref)
    pltpu.make_async_copy(abuf, a_out, asem).start()
    all_wait(1, 36)
    b1 = core(z1, h_res[1] + known)
    coef = jnp.concatenate([z1, fold1, fold2, -b1], axis=0)

    def second_panel(f_ref, c_ref, index):
        @pl.when(index == 2)
        def _():
            f_ref[1, 0:NB, :] = f_ref[1, 0:NB, :] + r1

        c_ref[1] = dot3(
            jnp.concatenate([c_ref[0], f_ref[0], f_ref[1]], axis=1), coef[NB:], NN
        )

    def second_panel_product(c_ref, w, index):
        c_ref[1] = c_ref[1] + dot3(w, coef[:NB], NN)

        @pl.when(index <= 1)
        def _():
            c_ref[1, 0:NB, :] = zero_tile

    second_panel(panel_r, cor_r, r)
    second_panel(panel_c, cor_c, c)
    gather_rows_wait(wc.at[1], 39)
    second_panel_product(cor_c, flat(wc.at[1]), c)
    keep_right(1, panel_c[1], cor_c[1])
    pltpu.make_async_copy(qh.at[1], qh_out, osem).start()
    pltpu.make_async_copy(ql.at[1], ql_out, osem2).start()
    gather_cols_wait(wr.at[1], 42)
    second_panel_product(cor_r, wr[1], r)
    keep_left(1, cor_r[1], panel_r[1])
    last_high = pltpu.make_async_copy(lh.at[1], lh_out, osem3)
    last_low = pltpu.make_async_copy(ll.at[1], ll_out, osem4)
    last_high.start()
    last_low.start()
    pltpu.make_async_copy(abuf, a_out, asem).wait()
    pltpu.make_async_copy(qh.at[1], qh_out, osem).wait()
    pltpu.make_async_copy(ql.at[1], ql_out, osem2).wait()
    last_high.wait()
    last_low.wait()


def update_kernel(tiles, a_ref, lh, ll, qh, ql, o_ref):
    high = lh[...]
    low = ll[...]
    for b in range(0, tiles, 2):
        cols = slice(b * NB, (b + 2) * NB)
        change = mxu(high, qh[:, cols], NN) + (
            mxu(high, ql[:, cols], NN) + mxu(low, qh[:, cols], NN)
        )
        for k in range(high.shape[0] // NB):
            for j in range(2):
                spot = pl.ds(k * NB * tiles + b + j, NB, stride=tiles)
                part = change[k * NB : (k + 1) * NB, j * NB : (j + 1) * NB]
                o_ref[spot, :] = a_ref[spot, :] - part


def local(hamiltonian):
    tiles = hamiltonian.shape[0]
    n = lax.axis_size("row")
    rows = tiles * NB
    ch = rows // n
    pc = NB // n
    half = n // 2
    f32 = jnp.float32
    bf16 = jnp.bfloat16
    block = hamiltonian.reshape(rows * tiles, NB)
    shapes = [
        ((rows * tiles, NB), f32),
        ((rows, rows), bf16),
        ((rows, rows), bf16),
        ((rows, rows), bf16),
        ((rows, rows), bf16),
        ((rows, NB), f32),
        ((rows, NB), f32),
        ((3, rows, NB), f32),
        ((3, half, 2, ch, NB), f32),
        ((rows, NB), f32),
        ((n, ch, NB), f32),
        ((half, 2, ch, NB), f32),
        ((half, ch, NB), f32),
        ((half, ch, NB), f32),
        ((half, ch, NB), f32),
        ((2, ch, NB), f32),
        ((2, rows, NB), f32),
        ((2, half, 2, ch, NB), f32),
        ((2, rows, NB), f32),
        ((2, rows, NB), f32),
        ((2, rows, NB), f32),
        ((2, rows, NB), f32),
        ((2, rows, 2 * NB), bf16),
        ((2, rows, 2 * NB), bf16),
        ((2, 2 * NB, rows), bf16),
        ((2, 2 * NB, rows), bf16),
        ((4, 3, NB, NB), f32),
        ((4, n, 3, pc, NB), f32),
        ((4, 6, NB, NB), f32),
        ((4, NB, NB), f32),
        ((4, n, pc, NB), f32),
        ((4, pc, NB), f32),
        ((4, n, pc, NB), f32),
        ((4, NB, NB), f32),
    ] + [((NB, NB), f32)] * 5
    anywhere = pl.BlockSpec(memory_space=pl.ANY)
    left = jax.ShapeDtypeStruct((rows, 2 * NB), bf16)
    right = jax.ShapeDtypeStruct((2 * NB, rows), bf16)
    parts = pl.pallas_call(
        functools.partial(reduce_kernel, n, tiles),
        out_shape=[jax.ShapeDtypeStruct((rows * tiles, NB), f32), left, left, right, right],
        in_specs=[anywhere],
        out_specs=[anywhere] * 5,
        scratch_shapes=[pltpu.VMEM(*shape) for shape in shapes]
        + [pltpu.SemaphoreType.DMA] * 5
        + [pltpu.SemaphoreType.DMA((55,))] * 2,
        compiler_params=pltpu.CompilerParams(
            collective_id=0, has_side_effects=True, vmem_limit_bytes=VMEM_LIMIT
        ),
        name="reduce_panels",
    )(block)
    step = min(rows, 2 * NB)
    block_spec = pl.BlockSpec((step * tiles, NB), lambda i: (i, 0))
    left_spec = pl.BlockSpec((step, 2 * NB), lambda i: (i, 0))
    right_spec = pl.BlockSpec((2 * NB, rows), lambda i: (0, 0))
    result = pl.pallas_call(
        functools.partial(update_kernel, tiles),
        out_shape=jax.ShapeDtypeStruct((rows * tiles, NB), f32),
        grid=(rows // step,),
        in_specs=[block_spec, left_spec, left_spec, right_spec, right_spec],
        out_specs=block_spec,
        compiler_params=pltpu.CompilerParams(vmem_limit_bytes=VMEM_LIMIT),
        name="update_matrix",
    )(*parts)
    return result.reshape(hamiltonian.shape)


def solution(mesh):
    spec = P(None, "row", None, None, "col", None)
    return jax.shard_map(local, mesh=mesh, in_specs=(spec,), out_specs=spec, check_vma=False)
```
